32 devices in a mesh: seq: 8 (over z, x), ctx: 4 (over y, core).
Axes of the slice: x: 2, y: 2, z: 4, core: 2. Of those that a mesh axis runs over, the one named last changes fastest.
Arguments:
- queries: bfloat16 [512, 1024], P(('seq', 'ctx'))
- new_token_keys: bfloat16 [512, 128], P(('seq', 'ctx'))
- new_token_values: bfloat16 [512, 128], P(('seq', 'ctx')), may hold values from -0.796875 to 0.796875
- cache_keys: bfloat16 [8, 32768, 128], P('seq', 'ctx'), as said below
- cache_values: bfloat16 [8, 32768, 128], P('seq', 'ctx'), as said below
- block_ids: int32 [8, 8, 4, 12], P('seq', None, 'ctx'), may hold values from 0 to 63, as said below
- block_counts: int32 [8, 8, 4], P('seq', None, 'ctx'), may hold values from 1 to 12, as said below
Outputs:
- attended: bfloat16 [512, 1024], P(('seq', 'ctx'))
The draws below stay inside these ranges and needn't reach their ends.
Inputs may be any that keep to these rules, and one draw needn't show every extreme that they name: `block_ids`: within one list of 12 entries the key blocks are distinct; only the first block_counts of them are used. `block_counts`: the most, 12, is reached in every draw. cache_keys[h] equals cache_keys[h2] where floor(h / 8) = floor(h2 / 8). cache_values[h] equals cache_values[h2] where floor(h / 8) = floor(h2 / 8).
All inputs are finite; a program needn't handle non-finite values.
Results may differ from the reference program's by a relative error of at most 0.0075.
Values may be sent and summed in bfloat16 or wider, within the bound.
No kernel may reach another device: no remote copies, remote signals or barrier semaphores. Data moves between devices by JAX's collectives and lax.ppermute only.
A program may use at most 64 MiB of HBM per device.

```python
import math
import jax
import jax.numpy as jnp
from jax import lax

HEAD_WIDTH = 128
HEADS_PER_GROUP = 8
TILE_QUERY_ROWS = 64
KROWS = 128
KQ = 12
CTX_DEV = 8192
QUERY_HEAD_COUNT = 8
KEY_VALUE_HEADS = 1
NEW_TOKENS = 512
CACHED_TOKENS = 32768
QB = 8
KBQ = 64
N_CTX = 4


def listed_blocks(key):
    cache_quarters = CACHED_TOKENS // CTX_DEV
    ranking = jax.random.randint(key, (QUERY_HEAD_COUNT, QB, cache_quarters, KBQ), 0, 2 ** 20) * KBQ + jnp.arange(KBQ, dtype=jnp.int32)
    order = jnp.argsort(ranking, axis=-1, stable=True)
    return order[..., :KQ].astype(jnp.int32)


def cache_common(key, salt, dispersed):
    provider = jax.random.fold_in(key, salt)
    unscaled = dispersed * jax.random.normal(provider, (KEY_VALUE_HEADS, CACHED_TOKENS, HEAD_WIDTH), jnp.float32)
    return jnp.repeat(unscaled.astype(jnp.bfloat16), HEADS_PER_GROUP, axis=0)


def draw_cache_keys(key, part):
    return cache_common(key, 301, 1.5)


def draw_cache_values(key, part):
    return cache_common(key, 302, 0.45)


def simple_rows(provider, columns):
    return 1.5 * jax.random.normal(provider, (NEW_TOKENS, columns), jnp.float32)


def draw_queries(key, part):
    final_output = simple_rows(jax.random.fold_in(key, 401), QUERY_HEAD_COUNT * HEAD_WIDTH)
    return final_output.astype(jnp.bfloat16)


def draw_new_token_keys(key, part):
    final_output = simple_rows(jax.random.fold_in(key, 402), KEY_VALUE_HEADS * HEAD_WIDTH)
    return final_output.astype(jnp.bfloat16)


def draw_block_ids(key, part):
    return listed_blocks(key)


def draw_block_counts(key, part):
    cache_quarters = CACHED_TOKENS // CTX_DEV
    upper = jax.random.randint(jax.random.fold_in(key, 601), (QUERY_HEAD_COUNT, 1, cache_quarters), max(1, KQ // 2), KQ + 1)
    lower = jnp.maximum(1, upper // 2)
    counts = jax.random.randint(jax.random.fold_in(key, 602), (QUERY_HEAD_COUNT, QB, cache_quarters), lower, upper + 1)
    where_full = jax.random.randint(jax.random.fold_in(key, 603), (), 0, QUERY_HEAD_COUNT * QB * cache_quarters)
    counts = counts.reshape(-1).at[where_full].set(KQ).reshape(QUERY_HEAD_COUNT, QB, cache_quarters)
    return counts.astype(jnp.int32)


def block_levels(stream_key, extent, cuts, low, largest):
    def one(dim, blocks):
        draws = jax.random.uniform(jax.random.fold_in(jax.random.fold_in(stream_key, 6), dim), (blocks,), jnp.float32, low / len(cuts), largest / len(cuts))
        return jnp.repeat(jnp.exp(draws), extent[dim] // blocks).reshape((-1,) + (1,) * (len(extent) - dim - 1))

    loudness = one(*cuts[0])
    for cut in cuts[1:]:
        loudness = loudness * one(*cut)
    return loudness


def setup_inputs(seed: int = 0) -> dict:
    streams_of = jax.random.split(jax.random.key(seed), 8)
    queries = draw_queries(jax.random.fold_in(streams_of[7], 71), 0)
    new_token_keys = draw_new_token_keys(jax.random.fold_in(streams_of[7], 71), 0)
    new_token_values = jnp.clip(jax.random.uniform(streams_of[2], (NEW_TOKENS, KEY_VALUE_HEADS * HEAD_WIDTH), jnp.float32, -0.796875, 0.796875) * block_levels(streams_of[2], (NEW_TOKENS, KEY_VALUE_HEADS * HEAD_WIDTH), ((0, 32),), -0.4, 0.0), -0.796875, 0.796875).astype(jnp.bfloat16)
    cache_keys = draw_cache_keys(jax.random.fold_in(streams_of[7], 71), 0)
    cache_values = draw_cache_values(jax.random.fold_in(streams_of[7], 71), 0)
    block_ids = draw_block_ids(jax.random.fold_in(streams_of[7], 71), 0)
    block_counts = draw_block_counts(jax.random.fold_in(streams_of[7], 71), 0)
    return dict(queries=queries, new_token_keys=new_token_keys, new_token_values=new_token_values, cache_keys=cache_keys, cache_values=cache_values, block_ids=block_ids, block_counts=block_counts)


def head_attend(query_head, key_head, value_head, cached_keys, cached_values, listed, used):
    tile_keys = cached_keys.reshape(N_CTX * KBQ, KROWS, HEAD_WIDTH)
    tile_values = cached_values.reshape(N_CTX * KBQ, KROWS, HEAD_WIDTH)
    offsets = jnp.arange(N_CTX, dtype=jnp.int32)[None, :, None] * KBQ
    global_ids = (offsets + listed).reshape(QB, N_CTX * KQ)
    selected_keys = tile_keys[global_ids].reshape(QB, N_CTX * KQ * KROWS, HEAD_WIDTH)
    picked_values = tile_values[global_ids].reshape(QB, N_CTX * KQ * KROWS, HEAD_WIDTH)
    slot_ok = (jnp.arange(KQ, dtype=jnp.int32)[None, None, :] < used[:, :, None]).reshape(QB, N_CTX * KQ)
    slot_ok = jnp.repeat(slot_ok, KROWS, axis=1)
    padded_keys = jnp.concatenate([jnp.zeros((KROWS, HEAD_WIDTH), jnp.bfloat16), key_head]).reshape(NEW_TOKENS // KROWS + 1, KROWS, HEAD_WIDTH)
    padded_values = jnp.concatenate([jnp.zeros((KROWS, HEAD_WIDTH), jnp.bfloat16), value_head]).reshape(NEW_TOKENS // KROWS + 1, KROWS, HEAD_WIDTH)
    block_index = jnp.arange(QB, dtype=jnp.int32)
    key_block = block_index * TILE_QUERY_ROWS // KROWS
    nearby_keys = jnp.concatenate([padded_keys[key_block], padded_keys[key_block + 1]], axis=1)
    near_values = jnp.concatenate([padded_values[key_block], padded_values[key_block + 1]], axis=1)
    positions = (key_block[:, None] - 1) * KROWS + jnp.arange(2 * KROWS, dtype=jnp.int32)[None, :]
    query_pos = block_index[:, None] * TILE_QUERY_ROWS + jnp.arange(TILE_QUERY_ROWS, dtype=jnp.int32)[None, :]
    near_ok = (positions[:, None, :] >= 0) & (positions[:, None, :] <= query_pos[:, :, None])
    every_key = jnp.concatenate([selected_keys, nearby_keys], axis=1)
    every_value = jnp.concatenate([picked_values, near_values], axis=1)
    visible = jnp.concatenate([jnp.broadcast_to(slot_ok[:, None, :], (QB, TILE_QUERY_ROWS, N_CTX * KQ * KROWS)), near_ok], axis=2)
    tiled_queries = query_head.reshape(QB, TILE_QUERY_ROWS, HEAD_WIDTH)
    logit_scores = jnp.einsum('pmt,pyt->pmy', tiled_queries.astype(jnp.float32), every_key.astype(jnp.float32)) * (1.0 / math.sqrt(HEAD_WIDTH))
    top = lax.optimization_barrier(jnp.max(jnp.where(visible, logit_scores, -jnp.inf), axis=-1, keepdims=True))
    exponent_terms = jnp.where(visible, jnp.exp(logit_scores - top), jnp.float32(0.0))
    totals = lax.optimization_barrier(jnp.sum(exponent_terms, axis=-1, keepdims=True))
    attention_weights = exponent_terms.astype(jnp.bfloat16)
    blended = jnp.einsum('nst,ntw->nsw', attention_weights.astype(jnp.float32), every_value.astype(jnp.float32))
    return (blended / totals).astype(jnp.bfloat16).reshape(NEW_TOKENS, HEAD_WIDTH)

def reference(queries, new_token_keys, new_token_values, cache_keys, cache_values, block_ids, block_counts):
    query_stack = queries.reshape(NEW_TOKENS, QUERY_HEAD_COUNT, HEAD_WIDTH).transpose(1, 0, 2)
    stacked_keys = new_token_keys.reshape(NEW_TOKENS, KEY_VALUE_HEADS, HEAD_WIDTH).transpose(1, 0, 2)
    stacked_values = new_token_values.reshape(NEW_TOKENS, KEY_VALUE_HEADS, HEAD_WIDTH).transpose(1, 0, 2)
    head_index = jnp.arange(QUERY_HEAD_COUNT, dtype=jnp.int32)

    def one_head(operands):
        query_head, cached_keys, cached_values, listed, used, index = operands
        kv_index = index // HEADS_PER_GROUP
        key_head = lax.dynamic_index_in_dim(stacked_keys, kv_index, 0, keepdims=False)
        value_head = lax.dynamic_index_in_dim(stacked_values, kv_index, 0, keepdims=False)
        return head_attend(query_head, key_head, value_head, cached_keys, cached_values, listed, used)
    outputs = lax.map(one_head, (query_stack, cache_keys, cache_values, block_ids, block_counts, head_index))
    return outputs.transpose(1, 0, 2).reshape(NEW_TOKENS, QUERY_HEAD_COUNT * HEAD_WIDTH)
```

```python
import math

import jax
import jax.numpy as jnp
from jax import lax
from jax.experimental import pallas as pl
from jax.experimental.pallas import tpu as pltpu
from jax.sharding import PartitionSpec as P

HEADS_PER_GROUP = 8
TILE_QUERY_ROWS = 64
KROWS = 128
KQ = 12
LANES = 128
LISTED = KQ + 1
LOG2E = 1.4426950408889634


def nt(a, b):
    return lax.dot_general(a, b, (((1,), (1,)), ((), ())), preferred_element_type=jnp.float32)


def attend_kernel(lists, q_ref, near_ref, k_ref, v_ref, out_ref, s_scr):
    ctx_count, groups, local_rows, _ = q_ref.shape
    blocks = lists.shape[0] // (HEADS_PER_GROUP * LISTED)
    member = lax.rem(lax.axis_index("seq"), HEADS_PER_GROUP)
    quarter = lax.axis_index("ctx")
    rows = TILE_QUERY_ROWS
    head_size = k_ref.shape[2]
    scale = LOG2E / math.sqrt(head_size)
    lane = lax.broadcasted_iota(jnp.int32, (rows, LANES), 1)

    def one_block(group):
        block = group * HEADS_PER_GROUP + member
        base = jnp.maximum((block * rows // KROWS) * (KROWS // rows) - KROWS // rows, 0)
        near = near_ref[pl.ds(base, 2 * KROWS // rows)].reshape(rows, 2 * head_size)
        near = jnp.concatenate([near, near], axis=0)
        near_k, near_v = near[:, :head_size], near[:, head_size:]
        position = (base + lane // local_rows) * rows + quarter * local_rows + lax.rem(lane, local_rows)
        token = block * rows + lax.broadcasted_iota(jnp.int32, (rows, LANES), 0)
        near_ok = (lane < rows) & (position <= token)

        def one_head(head, stats):
            first = (head * blocks + block) * LISTED
            count = lists[first + KQ]
            columns = pl.ds(pl.multiple_of(head * head_size, LANES), head_size)
            q = q_ref[:, group, :, columns].reshape(rows, head_size)
            s_near = jnp.where(near_ok, nt(q, near_k), -jnp.inf)
            high = s_near
            for slot in range(KQ):
                s = nt(q, k_ref[lists[first + slot]])
                s = jnp.where(slot < count, s, -jnp.inf)
                s_scr[slot] = s
                high = jnp.maximum(high, s)
            top = jnp.max(high, axis=1, keepdims=True) * scale
            p = jnp.exp2(s_near * scale - top)
            total = p
            acc = jnp.dot(p.astype(jnp.bfloat16), near_v, preferred_element_type=jnp.float32)
            for slot in range(0, KQ, 2):
                pair = []
                for part in (slot, slot + 1):
                    p = jnp.exp2(s_scr[part] * scale - top)
                    total = total + p
                    pair.append(p.astype(jnp.bfloat16))
                values = jnp.concatenate(
                    [v_ref[lists[first + slot]], v_ref[lists[first + slot + 1]]], axis=0
                )
                acc = acc + jnp.dot(
                    jnp.concatenate(pair, axis=1), values, preferred_element_type=jnp.float32
                )
            out_ref[:, group, :, columns] = acc.astype(jnp.bfloat16).reshape(
                ctx_count, local_rows, head_size
            )
            total = jnp.sum(total, axis=1, keepdims=True)
            stats = jnp.where(lane == head, top, stats)
            return jnp.where(lane == head + HEADS_PER_GROUP, total, stats)

        stats = lax.fori_loop(
            0, HEADS_PER_GROUP, one_head, jnp.zeros((rows, LANES), jnp.float32)
        )
        packed = jnp.zeros((rows, LANES), jnp.float32)
        for step in range(3):
            part = stats.astype(jnp.bfloat16).astype(jnp.float32)
            stats = stats - part
            shift = step * 2 * HEADS_PER_GROUP
            packed = packed + (pltpu.roll(part, shift, 1) if shift else part)
        width = HEADS_PER_GROUP * head_size
        out_ref[:, group, :, width:] = packed.astype(jnp.bfloat16).reshape(
            ctx_count, local_rows, LANES
        )

    if groups == 1:
        one_block(0)
    else:
        pl.loop(0, groups)(one_block)


def merge_kernel(in_ref, out_ref):
    ctx_count, groups, local_rows, full = in_ref.shape
    width = full - LANES
    head_size = width // HEADS_PER_GROUP

    def one_block(group):
        stats = []
        for part in range(ctx_count):
            packed = in_ref[part, group, :, width:].astype(jnp.float32)
            one = packed
            for step in (1, 2):
                one = one + pltpu.roll(packed, LANES - step * 2 * HEADS_PER_GROUP, 1)
            stats.append(one)
        top = stats[0]
        for one in stats[1:]:
            top = jnp.maximum(top, one)
        factors = [jnp.exp2(one - top) for one in stats]
        total = jnp.zeros((local_rows, LANES), jnp.float32)
        for one, factor in zip(stats, factors):
            total = total + pltpu.roll(one, LANES - HEADS_PER_GROUP, 1) * factor
        inverse = 1.0 / total
        factors = [factor * inverse for factor in factors]
        for head in range(HEADS_PER_GROUP):
            columns = slice(head * head_size, (head + 1) * head_size)
            mixed = jnp.zeros((local_rows, head_size), jnp.float32)
            for part in range(ctx_count):
                mixed = mixed + in_ref[part, group, :, columns].astype(jnp.float32) * (
                    factors[part][:, head : head + 1]
                )
            out_ref[group, :, columns] = mixed.astype(jnp.bfloat16)

    if groups == 1:
        one_block(0)
    else:
        pl.loop(0, groups)(one_block)


def body(
    queries, new_token_keys, new_token_values, cache_keys, cache_values, block_ids, block_counts
):
    seq_count = lax.axis_size("seq")
    ctx_count = lax.axis_size("ctx")
    head_size = cache_keys.shape[2]
    local_rows = queries.shape[0]
    blocks = block_ids.shape[1]
    groups = seq_count // HEADS_PER_GROUP
    width = HEADS_PER_GROUP * head_size
    assert local_rows * ctx_count == TILE_QUERY_ROWS and cache_keys.shape[0] == 1
    same_group = None
    if groups > 1:
        same_group = [
            [g * HEADS_PER_GROUP + r for r in range(HEADS_PER_GROUP)] for g in range(groups)
        ]
        same_member = [
            [g * HEADS_PER_GROUP + r for g in range(groups)] for r in range(HEADS_PER_GROUP)
        ]

    def to_groups(rows):
        pieces = rows.reshape(local_rows, groups, -1).transpose(1, 0, 2)
        if groups == 1:
            return pieces
        return lax.all_to_all(
            pieces, "seq", split_axis=0, concat_axis=0, tiled=True, axis_index_groups=same_member
        )

    queries = to_groups(queries)
    pairs = jnp.concatenate([to_groups(new_token_keys), to_groups(new_token_values)], axis=2)
    listed = jnp.concatenate([block_ids[0, :, 0, :], block_counts[0, :, :]], axis=1)
    listed = listed.astype(jnp.bfloat16).reshape(-1)
    tile = groups * local_rows * LANES
    listed = jnp.pad(listed, (0, -listed.shape[0] % tile))
    listed = listed.reshape(groups, local_rows, -1)
    packed = jnp.concatenate([pairs, listed], axis=2)
    packed = lax.all_gather(packed, "seq", axis=0, axis_index_groups=same_group)
    near = packed[..., : 2 * head_size].transpose(1, 0, 2, 3)
    near = near.reshape(seq_count, local_rows, 2 * head_size)
    lists = packed[..., 2 * head_size :].reshape(HEADS_PER_GROUP, -1)[:, : blocks * LISTED]
    lists = lists.astype(jnp.int32).reshape(-1)
    queries = lax.all_gather(queries, "ctx", axis=0)

    vmem = pl.BlockSpec(memory_space=pltpu.VMEM)
    partial = pl.pallas_call(
        attend_kernel,
        out_shape=jax.ShapeDtypeStruct(
            (ctx_count, groups, local_rows, width + LANES), jnp.bfloat16
        ),
        in_specs=[pl.BlockSpec(memory_space=pltpu.SMEM)] + [vmem] * 4,
        out_specs=vmem,
        scratch_shapes=[pltpu.VMEM((KQ, TILE_QUERY_ROWS, KROWS), jnp.float32)],
        compiler_params=pltpu.CompilerParams(vmem_limit_bytes=24 * 1024 * 1024),
        name="attend",
    )(
        lists,
        queries,
        near,
        cache_keys.reshape(-1, KROWS, head_size),
        cache_values.reshape(-1, KROWS, head_size),
    )
    partial = lax.all_to_all(partial, "ctx", split_axis=0, concat_axis=0, tiled=True)
    merged = pl.pallas_call(
        merge_kernel,
        out_shape=jax.ShapeDtypeStruct((groups, local_rows, width), jnp.bfloat16),
        in_specs=[vmem],
        out_specs=vmem,
        name="merge",
    )(partial)
    if groups > 1:
        merged = lax.all_to_all(
            merged, "seq", split_axis=0, concat_axis=0, tiled=True, axis_index_groups=same_member
        )
    return merged.transpose(1, 0, 2).reshape(local_rows, groups * width)


def solution(mesh):
    return jax.shard_map(
        body,
        mesh=mesh,
        in_specs=(
            P(("seq", "ctx"), None),
            P(("seq", "ctx"), None),
            P(("seq", "ctx"), None),
            P("seq", "ctx", None),
            P("seq", "ctx", None),
            P("seq", None, "ctx", None),
            P("seq", None, "ctx"),
        ),
        out_specs=P(("seq", "ctx"), None),
        check_vma=False,
    )
```

```python
import math

import jax
import jax.numpy as jnp
from jax import lax
from jax.experimental import pallas as pl
from jax.experimental.pallas import tpu as pltpu
from jax.sharding import PartitionSpec as P

HEADS_PER_GROUP = 8
TILE_QUERY_ROWS = 64
KROWS = 128
KQ = 12
LANES = 128
CTX = 4
NEAR = 2 * KROWS // TILE_QUERY_ROWS
LOG2E = 1.4426950408889634


def nt(a, b):
    return lax.dot_general(a, b, (((1,), (1,)), ((), ())), preferred_element_type=jnp.float32)


def attend_kernel(lists, *refs):
    q_refs, near_refs = refs[:CTX], refs[CTX : CTX + NEAR]
    k_ref, v_ref = refs[CTX + NEAR : CTX + NEAR + 2]
    out_refs, s_scr = refs[CTX + NEAR + 2 : -1], refs[-1]
    groups, local_rows, _ = q_refs[0].shape
    member = lax.rem(lax.axis_index("seq"), HEADS_PER_GROUP)
    quarter = lax.axis_index("ctx")
    rows = TILE_QUERY_ROWS
    head_size = k_ref.shape[2]
    scale = LOG2E / math.sqrt(head_size)
    lane = lax.broadcasted_iota(jnp.int32, (rows, LANES), 1)
    sublane = lax.broadcasted_iota(jnp.int32, (rows, LANES), 0)

    def one_block(group):
        block = group * HEADS_PER_GROUP + member
        near = []
        for back, near_ref in enumerate(near_refs):
            place = jnp.maximum(group - jnp.where(member < back, 1, 0), 0)
            near.append(near_ref[place])
        near = jnp.concatenate(near + near, axis=0)
        near_k, near_v = near[:, :head_size], near[:, head_size:]
        position = (block - lane // local_rows) * rows + quarter * local_rows + lane % local_rows
        token = block * rows + ((sublane // local_rows) ^ quarter) * local_rows + sublane % local_rows
        oldest = jnp.maximum((block * rows // KROWS - 1) * KROWS, 0)
        near_ok = (lane < rows) & (position <= token) & (position >= oldest)

        def one_head(turn, stats):
            head = lax.rem(member - turn + HEADS_PER_GROUP, HEADS_PER_GROUP)
            count = lists[turn, block, KQ]
            columns = pl.ds(pl.multiple_of(head * head_size, LANES), head_size)
            q = jnp.concatenate([q_ref[group, :, columns] for q_ref in q_refs], axis=0)
            s_near = jnp.where(near_ok, nt(q, near_k), -jnp.inf)
            high = s_near
            for slot in range(KQ):
                s = nt(q, k_ref[lists[turn, block, slot]])
                s = jnp.where(slot < count, s, -jnp.inf)
                s_scr[slot] = s
                high = jnp.maximum(high, s)
            top = jnp.max(high, axis=1, keepdims=True) * scale
            p = jnp.exp2(s_near * scale - top)
            total = p
            acc = jnp.dot(p.astype(jnp.bfloat16), near_v, preferred_element_type=jnp.float32)
            for slot in range(0, KQ, 2):
                pair = []
                for part in (slot, slot + 1):
                    p = jnp.exp2(s_scr[part] * scale - top)
                    total = total + p
                    pair.append(p.astype(jnp.bfloat16))
                values = jnp.concatenate(
                    [v_ref[lists[turn, block, slot]], v_ref[lists[turn, block, slot + 1]]], axis=0
                )
                acc = acc + jnp.dot(
                    jnp.concatenate(pair, axis=1), values, preferred_element_type=jnp.float32
                )
            acc = acc.astype(jnp.bfloat16)
            for part, out_ref in enumerate(out_refs):
                out_ref[group, :, columns] = acc[part * local_rows : (part + 1) * local_rows]
            total = jnp.sum(total, axis=1, keepdims=True)
            stats = jnp.where(lane == head, top, stats)
            return jnp.where(lane == head + HEADS_PER_GROUP, total, stats)

        stats = lax.fori_loop(
            0, HEADS_PER_GROUP, one_head, jnp.zeros((rows, LANES), jnp.float32)
        )
        packed = jnp.zeros((rows, LANES), jnp.float32)
        for step in range(3):
            part = stats.astype(jnp.bfloat16).astype(jnp.float32)
            stats = stats - part
            shift = step * 2 * HEADS_PER_GROUP
            packed = packed + (pltpu.roll(part, shift, 1) if shift else part)
        packed = packed.astype(jnp.bfloat16)
        width = HEADS_PER_GROUP * head_size
        for part, out_ref in enumerate(out_refs):
            out_ref[group, :, width:] = packed[part * local_rows : (part + 1) * local_rows]

    if groups == 1:
        one_block(0)
    else:
        pl.loop(0, groups)(one_block)


def merge_kernel(*refs):
    in_refs, out_ref = refs[:-1], refs[-1]
    groups, local_rows, full = in_refs[0].shape
    width = full - LANES
    head_size = width // HEADS_PER_GROUP

    def one_block(group):
        stats = []
        for in_ref in in_refs:
            packed = in_ref[group, :, width:].astype(jnp.float32)
            one = packed
            for step in (1, 2):
                one = one + pltpu.roll(packed, LANES - step * 2 * HEADS_PER_GROUP, 1)
            stats.append(one)
        top = stats[0]
        for one in stats[1:]:
            top = jnp.maximum(top, one)
        factors = [jnp.exp2(one - top) for one in stats]
        total = jnp.zeros((local_rows, LANES), jnp.float32)
        for one, factor in zip(stats, factors):
            total = total + pltpu.roll(one, LANES - HEADS_PER_GROUP, 1) * factor
        inverse = 1.0 / total
        factors = [factor * inverse for factor in factors]
        for head in range(HEADS_PER_GROUP):
            columns = slice(head * head_size, (head + 1) * head_size)
            mixed = jnp.zeros((local_rows, head_size), jnp.float32)
            for in_ref, factor in zip(in_refs, factors):
                mixed = mixed + in_ref[group, :, columns].astype(jnp.float32) * (
                    factor[:, head : head + 1]
                )
            out_ref[group, :, columns] = mixed.astype(jnp.bfloat16)

    if groups == 1:
        one_block(0)
    else:
        pl.loop(0, groups)(one_block)


def from_member(value, back, seq_count):
    pairs = []
    for device in range(seq_count):
        first = device - device % HEADS_PER_GROUP
        pairs.append((device, first + (device + back) % HEADS_PER_GROUP))
    return lax.ppermute(value, "seq", pairs)


def from_quarter(value, mask):
    return lax.ppermute(value, "ctx", [(device, device ^ mask) for device in range(CTX)])


def body(
    queries, new_token_keys, new_token_values, cache_keys, cache_values, block_ids, block_counts
):
    seq_count = lax.axis_size("seq")
    head_size = cache_keys.shape[2]
    local_rows = queries.shape[0]
    groups = seq_count // HEADS_PER_GROUP
    width = HEADS_PER_GROUP * head_size
    assert lax.axis_size("ctx") == CTX and cache_keys.shape[0] == 1
    assert local_rows * CTX == TILE_QUERY_ROWS
    if groups > 1:
        same_member = [
            [g * HEADS_PER_GROUP + r for g in range(groups)] for r in range(HEADS_PER_GROUP)
        ]

    def to_groups(rows):
        pieces = rows.reshape(local_rows, groups, -1).transpose(1, 0, 2)
        if groups == 1:
            return pieces
        return lax.all_to_all(
            pieces, "seq", split_axis=0, concat_axis=0, tiled=True, axis_index_groups=same_member
        )

    lists = jnp.concatenate([block_ids[0, :, 0, :], block_counts[0, :, :]], axis=1)
    lists = [lists] + [from_member(lists, back, seq_count) for back in range(1, HEADS_PER_GROUP)]
    queries = to_groups(queries)
    queries = [queries] + [from_quarter(queries, mask) for mask in range(1, CTX)]
    pairs = jnp.concatenate([to_groups(new_token_keys), to_groups(new_token_values)], axis=2)
    near = [pairs] + [from_member(pairs, back, seq_count) for back in range(1, NEAR)]

    vmem = pl.BlockSpec(memory_space=pltpu.VMEM)
    partial = pl.pallas_call(
        attend_kernel,
        out_shape=[
            jax.ShapeDtypeStruct((groups, local_rows, width + LANES), jnp.bfloat16)
        ] * CTX,
        in_specs=[pl.BlockSpec(memory_space=pltpu.SMEM)] + [vmem] * (CTX + NEAR + 2),
        out_specs=[vmem] * CTX,
        scratch_shapes=[pltpu.VMEM((KQ, TILE_QUERY_ROWS, KROWS), jnp.float32)],
        compiler_params=pltpu.CompilerParams(vmem_limit_bytes=24 * 1024 * 1024),
        name="attend",
    )(
        jnp.stack(lists),
        *queries,
        *near,
        cache_keys.reshape(-1, KROWS, head_size),
        cache_values.reshape(-1, KROWS, head_size),
    )
    partial = [partial[0]] + [from_quarter(partial[mask], mask) for mask in range(1, CTX)]
    merged = pl.pallas_call(
        merge_kernel,
        out_shape=jax.ShapeDtypeStruct((groups, local_rows, width), jnp.bfloat16),
        in_specs=[vmem] * CTX,
        out_specs=vmem,
        name="merge",
    )(*partial)
    if groups > 1:
        merged = lax.all_to_all(
            merged, "seq", split_axis=0, concat_axis=0, tiled=True, axis_index_groups=same_member
        )
    return merged.transpose(1, 0, 2).reshape(local_rows, groups * width)


def solution(mesh):
    return jax.shard_map(
        body,
        mesh=mesh,
        in_specs=(
            P(("seq", "ctx"), None),
            P(("seq", "ctx"), None),
            P(("seq", "ctx"), None),
            P("seq", "ctx", None),
            P("seq", "ctx", None),
            P("seq", None, "ctx", None),
            P("seq", None, "ctx"),
        ),
        out_specs=P(("seq", "ctx"), None),
        check_vma=False,
    )
```

```python
import math

import jax
import jax.numpy as jnp
from jax import lax
from jax.experimental import pallas as pl
from jax.experimental.pallas import tpu as pltpu
from jax.sharding import PartitionSpec as P

HEADS_PER_GROUP = 8
TILE_QUERY_ROWS = 64
KROWS = 128
KQ = 12
LANES = 128
CTX = 4
NEAR = 2 * KROWS // TILE_QUERY_ROWS
AT_ONCE = 2
PREPARE_VMEM = 16 * 1024 * 1024
LOG2E = 1.4426950408889634


def nt(a, b):
    return lax.dot_general(a, b, (((1,), (1,)), ((), ())), preferred_element_type=jnp.float32)


def prepare_kernel(*refs):
    keys, values, ids, counts = refs[:4]
    sources, out_ref, targets = refs[4:7], refs[7], refs[8:11]
    own_keys, own_values, own_ids, own_counts, scratch, sems = refs[11:]
    small = [
        pltpu.make_async_copy(source, target, sems.at[i])
        for i, (source, target) in enumerate(
            zip((keys, values, ids, counts), (own_keys, own_values, own_ids, own_counts))
        )
    ]
    large = [
        pltpu.make_async_copy(source, target, sems.at[4 + i])
        for i, (source, target) in enumerate(zip(sources, targets))
    ]
    for copy in small + large:
        copy.start()
    members, groups, _, full = out_ref.shape
    blocks = ids.shape[1]
    scratch[...] = jnp.zeros_like(scratch)
    for copy in small:
        copy.wait()
    for member in range(members):
        for group in range(groups):
            block = group * members + member
            scratch[0:1, :KQ] = own_ids[0, block].astype(jnp.float32)
            scratch[1:2, :blocks] = own_counts[...].astype(jnp.float32)
            out_ref[member, group, :, : full - 2 * LANES] = own_keys[group]
            out_ref[member, group, :, full - 2 * LANES : full - LANES] = own_values[group]
            out_ref[member, group, :, full - LANES :] = scratch[...].astype(jnp.bfloat16)
    for copy in large:
        copy.wait()


def attend_kernel(lists, near_ref, k_ref, v_ref, *refs):
    q_refs, out_refs = refs[:CTX], refs[CTX : 2 * CTX]
    s_scr, m_scr, l_scr = refs[2 * CTX :]
    groups, local_rows, _ = q_refs[0].shape
    member = lax.rem(lax.axis_index("seq"), HEADS_PER_GROUP)
    quarter = lax.axis_index("ctx")
    rows = TILE_QUERY_ROWS
    head_size = k_ref.shape[2]
    scale = LOG2E / math.sqrt(head_size)
    lane = lax.broadcasted_iota(jnp.int32, (rows, LANES), 1)
    sublane = lax.broadcasted_iota(jnp.int32, (rows, LANES), 0)

    def one_block(group):
        block = group * HEADS_PER_GROUP + member
        near = []
        for back in range(NEAR):
            place = jnp.maximum(group - jnp.where(member < back, 1, 0), 0)
            near.append(near_ref[lax.rem(member - back + HEADS_PER_GROUP, HEADS_PER_GROUP), place])
        near = jnp.concatenate(near + near, axis=0)
        near_k, near_v = near[:, :head_size], near[:, head_size : 2 * head_size]
        position = (block - lane // local_rows) * rows + quarter * local_rows + lane % local_rows
        token = block * rows + ((sublane // local_rows) ^ quarter) * local_rows + sublane % local_rows
        oldest = jnp.maximum((block * rows // KROWS - 1) * KROWS, 0)
        near_ok = (lane < rows) & (position <= token) & (position >= oldest)

        def columns_of(head):
            return pl.ds(pl.multiple_of(head * head_size, LANES), head_size)

        def scores(head):
            count = lists[head, group, 1, block]
            q = jnp.concatenate([q_ref[group, :, columns_of(head)] for q_ref in q_refs], axis=0)
            s = jnp.where(near_ok, nt(q, near_k), -jnp.inf)
            s_scr[head, KQ] = s
            high = s
            for slot in range(0, KQ, 2):
                keys = [k_ref[lists[head, group, 0, slot + i]] for i in range(2)]
                both = nt(q, jnp.concatenate(keys, axis=0))
                for i in range(2):
                    s = both[:, i * KROWS : (i + 1) * KROWS]
                    s = jnp.where(slot + i < count, s, -jnp.inf)
                    s_scr[head, slot + i] = s
                    high = jnp.maximum(high, s)
            m_scr[head] = high

        def sums(head):
            top = m_scr[head]
            total = jnp.exp2(s_scr[head, KQ] * scale - top)
            acc = jnp.dot(total.astype(jnp.bfloat16), near_v, preferred_element_type=jnp.float32)
            for slot in range(0, KQ, 2):
                pair = []
                for part in (slot, slot + 1):
                    p = jnp.exp2(s_scr[head, part] * scale - top)
                    total = total + p
                    pair.append(p.astype(jnp.bfloat16))
                values = [v_ref[lists[head, group, 0, slot + i]] for i in range(2)]
                acc = acc + jnp.dot(
                    jnp.concatenate(pair, axis=1),
                    jnp.concatenate(values, axis=0),
                    preferred_element_type=jnp.float32,
                )
            acc = acc.astype(jnp.bfloat16)
            for part, out_ref in enumerate(out_refs):
                out_ref[group, :, columns_of(head)] = acc[
                    part * local_rows : (part + 1) * local_rows
                ]
            l_scr[head] = total

        def in_steps(step):
            def several(turn, carry):
                for i in range(AT_ONCE):
                    step(turn * AT_ONCE + i)
                return carry

            lax.fori_loop(0, HEADS_PER_GROUP // AT_ONCE, several, 0)

        in_steps(scores)
        for head in range(HEADS_PER_GROUP):
            top = jnp.max(m_scr[head], axis=1, keepdims=True) * scale
            m_scr[head] = jnp.broadcast_to(top, (rows, LANES))
        in_steps(sums)
        stats = jnp.zeros((rows, LANES), jnp.float32)
        for head in range(HEADS_PER_GROUP):
            total = jnp.sum(l_scr[head], axis=1, keepdims=True)
            stats = jnp.where(lane == head, m_scr[head], stats)
            stats = jnp.where(lane == head + HEADS_PER_GROUP, total, stats)
        packed = jnp.zeros((rows, LANES), jnp.float32)
        for step in range(3):
            part = stats.astype(jnp.bfloat16).astype(jnp.float32)
            stats = stats - part
            shift = step * 2 * HEADS_PER_GROUP
            packed = packed + (pltpu.roll(part, shift, 1) if shift else part)
        packed = packed.astype(jnp.bfloat16)
        width = HEADS_PER_GROUP * head_size
        for part, out_ref in enumerate(out_refs):
            out_ref[group, :, width:] = packed[part * local_rows : (part + 1) * local_rows]

    if groups == 1:
        one_block(0)
    else:
        pl.loop(0, groups)(one_block)


def merge_kernel(*refs):
    in_refs, out_ref = refs[:-1], refs[-1]
    groups, local_rows, full = in_refs[0].shape
    width = full - LANES
    head_size = width // HEADS_PER_GROUP

    def one_block(group):
        stats = []
        for in_ref in in_refs:
            packed = in_ref[group, :, width:].astype(jnp.float32)
            one = packed
            for step in (1, 2):
                one = one + pltpu.roll(packed, LANES - step * 2 * HEADS_PER_GROUP, 1)
            stats.append(one)
        top = stats[0]
        for one in stats[1:]:
            top = jnp.maximum(top, one)
        factors = [jnp.exp2(one - top) for one in stats]
        total = jnp.zeros((local_rows, LANES), jnp.float32)
        for one, factor in zip(stats, factors):
            total = total + pltpu.roll(one, LANES - HEADS_PER_GROUP, 1) * factor
        inverse = 1.0 / total
        factors = [factor * inverse for factor in factors]
        for head in range(HEADS_PER_GROUP):
            columns = slice(head * head_size, (head + 1) * head_size)
            mixed = jnp.zeros((local_rows, head_size), jnp.float32)
            for in_ref, factor in zip(in_refs, factors):
                mixed = mixed + in_ref[group, :, columns].astype(jnp.float32) * (
                    factor[:, head : head + 1]
                )
            out_ref[group, :, columns] = mixed.astype(jnp.bfloat16)

    if groups == 1:
        one_block(0)
    else:
        pl.loop(0, groups)(one_block)


def from_quarter(value, mask):
    return lax.ppermute(value, "ctx", [(device, device ^ mask) for device in range(CTX)])


def body(
    queries, new_token_keys, new_token_values, cache_keys, cache_values, block_ids, block_counts
):
    seq_count = lax.axis_size("seq")
    head_size = cache_keys.shape[2]
    local_rows = queries.shape[0]
    blocks = block_ids.shape[1]
    groups = seq_count // HEADS_PER_GROUP
    width = HEADS_PER_GROUP * head_size
    assert lax.axis_size("ctx") == CTX and cache_keys.shape[0] == 1
    assert local_rows * CTX == TILE_QUERY_ROWS and blocks <= LANES
    same_group = same_member = None
    if groups > 1:
        same_group = [
            [g * HEADS_PER_GROUP + r for r in range(HEADS_PER_GROUP)] for g in range(groups)
        ]
        same_member = [
            [g * HEADS_PER_GROUP + r for g in range(groups)] for r in range(HEADS_PER_GROUP)
        ]

    def over_seq(pieces, members):
        return lax.all_to_all(
            pieces, "seq", split_axis=0, concat_axis=0, tiled=True, axis_index_groups=members
        )

    def to_groups(rows):
        pieces = rows.reshape(local_rows, groups, -1).transpose(1, 0, 2)
        return pieces if groups == 1 else over_seq(pieces, same_member)

    vmem = pl.BlockSpec(memory_space=pltpu.VMEM)
    hbm = pl.BlockSpec(memory_space=pltpu.HBM)
    smem = pl.BlockSpec(memory_space=pltpu.SMEM)
    queries = to_groups(queries)
    others = [from_quarter(queries, mask) for mask in range(1, CTX)]
    small = (
        to_groups(new_token_keys),
        to_groups(new_token_values),
        block_ids,
        block_counts.reshape(1, blocks),
    )
    large = (
        queries,
        cache_keys.reshape(-1, KROWS, head_size),
        cache_values.reshape(-1, KROWS, head_size),
    )
    packed, queries, keys, values = pl.pallas_call(
        prepare_kernel,
        out_shape=[
            jax.ShapeDtypeStruct(
                (HEADS_PER_GROUP, groups, local_rows, 2 * head_size + LANES), jnp.bfloat16
            )
        ]
        + [jax.ShapeDtypeStruct(one.shape, one.dtype) for one in large],
        in_specs=[hbm] * 7,
        out_specs=[vmem] * 4,
        scratch_shapes=[pltpu.VMEM(one.shape, one.dtype) for one in small]
        + [pltpu.VMEM((local_rows, LANES), jnp.float32), pltpu.SemaphoreType.DMA((7,))],
        compiler_params=pltpu.CompilerParams(vmem_limit_bytes=PREPARE_VMEM),
        name="prepare",
    )(*[pltpu.with_memory_space_constraint(one, pltpu.HBM) for one in small + large])
    near = over_seq(packed, same_group)
    lists = near[:, :, :2, 2 * head_size :].astype(jnp.int32)
    tile = (TILE_QUERY_ROWS, KROWS)
    partial = pl.pallas_call(
        attend_kernel,
        out_shape=[
            jax.ShapeDtypeStruct((groups, local_rows, width + LANES), jnp.bfloat16)
        ] * CTX,
        in_specs=[smem] + [vmem] * (3 + CTX),
        out_specs=[vmem] * CTX,
        scratch_shapes=[
            pltpu.VMEM((HEADS_PER_GROUP, KQ + 1) + tile, jnp.float32),
            pltpu.VMEM((HEADS_PER_GROUP,) + tile, jnp.float32),
            pltpu.VMEM((HEADS_PER_GROUP,) + tile, jnp.float32),
        ],
        compiler_params=pltpu.CompilerParams(vmem_limit_bytes=24 * 1024 * 1024),
        name="attend",
    )(lists, near, keys, values, queries, *others)
    partial = [partial[0]] + [from_quarter(partial[mask], mask) for mask in range(1, CTX)]
    merged = pl.pallas_call(
        merge_kernel,
        out_shape=jax.ShapeDtypeStruct((groups, local_rows, width), jnp.bfloat16),
        in_specs=[vmem] * CTX,
        out_specs=vmem,
        compiler_params=pltpu.CompilerParams(vmem_limit_bytes=4 * 1024 * 1024),
        name="merge",
    )(*partial)
    if groups > 1:
        merged = over_seq(merged, same_member)
    return merged.transpose(1, 0, 2).reshape(local_rows, groups * width)


def solution(mesh):
    return jax.shard_map(
        body,
        mesh=mesh,
        in_specs=(
            P(("seq", "ctx"), None),
            P(("seq", "ctx"), None),
            P(("seq", "ctx"), None),
            P("seq", "ctx", None),
            P("seq", "ctx", None),
            P("seq", None, "ctx", None),
            P("seq", None, "ctx"),
        ),
        out_specs=P(("seq", "ctx"), None),
        check_vma=False,
    )
```

```python
import math

import jax
import jax.numpy as jnp
from jax import lax
from jax.experimental import pallas as pl
from jax.experimental.pallas import tpu as pltpu
from jax.sharding import PartitionSpec as P

HEADS_PER_GROUP = 8
TILE_QUERY_ROWS = 64
KROWS = 128
KQ = 12
LANES = 128
CTX = 4
NEAR = 2 * KROWS // TILE_QUERY_ROWS
AT_ONCE = 4
MIB = 1024 * 1024
LOG2E = 1.4426950408889634


def nt(a, b):
    return lax.dot_general(a, b, (((1,), (1,)), ((), ())), preferred_element_type=jnp.float32)


def pack_kernel(*refs):
    sources, out_ref, targets = refs[:4], refs[4], refs[5:9]
    scratch, sems = refs[9:]
    copies = [
        pltpu.make_async_copy(source, target, sems.at[i])
        for i, (source, target) in enumerate(zip(sources, targets))
    ]
    for copy in copies:
        copy.start()
    keys, values, ids, counts = targets
    members, groups, _, full = out_ref.shape
    blocks = ids.shape[1]
    scratch[...] = jnp.zeros_like(scratch)
    for copy in copies:
        copy.wait()
    for member in range(members):
        for group in range(groups):
            block = group * members + member
            scratch[0:1, :KQ] = ids[0, block].astype(jnp.float32)
            scratch[1:2, :blocks] = counts[...].astype(jnp.float32)
            out_ref[member, group, :, : full - 2 * LANES] = keys[group]
            out_ref[member, group, :, full - 2 * LANES : full - LANES] = values[group]
            out_ref[member, group, :, full - LANES :] = scratch[...].astype(jnp.bfloat16)


def fetch_kernel(*refs):
    count = len(refs) // 2
    copies = [
        pltpu.make_async_copy(refs[i], refs[count + i], refs[-1].at[i]) for i in range(count)
    ]
    for copy in copies:
        copy.start()
    for copy in copies:
        copy.wait()


def attend_kernel(lists, near_ref, k_ref, v_hbm, *refs):
    q_refs, out_refs = refs[:CTX], refs[CTX : 2 * CTX]
    s_scr, m_scr, l_scr, v_ref, sem = refs[2 * CTX :]
    v_copy = pltpu.make_async_copy(v_hbm, v_ref, sem)
    v_copy.start()
    groups, local_rows, _ = q_refs[0].shape
    member = lax.rem(lax.axis_index("seq"), HEADS_PER_GROUP)
    quarter = lax.axis_index("ctx")
    rows = TILE_QUERY_ROWS
    head_size = k_ref.shape[2]
    scale = LOG2E / math.sqrt(head_size)
    lane = lax.broadcasted_iota(jnp.int32, (rows, LANES), 1)
    sublane = lax.broadcasted_iota(jnp.int32, (rows, LANES), 0)

    def one_block(group):
        block = group * HEADS_PER_GROUP + member
        near = []
        for back in range(NEAR):
            place = jnp.maximum(group - jnp.where(member < back, 1, 0), 0)
            near.append(near_ref[lax.rem(member - back + HEADS_PER_GROUP, HEADS_PER_GROUP), place])
        near = jnp.concatenate(near + near, axis=0)
        near_k, near_v = near[:, :head_size], near[:, head_size : 2 * head_size]
        position = (block - lane // local_rows) * rows + quarter * local_rows + lane % local_rows
        token = block * rows + ((sublane // local_rows) ^ quarter) * local_rows + sublane % local_rows
        oldest = jnp.maximum((block * rows // KROWS - 1) * KROWS, 0)
        near_ok = (lane < rows) & (position <= token) & (position >= oldest)

        def columns_of(head):
            return pl.ds(pl.multiple_of(head * head_size, LANES), head_size)

        def scores(head):
            count = lists[head, group, 1, block]
            q = jnp.concatenate([q_ref[group, :, columns_of(head)] for q_ref in q_refs], axis=0)
            s = jnp.where(near_ok, nt(q, near_k), -jnp.inf)
            s_scr[head, KQ] = s
            high = s
            for slot in range(0, KQ, 2):
                keys = [k_ref[lists[head, group, 0, slot + i]] for i in range(2)]
                both = nt(q, jnp.concatenate(keys, axis=0))
                for i in range(2):
                    s = both[:, i * KROWS : (i + 1) * KROWS]
                    s = jnp.where(slot + i < count, s, -jnp.inf)
                    s_scr[head, slot + i] = s
                    high = jnp.maximum(high, s)
            m_scr[head] = high

        def sums(head):
            top = m_scr[head]
            total = jnp.exp2(s_scr[head, KQ] * scale - top)
            acc = jnp.dot(total.astype(jnp.bfloat16), near_v, preferred_element_type=jnp.float32)
            for slot in range(0, KQ, 2):
                pair = []
                for part in (slot, slot + 1):
                    p = jnp.exp2(s_scr[head, part] * scale - top)
                    total = total + p
                    pair.append(p.astype(jnp.bfloat16))
                values = [v_ref[lists[head, group, 0, slot + i]] for i in range(2)]
                acc = acc + jnp.dot(
                    jnp.concatenate(pair, axis=1),
                    jnp.concatenate(values, axis=0),
                    preferred_element_type=jnp.float32,
                )
            acc = acc.astype(jnp.bfloat16)
            for part, out_ref in enumerate(out_refs):
                out_ref[group, :, columns_of(head)] = acc[
                    part * local_rows : (part + 1) * local_rows
                ]
            l_scr[head] = total

        def in_steps(step):
            def several(turn, carry):
                for i in range(AT_ONCE):
                    step(turn * AT_ONCE + i)
                return carry

            lax.fori_loop(0, HEADS_PER_GROUP // AT_ONCE, several, 0)

        in_steps(scores)
        for head in range(HEADS_PER_GROUP):
            top = jnp.max(m_scr[head], axis=1, keepdims=True) * scale
            m_scr[head] = jnp.broadcast_to(top, (rows, LANES))
        if groups == 1:
            v_copy.wait()
        else:
            pl.when(group == 0)(v_copy.wait)
        in_steps(sums)
        stats = jnp.zeros((rows, LANES), jnp.float32)
        for head in range(HEADS_PER_GROUP):
            total = jnp.sum(l_scr[head], axis=1, keepdims=True)
            stats = jnp.where(lane == head, m_scr[head], stats)
            stats = jnp.where(lane == head + HEADS_PER_GROUP, total, stats)
        packed = jnp.zeros((rows, LANES), jnp.float32)
        for step in range(3):
            part = stats.astype(jnp.bfloat16).astype(jnp.float32)
            stats = stats - part
            shift = step * 2 * HEADS_PER_GROUP
            packed = packed + (pltpu.roll(part, shift, 1) if shift else part)
        packed = packed.astype(jnp.bfloat16)
        width = HEADS_PER_GROUP * head_size
        for part, out_ref in enumerate(out_refs):
            out_ref[group, :, width:] = packed[part * local_rows : (part + 1) * local_rows]

    if groups == 1:
        one_block(0)
    else:
        pl.loop(0, groups)(one_block)


def merge_kernel(*refs):
    in_refs, out_ref = refs[:-1], refs[-1]
    groups, local_rows, full = in_refs[0].shape
    width = full - LANES
    head_size = width // HEADS_PER_GROUP

    def one_block(group):
        stats = []
        for in_ref in in_refs:
            packed = in_ref[group, :, width:].astype(jnp.float32)
            one = packed
            for step in (1, 2):
                one = one + pltpu.roll(packed, LANES - step * 2 * HEADS_PER_GROUP, 1)
            stats.append(one)
        top = stats[0]
        for one in stats[1:]:
            top = jnp.maximum(top, one)
        factors = [jnp.exp2(one - top) for one in stats]
        total = jnp.zeros((local_rows, LANES), jnp.float32)
        for one, factor in zip(stats, factors):
            total = total + pltpu.roll(one, LANES - HEADS_PER_GROUP, 1) * factor
        inverse = 1.0 / total
        factors = [factor * inverse for factor in factors]
        for head in range(HEADS_PER_GROUP):
            columns = slice(head * head_size, (head + 1) * head_size)
            mixed = jnp.zeros((local_rows, head_size), jnp.float32)
            for in_ref, factor in zip(in_refs, factors):
                mixed = mixed + in_ref[group, :, columns].astype(jnp.float32) * (
                    factor[:, head : head + 1]
                )
            out_ref[group, :, columns] = mixed.astype(jnp.bfloat16)

    if groups == 1:
        one_block(0)
    else:
        pl.loop(0, groups)(one_block)


def from_quarter(value, mask):
    return lax.ppermute(value, "ctx", [(device, device ^ mask) for device in range(CTX)])


def body(
    queries, new_token_keys, new_token_values, cache_keys, cache_values, block_ids, block_counts
):
    seq_count = lax.axis_size("seq")
    head_size = cache_keys.shape[2]
    local_rows = queries.shape[0]
    blocks = block_ids.shape[1]
    groups = seq_count // HEADS_PER_GROUP
    width = HEADS_PER_GROUP * head_size
    assert lax.axis_size("ctx") == CTX and cache_keys.shape[0] == 1
    assert local_rows * CTX == TILE_QUERY_ROWS and blocks <= LANES
    same_group = same_member = None
    if groups > 1:
        same_group = [
            [g * HEADS_PER_GROUP + r for r in range(HEADS_PER_GROUP)] for g in range(groups)
        ]
        same_member = [
            [g * HEADS_PER_GROUP + r for g in range(groups)] for r in range(HEADS_PER_GROUP)
        ]

    def over_seq(pieces, members):
        return lax.all_to_all(
            pieces, "seq", split_axis=0, concat_axis=0, tiled=True, axis_index_groups=members
        )

    def in_hbm(value):
        return pltpu.with_memory_space_constraint(value, pltpu.HBM)

    def to_groups(rows):
        pieces = rows.reshape(local_rows, groups, -1).transpose(1, 0, 2)
        return pieces if groups == 1 else over_seq(pieces, same_member)

    vmem = pl.BlockSpec(memory_space=pltpu.VMEM)
    hbm = pl.BlockSpec(memory_space=pltpu.HBM)
    smem = pl.BlockSpec(memory_space=pltpu.SMEM)
    queries = to_groups(queries)
    others = [from_quarter(queries, mask) for mask in range(1, CTX)]
    small = (
        to_groups(new_token_keys),
        to_groups(new_token_values),
        block_ids,
        block_counts.reshape(1, blocks),
    )
    packed = pl.pallas_call(
        pack_kernel,
        out_shape=jax.ShapeDtypeStruct(
            (HEADS_PER_GROUP, groups, local_rows, 2 * head_size + LANES), jnp.bfloat16
        ),
        in_specs=[hbm] * 4,
        out_specs=vmem,
        scratch_shapes=[pltpu.VMEM(one.shape, one.dtype) for one in small]
        + [pltpu.VMEM((local_rows, LANES), jnp.float32), pltpu.SemaphoreType.DMA((4,))],
        compiler_params=pltpu.CompilerParams(vmem_limit_bytes=4 * MIB),
        cost_estimate=pl.CostEstimate(flops=0, bytes_accessed=12 * MIB, transcendentals=0),
        name="pack",
    )(*[in_hbm(one) for one in small])
    large = (queries, cache_keys.reshape(-1, KROWS, head_size))
    queries, keys = pl.pallas_call(
        fetch_kernel,
        out_shape=[jax.ShapeDtypeStruct(one.shape, one.dtype) for one in large],
        in_specs=[hbm] * 2,
        out_specs=[vmem] * 2,
        scratch_shapes=[pltpu.SemaphoreType.DMA((2,))],
        compiler_params=pltpu.CompilerParams(vmem_limit_bytes=4 * MIB),
        cost_estimate=pl.CostEstimate(flops=0, bytes_accessed=4 * MIB, transcendentals=0),
        name="fetch",
    )(*[in_hbm(one) for one in large])
    near = over_seq(packed, same_group)
    lists = near[:, :, :2, 2 * head_size :].astype(jnp.int32)
    tile = (TILE_QUERY_ROWS, KROWS)
    values = cache_values.reshape(-1, KROWS, head_size)
    partial = pl.pallas_call(
        attend_kernel,
        out_shape=[
            jax.ShapeDtypeStruct((groups, local_rows, width + LANES), jnp.bfloat16)
        ] * CTX,
        in_specs=[smem, vmem, vmem, hbm] + [vmem] * CTX,
        out_specs=[vmem] * CTX,
        scratch_shapes=[
            pltpu.VMEM((HEADS_PER_GROUP, KQ + 1) + tile, jnp.float32),
            pltpu.VMEM((HEADS_PER_GROUP,) + tile, jnp.float32),
            pltpu.VMEM((HEADS_PER_GROUP,) + tile, jnp.float32),
            pltpu.VMEM(values.shape, values.dtype),
            pltpu.SemaphoreType.DMA,
        ],
        compiler_params=pltpu.CompilerParams(vmem_limit_bytes=24 * MIB),
        name="attend",
    )(lists, near, keys, in_hbm(values), queries, *others)
    partial = [partial[0]] + [from_quarter(partial[mask], mask) for mask in range(1, CTX)]
    merged = pl.pallas_call(
        merge_kernel,
        out_shape=jax.ShapeDtypeStruct((groups, local_rows, width), jnp.bfloat16),
        in_specs=[vmem] * CTX,
        out_specs=vmem,
        compiler_params=pltpu.CompilerParams(vmem_limit_bytes=4 * MIB),
        name="merge",
    )(*partial)
    if groups > 1:
        merged = over_seq(merged, same_member)
    return merged.transpose(1, 0, 2).reshape(local_rows, groups * width)


def solution(mesh):
    return jax.shard_map(
        body,
        mesh=mesh,
        in_specs=(
            P(("seq", "ctx"), None),
            P(("seq", "ctx"), None),
            P(("seq", "ctx"), None),
            P("seq", "ctx", None),
            P("seq", "ctx", None),
            P("seq", None, "ctx", None),
            P("seq", None, "ctx"),
        ),
        out_specs=P(("seq", "ctx"), None),
        check_vma=False,
    )
```

```python
import math

import jax
import jax.numpy as jnp
from jax import lax
from jax.experimental import pallas as pl
from jax.experimental.pallas import tpu as pltpu
from jax.sharding import PartitionSpec as P

HEADS_PER_GROUP = 8
TILE_QUERY_ROWS = 64
KROWS = 128
KQ = 12
LANES = 128
CTX = 4
NEAR = 2 * KROWS // TILE_QUERY_ROWS
AT_ONCE = 8
MIB = 1024 * 1024
LOG2E = 1.4426950408889634


def nt(a, b):
    return lax.dot_general(a, b, (((1,), (1,)), ((), ())), preferred_element_type=jnp.float32)


def pack_kernel(*refs):
    sources, out_ref, targets = refs[:4], refs[4], refs[5:9]
    scratch, sems = refs[9:]
    copies = [
        pltpu.make_async_copy(source, target, sems.at[i])
        for i, (source, target) in enumerate(zip(sources, targets))
    ]
    for copy in copies:
        copy.start()
    keys, values, ids, counts = targets
    members, groups, _, full = out_ref.shape
    blocks = ids.shape[1]
    scratch[...] = jnp.zeros_like(scratch)
    for copy in copies:
        copy.wait()
    for member in range(members):
        for group in range(groups):
            block = group * members + member
            scratch[0:1, :KQ] = ids[0, block].astype(jnp.float32)
            scratch[1:2, :blocks] = counts[...].astype(jnp.float32)
            out_ref[member, group, :, : full - 2 * LANES] = keys[group]
            out_ref[member, group, :, full - 2 * LANES : full - LANES] = values[group]
            out_ref[member, group, :, full - LANES :] = scratch[...].astype(jnp.bfloat16)


def fetch_kernel(*refs):
    count = len(refs) // 2
    copies = [
        pltpu.make_async_copy(refs[i], refs[count + i], refs[-1].at[i]) for i in range(count)
    ]
    for copy in copies:
        copy.start()
    for copy in copies:
        copy.wait()


def attend_kernel(lists, near_ref, k_ref, v_hbm, *refs):
    q_refs, out_refs = refs[:CTX], refs[CTX : 2 * CTX]
    s_scr, m_scr, l_scr, v_ref, sem = refs[2 * CTX :]
    v_copy = pltpu.make_async_copy(v_hbm, v_ref, sem)
    v_copy.start()
    groups, local_rows, _ = q_refs[0].shape
    member = lax.rem(lax.axis_index("seq"), HEADS_PER_GROUP)
    quarter = lax.axis_index("ctx")
    rows = TILE_QUERY_ROWS
    head_size = k_ref.shape[2]
    scale = LOG2E / math.sqrt(head_size)
    lane = lax.broadcasted_iota(jnp.int32, (rows, LANES), 1)
    sublane = lax.broadcasted_iota(jnp.int32, (rows, LANES), 0)

    def one_block(group):
        block = group * HEADS_PER_GROUP + member
        near = []
        for back in range(NEAR):
            place = jnp.maximum(group - jnp.where(member < back, 1, 0), 0)
            near.append(near_ref[lax.rem(member - back + HEADS_PER_GROUP, HEADS_PER_GROUP), place])
        near = jnp.concatenate(near + near, axis=0)
        near_k, near_v = near[:, :head_size], near[:, head_size : 2 * head_size]
        position = (block - lane // local_rows) * rows + quarter * local_rows + lane % local_rows
        token = block * rows + ((sublane // local_rows) ^ quarter) * local_rows + sublane % local_rows
        oldest = jnp.maximum((block * rows // KROWS - 1) * KROWS, 0)
        near_ok = (lane < rows) & (position <= token) & (position >= oldest)

        def columns_of(head):
            return pl.ds(pl.multiple_of(head * head_size, LANES), head_size)

        def scores(head):
            count = lists[head, group, 1, block]
            q = jnp.concatenate([q_ref[group, :, columns_of(head)] for q_ref in q_refs], axis=0)
            s = jnp.where(near_ok, nt(q, near_k), -jnp.inf)
            s_scr[head, KQ] = s
            high = s
            for slot in range(0, KQ, 2):
                keys = [k_ref[lists[head, group, 0, slot + i]] for i in range(2)]
                both = nt(q, jnp.concatenate(keys, axis=0))
                for i in range(2):
                    s = both[:, i * KROWS : (i + 1) * KROWS]
                    s = jnp.where(slot + i < count, s, -jnp.inf)
                    s_scr[head, slot + i] = s
                    high = jnp.maximum(high, s)
            m_scr[head] = high

        def sums(head):
            top = m_scr[head]
            total = jnp.exp2(s_scr[head, KQ] * scale - top)
            acc = jnp.dot(total.astype(jnp.bfloat16), near_v, preferred_element_type=jnp.float32)
            for slot in range(0, KQ, 2):
                pair = []
                for part in (slot, slot + 1):
                    p = jnp.exp2(s_scr[head, part] * scale - top)
                    total = total + p
                    pair.append(p.astype(jnp.bfloat16))
                values = [v_ref[lists[head, group, 0, slot + i]] for i in range(2)]
                acc = acc + jnp.dot(
                    jnp.concatenate(pair, axis=1),
                    jnp.concatenate(values, axis=0),
                    preferred_element_type=jnp.float32,
                )
            acc = acc.astype(jnp.bfloat16)
            for part, out_ref in enumerate(out_refs):
                out_ref[group, :, columns_of(head)] = acc[
                    part * local_rows : (part + 1) * local_rows
                ]
            l_scr[head] = total

        def in_steps(step):
            def several(turn, carry):
                for i in range(AT_ONCE):
                    step(turn * AT_ONCE + i)
                return carry

            lax.fori_loop(0, HEADS_PER_GROUP // AT_ONCE, several, 0)

        in_steps(scores)
        for head in range(HEADS_PER_GROUP):
            top = jnp.max(m_scr[head], axis=1, keepdims=True) * scale
            m_scr[head] = jnp.broadcast_to(top, (rows, LANES))
        if groups == 1:
            v_copy.wait()
        else:
            pl.when(group == 0)(v_copy.wait)
        in_steps(sums)
        stats = jnp.zeros((rows, LANES), jnp.float32)
        for head in range(HEADS_PER_GROUP):
            total = jnp.sum(l_scr[head], axis=1, keepdims=True)
            stats = jnp.where(lane == head, m_scr[head], stats)
            stats = jnp.where(lane == head + HEADS_PER_GROUP, total, stats)
        packed = jnp.zeros((rows, LANES), jnp.float32)
        for step in range(3):
            part = stats.astype(jnp.bfloat16).astype(jnp.float32)
            stats = stats - part
            shift = step * 2 * HEADS_PER_GROUP
            packed = packed + (pltpu.roll(part, shift, 1) if shift else part)
        packed = packed.astype(jnp.bfloat16)
        width = HEADS_PER_GROUP * head_size
        for part, out_ref in enumerate(out_refs):
            out_ref[group, :, width:] = packed[part * local_rows : (part + 1) * local_rows]

    if groups == 1:
        one_block(0)
    else:
        pl.loop(0, groups)(one_block)


def merge_kernel(*refs):
    in_refs, out_ref = refs[:-1], refs[-1]
    groups, local_rows, full = in_refs[0].shape
    width = full - LANES
    head_size = width // HEADS_PER_GROUP

    def one_block(group):
        stats = []
        for in_ref in in_refs:
            packed = in_ref[group, :, width:].astype(jnp.float32)
            one = packed
            for step in (1, 2):
                one = one + pltpu.roll(packed, LANES - step * 2 * HEADS_PER_GROUP, 1)
            stats.append(one)
        top = stats[0]
        for one in stats[1:]:
            top = jnp.maximum(top, one)
        factors = [jnp.exp2(one - top) for one in stats]
        total = jnp.zeros((local_rows, LANES), jnp.float32)
        for one, factor in zip(stats, factors):
            total = total + pltpu.roll(one, LANES - HEADS_PER_GROUP, 1) * factor
        inverse = 1.0 / total
        factors = [factor * inverse for factor in factors]
        for head in range(HEADS_PER_GROUP):
            columns = slice(head * head_size, (head + 1) * head_size)
            mixed = jnp.zeros((local_rows, head_size), jnp.float32)
            for in_ref, factor in zip(in_refs, factors):
                mixed = mixed + in_ref[group, :, columns].astype(jnp.float32) * (
                    factor[:, head : head + 1]
                )
            out_ref[group, :, columns] = mixed.astype(jnp.bfloat16)

    if groups == 1:
        one_block(0)
    else:
        pl.loop(0, groups)(one_block)


def from_quarter(value, mask):
    return lax.ppermute(value, "ctx", [(device, device ^ mask) for device in range(CTX)])


def body(
    queries, new_token_keys, new_token_values, cache_keys, cache_values, block_ids, block_counts
):
    seq_count = lax.axis_size("seq")
    head_size = cache_keys.shape[2]
    local_rows = queries.shape[0]
    blocks = block_ids.shape[1]
    groups = seq_count // HEADS_PER_GROUP
    width = HEADS_PER_GROUP * head_size
    assert lax.axis_size("ctx") == CTX and cache_keys.shape[0] == 1
    assert local_rows * CTX == TILE_QUERY_ROWS and blocks <= LANES
    same_group = same_member = None
    if groups > 1:
        same_group = [
            [g * HEADS_PER_GROUP + r for r in range(HEADS_PER_GROUP)] for g in range(groups)
        ]
        same_member = [
            [g * HEADS_PER_GROUP + r for g in range(groups)] for r in range(HEADS_PER_GROUP)
        ]

    def over_seq(pieces, members):
        return lax.all_to_all(
            pieces, "seq", split_axis=0, concat_axis=0, tiled=True, axis_index_groups=members
        )

    def in_hbm(value):
        return pltpu.with_memory_space_constraint(value, pltpu.HBM)

    def to_groups(rows):
        pieces = rows.reshape(local_rows, groups, -1).transpose(1, 0, 2)
        return pieces if groups == 1 else over_seq(pieces, same_member)

    vmem = pl.BlockSpec(memory_space=pltpu.VMEM)
    hbm = pl.BlockSpec(memory_space=pltpu.HBM)
    smem = pl.BlockSpec(memory_space=pltpu.SMEM)
    queries = to_groups(queries)
    far = from_quarter(queries, 2)
    others = [from_quarter(queries, 1), far, from_quarter(far, 1)]
    small = (
        to_groups(new_token_keys),
        to_groups(new_token_values),
        block_ids,
        block_counts.reshape(1, blocks),
    )
    packed = pl.pallas_call(
        pack_kernel,
        out_shape=jax.ShapeDtypeStruct(
            (HEADS_PER_GROUP, groups, local_rows, 2 * head_size + LANES), jnp.bfloat16
        ),
        in_specs=[hbm] * 4,
        out_specs=vmem,
        scratch_shapes=[pltpu.VMEM(one.shape, one.dtype) for one in small]
        + [pltpu.VMEM((local_rows, LANES), jnp.float32), pltpu.SemaphoreType.DMA((4,))],
        compiler_params=pltpu.CompilerParams(vmem_limit_bytes=4 * MIB),
        cost_estimate=pl.CostEstimate(flops=0, bytes_accessed=12 * MIB, transcendentals=0),
        name="pack",
    )(*[in_hbm(one) for one in small])
    large = (queries, cache_keys.reshape(-1, KROWS, head_size))
    queries, keys = pl.pallas_call(
        fetch_kernel,
        out_shape=[jax.ShapeDtypeStruct(one.shape, one.dtype) for one in large],
        in_specs=[hbm] * 2,
        out_specs=[vmem] * 2,
        scratch_shapes=[pltpu.SemaphoreType.DMA((2,))],
        compiler_params=pltpu.CompilerParams(vmem_limit_bytes=4 * MIB),
        cost_estimate=pl.CostEstimate(flops=0, bytes_accessed=4 * MIB, transcendentals=0),
        name="fetch",
    )(*[in_hbm(one) for one in large])
    near = over_seq(packed, same_group)
    lists = near[:, :, :2, 2 * head_size :].astype(jnp.int32)
    tile = (TILE_QUERY_ROWS, KROWS)
    values = cache_values.reshape(-1, KROWS, head_size)
    partial = pl.pallas_call(
        attend_kernel,
        out_shape=[
            jax.ShapeDtypeStruct((groups, local_rows, width + LANES), jnp.bfloat16)
        ] * CTX,
        in_specs=[smem, vmem, vmem, hbm] + [vmem] * CTX,
        out_specs=[vmem] * CTX,
        scratch_shapes=[
            pltpu.VMEM((HEADS_PER_GROUP, KQ + 1) + tile, jnp.float32),
            pltpu.VMEM((HEADS_PER_GROUP,) + tile, jnp.float32),
            pltpu.VMEM((HEADS_PER_GROUP,) + tile, jnp.float32),
            pltpu.VMEM(values.shape, values.dtype),
            pltpu.SemaphoreType.DMA,
        ],
        compiler_params=pltpu.CompilerParams(vmem_limit_bytes=24 * MIB),
        name="attend",
    )(lists, near, keys, in_hbm(values), queries, *others)
    partial = [partial[0]] + [from_quarter(partial[mask], mask) for mask in range(1, CTX)]
    merged = pl.pallas_call(
        merge_kernel,
        out_shape=jax.ShapeDtypeStruct((groups, local_rows, width), jnp.bfloat16),
        in_specs=[vmem] * CTX,
        out_specs=vmem,
        compiler_params=pltpu.CompilerParams(vmem_limit_bytes=4 * MIB),
        name="merge",
    )(*partial)
    if groups > 1:
        merged = over_seq(merged, same_member)
    return merged.transpose(1, 0, 2).reshape(local_rows, groups * width)


def solution(mesh):
    return jax.shard_map(
        body,
        mesh=mesh,
        in_specs=(
            P(("seq", "ctx"), None),
            P(("seq", "ctx"), None),
            P(("seq", "ctx"), None),
            P("seq", "ctx", None),
            P("seq", "ctx", None),
            P("seq", None, "ctx", None),
            P("seq", None, "ctx"),
        ),
        out_specs=P(("seq", "ctx"), None),
        check_vma=False,
    )
```

```python
import math

import jax
import jax.numpy as jnp
from jax import lax
from jax.experimental import pallas as pl
from jax.experimental.pallas import tpu as pltpu
from jax.sharding import PartitionSpec as P

HEADS_PER_GROUP = 8
TILE_QUERY_ROWS = 64
KROWS = 128
KQ = 12
LANES = 128
CTX = 4
NEAR = 2 * KROWS // TILE_QUERY_ROWS
AT_ONCE = 4
PAIRS_AT_ONCE = 8
MIB = 1024 * 1024
LOG2E = 1.4426950408889634


def nt(a, b):
    return lax.dot_general(a, b, (((1,), (1,)), ((), ())), preferred_element_type=jnp.float32)


def pack_kernel(*refs):
    sources, out_ref, targets = refs[:4], refs[4], refs[5:9]
    scratch, sems = refs[9:]
    copies = [
        pltpu.make_async_copy(source, target, sems.at[i])
        for i, (source, target) in enumerate(zip(sources, targets))
    ]
    for copy in copies:
        copy.start()
    keys, values, ids, counts = targets
    members, groups, _, full = out_ref.shape
    blocks = ids.shape[1]
    scratch[...] = jnp.zeros_like(scratch)
    for copy in copies:
        copy.wait()
    for member in range(members):
        for group in range(groups):
            block = group * members + member
            scratch[0:1, :KQ] = ids[0, block].astype(jnp.float32)
            scratch[1:2, :blocks] = counts[...].astype(jnp.float32)
            out_ref[member, group, :, : full - 2 * LANES] = keys[group]
            out_ref[member, group, :, full - 2 * LANES : full - LANES] = values[group]
            out_ref[member, group, :, full - LANES :] = scratch[...].astype(jnp.bfloat16)


def fetch_kernel(*refs):
    count = len(refs) // 2
    copies = [
        pltpu.make_async_copy(refs[i], refs[count + i], refs[-1].at[i]) for i in range(count)
    ]
    for copy in copies:
        copy.start()
    for copy in copies:
        copy.wait()


def attend_kernel(lists, near_ref, k_ref, v_hbm, *refs):
    q_refs, out_refs = refs[:CTX], refs[CTX : 2 * CTX]
    s_scr, near_scr, m_scr, l_scr, a_scr, v_ref, sem = refs[2 * CTX :]
    v_copy = pltpu.make_async_copy(v_hbm, v_ref, sem)
    v_copy.start()
    groups, local_rows, _ = q_refs[0].shape
    member = lax.rem(lax.axis_index("seq"), HEADS_PER_GROUP)
    quarter = lax.axis_index("ctx")
    rows = TILE_QUERY_ROWS
    head_size = k_ref.shape[2]
    scale = LOG2E / math.sqrt(head_size)
    lane = lax.broadcasted_iota(jnp.int32, (rows, LANES), 1)
    sublane = lax.broadcasted_iota(jnp.int32, (rows, LANES), 0)

    def one_block(group):
        block = group * HEADS_PER_GROUP + member
        near = []
        for back in range(NEAR):
            place = jnp.maximum(group - jnp.where(member < back, 1, 0), 0)
            near.append(near_ref[lax.rem(member - back + HEADS_PER_GROUP, HEADS_PER_GROUP), place])
        near = jnp.concatenate(near + near, axis=0)
        near_k, near_v = near[:, :head_size], near[:, head_size : 2 * head_size]
        position = (block - lane // local_rows) * rows + quarter * local_rows + lane % local_rows
        token = block * rows + ((sublane // local_rows) ^ quarter) * local_rows + sublane % local_rows
        oldest = jnp.maximum((block * rows // KROWS - 1) * KROWS, 0)
        near_ok = (lane < rows) & (position <= token) & (position >= oldest)

        def columns_of(head):
            return pl.ds(pl.multiple_of(head * head_size, LANES), head_size)

        def queries_of(head):
            return jnp.concatenate([q_ref[group, :, columns_of(head)] for q_ref in q_refs], axis=0)

        def over_heads(step):
            def several(turn, carry):
                for i in range(AT_ONCE):
                    step(turn * AT_ONCE + i)
                return carry

            lax.fori_loop(0, HEADS_PER_GROUP // AT_ONCE, several, 0)

        def over_pairs(step):
            def several(turn, place):
                head, slot = place
                for i in range(PAIRS_AT_ONCE):
                    here = jnp.minimum(head, HEADS_PER_GROUP - 1)
                    slot = jnp.where(head < HEADS_PER_GROUP, slot, KQ)
                    count = lists[here, group, 1, block]
                    blocks = [lists[here, group, 0, slot + part] for part in range(2)]
                    step(turn * PAIRS_AT_ONCE + i, here, slot, count, blocks)
                    last = slot + 2 >= count
                    head = jnp.where(last, head + 1, head)
                    slot = jnp.where(last, 0, slot + 2)
                return head, slot

            pairs = 0
            for head in range(HEADS_PER_GROUP):
                pairs = pairs + (lists[head, group, 1, block] + 1) // 2
            turns = (pairs + PAIRS_AT_ONCE - 1) // PAIRS_AT_ONCE
            lax.fori_loop(0, turns, several, (jnp.int32(0), jnp.int32(0)))

        def near_scores(head):
            s = jnp.where(near_ok, nt(queries_of(head), near_k), -jnp.inf)
            near_scr[head] = s
            m_scr[head] = s

        def pair_scores(place, head, slot, count, blocks):
            keys = jnp.concatenate([k_ref[one] for one in blocks], axis=0)
            both = nt(queries_of(head), keys)
            high = m_scr[head]
            for part in range(2):
                s = both[:, part * KROWS : (part + 1) * KROWS]
                s = jnp.where(slot + part < count, s, -jnp.inf)
                s_scr[place, part] = s
                high = jnp.maximum(high, s)
            m_scr[head] = high

        def near_sums(head):
            p = jnp.exp2(near_scr[head] * scale - m_scr[head])
            l_scr[head] = p
            a_scr[head] = jnp.dot(
                p.astype(jnp.bfloat16), near_v, preferred_element_type=jnp.float32
            )

        def pair_sums(place, head, slot, count, blocks):
            top = m_scr[head]
            both = [jnp.exp2(s_scr[place, part] * scale - top) for part in range(2)]
            mixed = jnp.dot(
                jnp.concatenate([p.astype(jnp.bfloat16) for p in both], axis=1),
                jnp.concatenate([v_ref[one] for one in blocks], axis=0),
                preferred_element_type=jnp.float32,
            )
            l_scr[head] += both[0] + both[1]
            a_scr[head] += mixed

        over_heads(near_scores)
        over_pairs(pair_scores)
        for head in range(HEADS_PER_GROUP):
            top = jnp.max(m_scr[head], axis=1, keepdims=True) * scale
            m_scr[head] = jnp.broadcast_to(top, (rows, LANES))
        if groups == 1:
            v_copy.wait()
        else:
            pl.when(group == 0)(v_copy.wait)
        over_heads(near_sums)
        over_pairs(pair_sums)
        stats = jnp.zeros((rows, LANES), jnp.float32)
        for head in range(HEADS_PER_GROUP):
            acc = a_scr[head].astype(jnp.bfloat16)
            for part, out_ref in enumerate(out_refs):
                out_ref[group, :, head * head_size : (head + 1) * head_size] = acc[
                    part * local_rows : (part + 1) * local_rows
                ]
            total = jnp.sum(l_scr[head], axis=1, keepdims=True)
            stats = jnp.where(lane == head, m_scr[head], stats)
            stats = jnp.where(lane == head + HEADS_PER_GROUP, total, stats)
        packed = jnp.zeros((rows, LANES), jnp.float32)
        for step in range(3):
            part = stats.astype(jnp.bfloat16).astype(jnp.float32)
            stats = stats - part
            shift = step * 2 * HEADS_PER_GROUP
            packed = packed + (pltpu.roll(part, shift, 1) if shift else part)
        packed = packed.astype(jnp.bfloat16)
        width = HEADS_PER_GROUP * head_size
        for part, out_ref in enumerate(out_refs):
            out_ref[group, :, width:] = packed[part * local_rows : (part + 1) * local_rows]

    if groups == 1:
        one_block(0)
    else:
        pl.loop(0, groups)(one_block)


def merge_kernel(*refs):
    in_refs, out_ref = refs[:-1], refs[-1]
    groups, local_rows, full = in_refs[0].shape
    width = full - LANES
    head_size = width // HEADS_PER_GROUP

    def one_block(group):
        stats = []
        for in_ref in in_refs:
            packed = in_ref[group, :, width:].astype(jnp.float32)
            one = packed
            for step in (1, 2):
                one = one + pltpu.roll(packed, LANES - step * 2 * HEADS_PER_GROUP, 1)
            stats.append(one)
        top = stats[0]
        for one in stats[1:]:
            top = jnp.maximum(top, one)
        factors = [jnp.exp2(one - top) for one in stats]
        total = jnp.zeros((local_rows, LANES), jnp.float32)
        for one, factor in zip(stats, factors):
            total = total + pltpu.roll(one, LANES - HEADS_PER_GROUP, 1) * factor
        inverse = 1.0 / total
        factors = [factor * inverse for factor in factors]
        for head in range(HEADS_PER_GROUP):
            columns = slice(head * head_size, (head + 1) * head_size)
            mixed = jnp.zeros((local_rows, head_size), jnp.float32)
            for in_ref, factor in zip(in_refs, factors):
                mixed = mixed + in_ref[group, :, columns].astype(jnp.float32) * (
                    factor[:, head : head + 1]
                )
            out_ref[group, :, columns] = mixed.astype(jnp.bfloat16)

    if groups == 1:
        one_block(0)
    else:
        pl.loop(0, groups)(one_block)


def from_quarter(value, mask):
    return lax.ppermute(value, "ctx", [(device, device ^ mask) for device in range(CTX)])


def body(
    queries, new_token_keys, new_token_values, cache_keys, cache_values, block_ids, block_counts
):
    seq_count = lax.axis_size("seq")
    head_size = cache_keys.shape[2]
    local_rows = queries.shape[0]
    blocks = block_ids.shape[1]
    groups = seq_count // HEADS_PER_GROUP
    width = HEADS_PER_GROUP * head_size
    assert lax.axis_size("ctx") == CTX and cache_keys.shape[0] == 1
    assert local_rows * CTX == TILE_QUERY_ROWS and blocks <= LANES
    same_group = same_member = None
    if groups > 1:
        same_group = [
            [g * HEADS_PER_GROUP + r for r in range(HEADS_PER_GROUP)] for g in range(groups)
        ]
        same_member = [
            [g * HEADS_PER_GROUP + r for g in range(groups)] for r in range(HEADS_PER_GROUP)
        ]

    def over_seq(pieces, members):
        return lax.all_to_all(
            pieces, "seq", split_axis=0, concat_axis=0, tiled=True, axis_index_groups=members
        )

    def in_hbm(value):
        return pltpu.with_memory_space_constraint(value, pltpu.HBM)

    def to_groups(rows):
        pieces = rows.reshape(local_rows, groups, -1).transpose(1, 0, 2)
        return pieces if groups == 1 else over_seq(pieces, same_member)

    vmem = pl.BlockSpec(memory_space=pltpu.VMEM)
    hbm = pl.BlockSpec(memory_space=pltpu.HBM)
    smem = pl.BlockSpec(memory_space=pltpu.SMEM)
    queries = to_groups(queries)
    others = [from_quarter(queries, mask) for mask in range(1, CTX)]
    small = (
        to_groups(new_token_keys),
        to_groups(new_token_values),
        block_ids,
        block_counts.reshape(1, blocks),
    )
    packed = pl.pallas_call(
        pack_kernel,
        out_shape=jax.ShapeDtypeStruct(
            (HEADS_PER_GROUP, groups, local_rows, 2 * head_size + LANES), jnp.bfloat16
        ),
        in_specs=[hbm] * 4,
        out_specs=vmem,
        scratch_shapes=[pltpu.VMEM(one.shape, one.dtype) for one in small]
        + [pltpu.VMEM((local_rows, LANES), jnp.float32), pltpu.SemaphoreType.DMA((4,))],
        compiler_params=pltpu.CompilerParams(vmem_limit_bytes=4 * MIB),
        cost_estimate=pl.CostEstimate(flops=0, bytes_accessed=12 * MIB, transcendentals=0),
        name="pack",
    )(*[in_hbm(one) for one in small])
    large = (queries, cache_keys.reshape(-1, KROWS, head_size))
    queries, keys = pl.pallas_call(
        fetch_kernel,
        out_shape=[jax.ShapeDtypeStruct(one.shape, one.dtype) for one in large],
        in_specs=[hbm] * 2,
        out_specs=[vmem] * 2,
        scratch_shapes=[pltpu.SemaphoreType.DMA((2,))],
        compiler_params=pltpu.CompilerParams(vmem_limit_bytes=4 * MIB),
        cost_estimate=pl.CostEstimate(flops=0, bytes_accessed=4 * MIB, transcendentals=0),
        name="fetch",
    )(*[in_hbm(one) for one in large])
    near = over_seq(packed, same_group)
    lists = near[:, :, :2, 2 * head_size :].astype(jnp.int32)
    tile = (TILE_QUERY_ROWS, KROWS)
    values = cache_values.reshape(-1, KROWS, head_size)
    partial = pl.pallas_call(
        attend_kernel,
        out_shape=[
            jax.ShapeDtypeStruct((groups, local_rows, width + LANES), jnp.bfloat16)
        ] * CTX,
        in_specs=[smem, vmem, vmem, hbm] + [vmem] * CTX,
        out_specs=[vmem] * CTX,
        scratch_shapes=[
            pltpu.VMEM((HEADS_PER_GROUP * KQ // 2, 2) + tile, jnp.float32),
            pltpu.VMEM((HEADS_PER_GROUP,) + tile, jnp.float32),
            pltpu.VMEM((HEADS_PER_GROUP,) + tile, jnp.float32),
            pltpu.VMEM((HEADS_PER_GROUP,) + tile, jnp.float32),
            pltpu.VMEM((HEADS_PER_GROUP,) + tile, jnp.float32),
            pltpu.VMEM(values.shape, values.dtype),
            pltpu.SemaphoreType.DMA,
        ],
        compiler_params=pltpu.CompilerParams(vmem_limit_bytes=24 * MIB),
        name="attend",
    )(lists, near, keys, in_hbm(values), queries, *others)
    partial = [from_quarter(partial[mask], mask) for mask in (2, 3, 1)] + [partial[0]]
    merged = pl.pallas_call(
        merge_kernel,
        out_shape=jax.ShapeDtypeStruct((groups, local_rows, width), jnp.bfloat16),
        in_specs=[vmem] * CTX,
        out_specs=vmem,
        compiler_params=pltpu.CompilerParams(vmem_limit_bytes=4 * MIB),
        name="merge",
    )(*partial)
    if groups > 1:
        merged = over_seq(merged, same_member)
    return merged.transpose(1, 0, 2).reshape(local_rows, groups * width)


def solution(mesh):
    return jax.shard_map(
        body,
        mesh=mesh,
        in_specs=(
            P(("seq", "ctx"), None),
            P(("seq", "ctx"), None),
            P(("seq", "ctx"), None),
            P("seq", "ctx", None),
            P("seq", "ctx", None),
            P("seq", None, "ctx", None),
            P("seq", None, "ctx"),
        ),
        out_specs=P(("seq", "ctx"), None),
        check_vma=False,
    )
```

```python
import math

import jax
import jax.numpy as jnp
from jax import lax
from jax.experimental import pallas as pl
from jax.experimental.pallas import tpu as pltpu
from jax.sharding import PartitionSpec as P

HEADS_PER_GROUP = 8
TILE_QUERY_ROWS = 64
KROWS = 128
KQ = 12
LANES = 128
CTX = 4
NEAR = 2 * KROWS // TILE_QUERY_ROWS
AT_ONCE = 4
V_COPIES = 4
MIB = 1024 * 1024
LOG2E = 1.4426950408889634


def nt(a, b):
    return lax.dot_general(a, b, (((1,), (1,)), ((), ())), preferred_element_type=jnp.float32)


def pack_kernel(keys, values, ids, counts, out_ref, own_ids, own_counts, scratch, tiles, sems):
    members, groups, local_rows, full = out_ref.shape
    blocks = ids.shape[1]
    head_size = keys.shape[2]
    own = [
        pltpu.make_async_copy(ids, own_ids, sems.at[0]),
        pltpu.make_async_copy(counts, own_counts, sems.at[1]),
    ]
    pairs = []
    for member in range(members):
        for half, source in enumerate((keys, values)):
            columns = pl.ds(half * head_size, head_size)
            pairs.append(
                pltpu.make_async_copy(
                    source, out_ref.at[member, :, :, columns], sems.at[3 + 2 * member + half]
                )
            )
    for copy in own + pairs:
        copy.start()
    scratch[...] = jnp.zeros_like(scratch)
    for copy in own:
        copy.wait()
    scratch[1:2, :blocks] = own_counts[...].astype(jnp.float32)
    for member in range(members):
        for group in range(groups):
            block = group * members + member
            scratch[0:1, :KQ] = own_ids[0, block].astype(jnp.float32)
            tiles[member, group] = scratch[...].astype(jnp.bfloat16)
    lists = pltpu.make_async_copy(
        tiles, out_ref.at[:, :, :, pl.ds(full - LANES, LANES)], sems.at[2]
    )
    lists.start()
    for copy in pairs:
        copy.wait()
    lists.wait()


def fetch_kernel(*refs):
    count = len(refs) // 2
    copies = [
        pltpu.make_async_copy(refs[i], refs[count + i], refs[-1].at[i]) for i in range(count)
    ]
    for copy in copies:
        copy.start()
    for copy in copies:
        copy.wait()


def attend_kernel(lists, near_ref, k_ref, v_hbm, *refs):
    q_refs, out_refs = refs[:CTX], refs[CTX : 2 * CTX]
    s_scr, m_scr, l_scr, v_ref, sem = refs[2 * CTX :]
    each = v_hbm.shape[0] // V_COPIES
    v_copies = []
    for i in range(V_COPIES):
        part = pl.ds(i * each, each)
        v_copies.append(pltpu.make_async_copy(v_hbm.at[part], v_ref.at[part], sem.at[i]))
        v_copies[i].start()
    groups, local_rows, _ = q_refs[0].shape
    member = lax.rem(lax.axis_index("seq"), HEADS_PER_GROUP)
    quarter = lax.axis_index("ctx")
    rows = TILE_QUERY_ROWS
    head_size = k_ref.shape[2]
    scale = LOG2E / math.sqrt(head_size)
    lane = lax.broadcasted_iota(jnp.int32, (rows, LANES), 1)
    sublane = lax.broadcasted_iota(jnp.int32, (rows, LANES), 0)

    def one_block(group):
        block = group * HEADS_PER_GROUP + member
        near = []
        for back in range(NEAR):
            place = jnp.maximum(group - jnp.where(member < back, 1, 0), 0)
            near.append(near_ref[lax.rem(member - back + HEADS_PER_GROUP, HEADS_PER_GROUP), place])
        near = jnp.concatenate(near + near, axis=0)
        near_k, near_v = near[:, :head_size], near[:, head_size : 2 * head_size]
        position = (block - lane // local_rows) * rows + quarter * local_rows + lane % local_rows
        token = block * rows + ((sublane // local_rows) ^ quarter) * local_rows + sublane % local_rows
        oldest = jnp.maximum((block * rows // KROWS - 1) * KROWS, 0)
        near_ok = (lane < rows) & (position <= token) & (position >= oldest)

        def columns_of(head):
            return pl.ds(pl.multiple_of(head * head_size, LANES), head_size)

        def scores(head):
            count = lists[head, group, 1, block]
            q = jnp.concatenate([q_ref[group, :, columns_of(head)] for q_ref in q_refs], axis=0)
            s = jnp.where(near_ok, nt(q, near_k), -jnp.inf)
            s_scr[head, KQ] = s
            high = s
            for slot in range(0, KQ, 2):
                keys = [k_ref[lists[head, group, 0, slot + i]] for i in range(2)]
                both = nt(q, jnp.concatenate(keys, axis=0))
                for i in range(2):
                    s = both[:, i * KROWS : (i + 1) * KROWS]
                    s = jnp.where(slot + i < count, s, -jnp.inf)
                    s_scr[head, slot + i] = s
                    high = jnp.maximum(high, s)
            m_scr[head] = high

        def sums(head):
            top = m_scr[head]
            total = jnp.exp2(s_scr[head, KQ] * scale - top)
            acc = jnp.dot(total.astype(jnp.bfloat16), near_v, preferred_element_type=jnp.float32)
            for slot in range(0, KQ, 2):
                pair = []
                for part in (slot, slot + 1):
                    p = jnp.exp2(s_scr[head, part] * scale - top)
                    total = total + p
                    pair.append(p.astype(jnp.bfloat16))
                values = [v_ref[lists[head, group, 0, slot + i]] for i in range(2)]
                acc = acc + jnp.dot(
                    jnp.concatenate(pair, axis=1),
                    jnp.concatenate(values, axis=0),
                    preferred_element_type=jnp.float32,
                )
            acc = acc.astype(jnp.bfloat16)
            for part, out_ref in enumerate(out_refs):
                out_ref[group, :, columns_of(head)] = acc[
                    part * local_rows : (part + 1) * local_rows
                ]
            l_scr[head] = total

        def in_steps(step):
            def several(turn, carry):
                for i in range(AT_ONCE):
                    step(turn * AT_ONCE + i)
                return carry

            lax.fori_loop(0, HEADS_PER_GROUP // AT_ONCE, several, 0)

        in_steps(scores)
        for head in range(HEADS_PER_GROUP):
            top = jnp.max(m_scr[head], axis=1, keepdims=True) * scale
            m_scr[head] = jnp.broadcast_to(top, (rows, LANES))
        for v_copy in v_copies:
            if groups == 1:
                v_copy.wait()
            else:
                pl.when(group == 0)(v_copy.wait)
        in_steps(sums)
        stats = jnp.zeros((rows, LANES), jnp.float32)
        for head in range(HEADS_PER_GROUP):
            total = jnp.sum(l_scr[head], axis=1, keepdims=True)
            stats = jnp.where(lane == head, m_scr[head], stats)
            stats = jnp.where(lane == head + HEADS_PER_GROUP, total, stats)
        packed = jnp.zeros((rows, LANES), jnp.float32)
        for step in range(3):
            part = stats.astype(jnp.bfloat16).astype(jnp.float32)
            stats = stats - part
            shift = step * 2 * HEADS_PER_GROUP
            packed = packed + (pltpu.roll(part, shift, 1) if shift else part)
        packed = packed.astype(jnp.bfloat16)
        width = HEADS_PER_GROUP * head_size
        for part, out_ref in enumerate(out_refs):
            out_ref[group, :, width:] = packed[part * local_rows : (part + 1) * local_rows]

    if groups == 1:
        one_block(0)
    else:
        pl.loop(0, groups)(one_block)


def merge_kernel(*refs):
    in_refs, out_ref = refs[:-1], refs[-1]
    groups, local_rows, full = in_refs[0].shape
    width = full - LANES
    head_size = width // HEADS_PER_GROUP

    def one_block(group):
        stats = []
        for in_ref in in_refs:
            packed = in_ref[group, :, width:].astype(jnp.float32)
            one = packed
            for step in (1, 2):
                one = one + pltpu.roll(packed, LANES - step * 2 * HEADS_PER_GROUP, 1)
            stats.append(one)
        top = stats[0]
        for one in stats[1:]:
            top = jnp.maximum(top, one)
        factors = [jnp.exp2(one - top) for one in stats]
        total = jnp.zeros((local_rows, LANES), jnp.float32)
        for one, factor in zip(stats, factors):
            total = total + pltpu.roll(one, LANES - HEADS_PER_GROUP, 1) * factor
        inverse = 1.0 / total
        factors = [factor * inverse for factor in factors]
        for head in range(HEADS_PER_GROUP):
            columns = slice(head * head_size, (head + 1) * head_size)
            mixed = jnp.zeros((local_rows, head_size), jnp.float32)
            for in_ref, factor in zip(in_refs, factors):
                mixed = mixed + in_ref[group, :, columns].astype(jnp.float32) * (
                    factor[:, head : head + 1]
                )
            out_ref[group, :, columns] = mixed.astype(jnp.bfloat16)

    if groups == 1:
        one_block(0)
    else:
        pl.loop(0, groups)(one_block)


def from_quarter(value, mask):
    return lax.ppermute(value, "ctx", [(device, device ^ mask) for device in range(CTX)])


def body(
    queries, new_token_keys, new_token_values, cache_keys, cache_values, block_ids, block_counts
):
    seq_count = lax.axis_size("seq")
    head_size = cache_keys.shape[2]
    local_rows = queries.shape[0]
    blocks = block_ids.shape[1]
    groups = seq_count // HEADS_PER_GROUP
    width = HEADS_PER_GROUP * head_size
    assert lax.axis_size("ctx") == CTX and cache_keys.shape[0] == 1
    assert local_rows * CTX == TILE_QUERY_ROWS and blocks <= LANES
    same_group = same_member = None
    if groups > 1:
        same_group = [
            [g * HEADS_PER_GROUP + r for r in range(HEADS_PER_GROUP)] for g in range(groups)
        ]
        same_member = [
            [g * HEADS_PER_GROUP + r for g in range(groups)] for r in range(HEADS_PER_GROUP)
        ]

    def over_seq(pieces, members):
        return lax.all_to_all(
            pieces, "seq", split_axis=0, concat_axis=0, tiled=True, axis_index_groups=members
        )

    def in_hbm(value):
        return pltpu.with_memory_space_constraint(value, pltpu.HBM)

    def to_groups(rows):
        pieces = rows.reshape(local_rows, groups, -1).transpose(1, 0, 2)
        return pieces if groups == 1 else over_seq(pieces, same_member)

    vmem = pl.BlockSpec(memory_space=pltpu.VMEM)
    hbm = pl.BlockSpec(memory_space=pltpu.HBM)
    smem = pl.BlockSpec(memory_space=pltpu.SMEM)
    queries = to_groups(queries)
    others = [from_quarter(queries, mask) for mask in range(1, CTX)]
    small = (
        to_groups(new_token_keys),
        to_groups(new_token_values),
        block_ids,
        block_counts.reshape(1, blocks),
    )
    packed = pl.pallas_call(
        pack_kernel,
        out_shape=jax.ShapeDtypeStruct(
            (HEADS_PER_GROUP, groups, local_rows, 2 * head_size + LANES), jnp.bfloat16
        ),
        in_specs=[hbm] * 4,
        out_specs=hbm,
        scratch_shapes=[
            pltpu.VMEM(small[2].shape, jnp.int32),
            pltpu.VMEM(small[3].shape, jnp.int32),
            pltpu.VMEM((local_rows, LANES), jnp.float32),
            pltpu.VMEM((HEADS_PER_GROUP, groups, local_rows, LANES), jnp.bfloat16),
            pltpu.SemaphoreType.DMA((3 + 2 * HEADS_PER_GROUP,)),
        ],
        compiler_params=pltpu.CompilerParams(vmem_limit_bytes=4 * MIB),
        cost_estimate=pl.CostEstimate(flops=0, bytes_accessed=12 * MIB, transcendentals=0),
        name="pack",
    )(*[in_hbm(one) for one in small])
    large = (queries, cache_keys.reshape(-1, KROWS, head_size))
    queries, keys = pl.pallas_call(
        fetch_kernel,
        out_shape=[jax.ShapeDtypeStruct(one.shape, one.dtype) for one in large],
        in_specs=[hbm] * 2,
        out_specs=[vmem] * 2,
        scratch_shapes=[pltpu.SemaphoreType.DMA((2,))],
        compiler_params=pltpu.CompilerParams(vmem_limit_bytes=4 * MIB),
        cost_estimate=pl.CostEstimate(flops=0, bytes_accessed=4 * MIB, transcendentals=0),
        name="fetch",
    )(*[in_hbm(one) for one in large])
    near = over_seq(packed, same_group)
    lists = near[:, :, :2, 2 * head_size :].astype(jnp.int32)
    tile = (TILE_QUERY_ROWS, KROWS)
    values = cache_values.reshape(-1, KROWS, head_size)
    partial = pl.pallas_call(
        attend_kernel,
        out_shape=[
            jax.ShapeDtypeStruct((groups, local_rows, width + LANES), jnp.bfloat16)
        ] * CTX,
        in_specs=[smem, vmem, vmem, hbm] + [vmem] * CTX,
        out_specs=[vmem] * CTX,
        scratch_shapes=[
            pltpu.VMEM((HEADS_PER_GROUP, KQ + 1) + tile, jnp.float32),
            pltpu.VMEM((HEADS_PER_GROUP,) + tile, jnp.float32),
            pltpu.VMEM((HEADS_PER_GROUP,) + tile, jnp.float32),
            pltpu.VMEM(values.shape, values.dtype),
            pltpu.SemaphoreType.DMA((V_COPIES,)),
        ],
        compiler_params=pltpu.CompilerParams(vmem_limit_bytes=24 * MIB),
        name="attend",
    )(lists, near, keys, in_hbm(values), queries, *others)
    partial = [partial[0]] + [from_quarter(partial[mask], mask) for mask in range(1, CTX)]
    merged = pl.pallas_call(
        merge_kernel,
        out_shape=jax.ShapeDtypeStruct((groups, local_rows, width), jnp.bfloat16),
        in_specs=[vmem] * CTX,
        out_specs=vmem,
        compiler_params=pltpu.CompilerParams(vmem_limit_bytes=4 * MIB),
        name="merge",
    )(*partial)
    if groups > 1:
        merged = over_seq(merged, same_member)
    return merged.transpose(1, 0, 2).reshape(local_rows, groups * width)


def solution(mesh):
    return jax.shard_map(
        body,
        mesh=mesh,
        in_specs=(
            P(("seq", "ctx"), None),
            P(("seq", "ctx"), None),
            P(("seq", "ctx"), None),
            P("seq", "ctx", None),
            P("seq", "ctx", None),
            P("seq", None, "ctx", None),
            P("seq", None, "ctx"),
        ),
        out_specs=P(("seq", "ctx"), None),
        check_vma=False,
    )
```

```python
import math

import jax
import jax.numpy as jnp
from jax import lax
from jax.experimental import pallas as pl
from jax.experimental.pallas import tpu as pltpu
from jax.sharding import PartitionSpec as P

HEADS_PER_GROUP = 8
TILE_QUERY_ROWS = 64
KROWS = 128
KQ = 12
LANES = 128
CTX = 4
NEAR = 2 * KROWS // TILE_QUERY_ROWS
AT_ONCE = 4
LIST_ROWS = 8
COUNTS_AT = 16
MIB = 1024 * 1024
LOG2E = 1.4426950408889634


def nt(a, b):
    return lax.dot_general(a, b, (((1,), (1,)), ((), ())), preferred_element_type=jnp.float32)


def pack_kernel(*refs):
    sources, out_ref, targets = refs[:4], refs[4], refs[5:9]
    scratch, sems = refs[9:]
    copies = [
        pltpu.make_async_copy(source, target, sems.at[i])
        for i, (source, target) in enumerate(zip(sources, targets))
    ]
    for copy in copies:
        copy.start()
    keys, values, ids, counts = targets
    members, groups, _, _ = out_ref.shape
    local_rows = keys.shape[1]
    blocks = ids.shape[1]
    scratch[...] = jnp.zeros_like(scratch)
    for copy in copies:
        copy.wait()
    scratch[0:1, COUNTS_AT : COUNTS_AT + blocks] = counts[...].astype(jnp.float32)
    for member in range(members):
        for group in range(groups):
            block = group * members + member
            scratch[0:1, :KQ] = ids[0, block].astype(jnp.float32)
            out_ref[member, group, :local_rows] = keys[group]
            out_ref[member, group, local_rows : 2 * local_rows] = values[group]
            out_ref[member, group, 2 * local_rows :] = scratch[...].astype(jnp.bfloat16)


def fetch_kernel(*refs):
    count = len(refs) // 2
    copies = [
        pltpu.make_async_copy(refs[i], refs[count + i], refs[-1].at[i]) for i in range(count)
    ]
    for copy in copies:
        copy.start()
    for copy in copies:
        copy.wait()


def attend_kernel(lists, near_ref, k_ref, v_hbm, *refs):
    q_refs, out_refs = refs[:CTX], refs[CTX : 2 * CTX]
    s_scr, m_scr, l_scr, v_ref, sem = refs[2 * CTX :]
    v_copy = pltpu.make_async_copy(v_hbm, v_ref, sem)
    v_copy.start()
    groups, local_rows, _ = q_refs[0].shape
    member = lax.rem(lax.axis_index("seq"), HEADS_PER_GROUP)
    quarter = lax.axis_index("ctx")
    rows = TILE_QUERY_ROWS
    head_size = k_ref.shape[2]
    scale = LOG2E / math.sqrt(head_size)
    shift, mask = local_rows.bit_length() - 1, local_rows - 1
    lane = lax.broadcasted_iota(jnp.int32, (rows, LANES), 1)
    sublane = lax.broadcasted_iota(jnp.int32, (rows, LANES), 0)

    def one_block(group):
        block = group * HEADS_PER_GROUP + member
        near = []
        for back in range(NEAR):
            place = jnp.maximum(group - jnp.where(member < back, 1, 0), 0)
            near.append(near_ref[lax.rem(member - back + HEADS_PER_GROUP, HEADS_PER_GROUP), place])
        near_k = jnp.concatenate([one[:local_rows] for one in near] * 2, axis=0)
        near_v = jnp.concatenate([one[local_rows : 2 * local_rows] for one in near] * 2, axis=0)
        position = (block - (lane >> shift)) * rows + quarter * local_rows + (lane & mask)
        token = block * rows + ((sublane >> shift) ^ quarter) * local_rows + (sublane & mask)
        oldest = jnp.maximum((block * rows // KROWS - 1) * KROWS, 0)
        near_ok = (lane < rows) & (position <= token) & (position >= oldest)

        def columns_of(head):
            return pl.ds(pl.multiple_of(head * head_size, LANES), head_size)

        def scores(head):
            count = lists[head, group, COUNTS_AT + block]
            q = jnp.concatenate([q_ref[group, :, columns_of(head)] for q_ref in q_refs], axis=0)
            s = jnp.where(near_ok, nt(q, near_k), -jnp.inf)
            s_scr[head, KQ] = s
            high = s
            for slot in range(0, KQ, 2):
                keys = [k_ref[lists[head, group, slot + i]] for i in range(2)]
                both = nt(q, jnp.concatenate(keys, axis=0))
                for i in range(2):
                    s = both[:, i * KROWS : (i + 1) * KROWS]
                    s = jnp.where(slot + i < count, s, -jnp.inf)
                    s_scr[head, slot + i] = s
                    high = jnp.maximum(high, s)
            m_scr[head] = high

        def sums(head):
            top = m_scr[head]
            total = jnp.exp2(s_scr[head, KQ] * scale - top)
            acc = jnp.dot(total.astype(jnp.bfloat16), near_v, preferred_element_type=jnp.float32)
            for slot in range(0, KQ, 2):
                pair = []
                for part in (slot, slot + 1):
                    p = jnp.exp2(s_scr[head, part] * scale - top)
                    total = total + p
                    pair.append(p.astype(jnp.bfloat16))
                values = [v_ref[lists[head, group, slot + i]] for i in range(2)]
                acc = acc + jnp.dot(
                    jnp.concatenate(pair, axis=1),
                    jnp.concatenate(values, axis=0),
                    preferred_element_type=jnp.float32,
                )
            acc = acc.astype(jnp.bfloat16)
            for part, out_ref in enumerate(out_refs):
                out_ref[group, :, columns_of(head)] = acc[
                    part * local_rows : (part + 1) * local_rows
                ]
            l_scr[head] = total

        def in_steps(step):
            def several(turn, carry):
                for i in range(AT_ONCE):
                    step(turn * AT_ONCE + i)
                return carry

            lax.fori_loop(0, HEADS_PER_GROUP // AT_ONCE, several, 0)

        in_steps(scores)
        for head in range(HEADS_PER_GROUP):
            top = jnp.max(m_scr[head], axis=1, keepdims=True) * scale
            m_scr[head] = jnp.broadcast_to(top, (rows, LANES))
        if groups == 1:
            v_copy.wait()
        else:
            pl.when(group == 0)(v_copy.wait)
        in_steps(sums)
        stats = jnp.zeros((rows, LANES), jnp.float32)
        for head in range(HEADS_PER_GROUP):
            total = jnp.sum(l_scr[head], axis=1, keepdims=True)
            stats = jnp.where(lane == head, m_scr[head], stats)
            stats = jnp.where(lane == head + HEADS_PER_GROUP, total, stats)
        packed = jnp.zeros((rows, LANES), jnp.float32)
        for step in range(3):
            part = stats.astype(jnp.bfloat16).astype(jnp.float32)
            stats = stats - part
            by = step * 2 * HEADS_PER_GROUP
            packed = packed + (pltpu.roll(part, by, 1) if by else part)
        packed = packed.astype(jnp.bfloat16)
        width = HEADS_PER_GROUP * head_size
        for part, out_ref in enumerate(out_refs):
            out_ref[group, :, width:] = packed[part * local_rows : (part + 1) * local_rows]

    if groups == 1:
        one_block(0)
    else:
        pl.loop(0, groups)(one_block)


def merge_kernel(*refs):
    in_refs, out_ref = refs[:-1], refs[-1]
    groups, local_rows, full = in_refs[0].shape
    width = full - LANES
    head_size = width // HEADS_PER_GROUP

    def one_block(group):
        stats = []
        for in_ref in in_refs:
            packed = in_ref[group, :, width:].astype(jnp.float32)
            one = packed
            for step in (1, 2):
                one = one + pltpu.roll(packed, LANES - step * 2 * HEADS_PER_GROUP, 1)
            stats.append(one)
        top = stats[0]
        for one in stats[1:]:
            top = jnp.maximum(top, one)
        factors = [jnp.exp2(one - top) for one in stats]
        total = jnp.zeros((local_rows, LANES), jnp.float32)
        for one, factor in zip(stats, factors):
            total = total + pltpu.roll(one, LANES - HEADS_PER_GROUP, 1) * factor
        inverse = 1.0 / total
        factors = [factor * inverse for factor in factors]
        for head in range(HEADS_PER_GROUP):
            columns = slice(head * head_size, (head + 1) * head_size)
            mixed = jnp.zeros((local_rows, head_size), jnp.float32)
            for in_ref, factor in zip(in_refs, factors):
                mixed = mixed + in_ref[group, :, columns].astype(jnp.float32) * (
                    factor[:, head : head + 1]
                )
            out_ref[group, :, columns] = mixed.astype(jnp.bfloat16)

    if groups == 1:
        one_block(0)
    else:
        pl.loop(0, groups)(one_block)


def from_quarter(value, mask):
    return lax.ppermute(value, "ctx", [(device, device ^ mask) for device in range(CTX)])


def body(
    queries, new_token_keys, new_token_values, cache_keys, cache_values, block_ids, block_counts
):
    seq_count = lax.axis_size("seq")
    head_size = cache_keys.shape[2]
    local_rows = queries.shape[0]
    blocks = block_ids.shape[1]
    groups = seq_count // HEADS_PER_GROUP
    width = HEADS_PER_GROUP * head_size
    assert lax.axis_size("ctx") == CTX and cache_keys.shape[0] == 1
    assert local_rows * CTX == TILE_QUERY_ROWS and blocks <= LANES - COUNTS_AT
    assert head_size == LANES and local_rows & (local_rows - 1) == 0
    same_group = same_member = None
    if groups > 1:
        same_group = [
            [g * HEADS_PER_GROUP + r for r in range(HEADS_PER_GROUP)] for g in range(groups)
        ]
        same_member = [
            [g * HEADS_PER_GROUP + r for g in range(groups)] for r in range(HEADS_PER_GROUP)
        ]

    def over_seq(pieces, members):
        return lax.all_to_all(
            pieces, "seq", split_axis=0, concat_axis=0, tiled=True, axis_index_groups=members
        )

    def in_hbm(value):
        return pltpu.with_memory_space_constraint(value, pltpu.HBM)

    def to_groups(rows):
        pieces = rows.reshape(local_rows, groups, -1).transpose(1, 0, 2)
        return pieces if groups == 1 else over_seq(pieces, same_member)

    vmem = pl.BlockSpec(memory_space=pltpu.VMEM)
    hbm = pl.BlockSpec(memory_space=pltpu.HBM)
    smem = pl.BlockSpec(memory_space=pltpu.SMEM)
    queries = to_groups(queries)
    others = [from_quarter(queries, mask) for mask in range(1, CTX)]
    small = (
        to_groups(new_token_keys),
        to_groups(new_token_values),
        block_ids,
        block_counts.reshape(1, blocks),
    )
    packed = pl.pallas_call(
        pack_kernel,
        out_shape=jax.ShapeDtypeStruct(
            (HEADS_PER_GROUP, groups, 2 * local_rows + LIST_ROWS, LANES), jnp.bfloat16
        ),
        in_specs=[hbm] * 4,
        out_specs=vmem,
        scratch_shapes=[pltpu.VMEM(one.shape, one.dtype) for one in small]
        + [pltpu.VMEM((LIST_ROWS, LANES), jnp.float32), pltpu.SemaphoreType.DMA((4,))],
        compiler_params=pltpu.CompilerParams(vmem_limit_bytes=4 * MIB),
        cost_estimate=pl.CostEstimate(flops=0, bytes_accessed=12 * MIB, transcendentals=0),
        name="pack",
    )(*[in_hbm(one) for one in small])
    large = (queries, cache_keys.reshape(-1, KROWS, head_size))
    queries, keys = pl.pallas_call(
        fetch_kernel,
        out_shape=[jax.ShapeDtypeStruct(one.shape, one.dtype) for one in large],
        in_specs=[hbm] * 2,
        out_specs=[vmem] * 2,
        scratch_shapes=[pltpu.SemaphoreType.DMA((2,))],
        compiler_params=pltpu.CompilerParams(vmem_limit_bytes=4 * MIB),
        cost_estimate=pl.CostEstimate(flops=0, bytes_accessed=4 * MIB, transcendentals=0),
        name="fetch",
    )(*[in_hbm(one) for one in large])
    near = over_seq(packed, same_group)
    lists = near[:, :, 2 * local_rows].astype(jnp.int32)
    tile = (TILE_QUERY_ROWS, KROWS)
    values = cache_values.reshape(-1, KROWS, head_size)
    partial = pl.pallas_call(
        attend_kernel,
        out_shape=[
            jax.ShapeDtypeStruct((groups, local_rows, width + LANES), jnp.bfloat16)
        ] * CTX,
        in_specs=[smem, vmem, vmem, hbm] + [vmem] * CTX,
        out_specs=[vmem] * CTX,
        scratch_shapes=[
            pltpu.VMEM((HEADS_PER_GROUP, KQ + 1) + tile, jnp.float32),
            pltpu.VMEM((HEADS_PER_GROUP,) + tile, jnp.float32),
            pltpu.VMEM((HEADS_PER_GROUP,) + tile, jnp.float32),
            pltpu.VMEM(values.shape, values.dtype),
            pltpu.SemaphoreType.DMA,
        ],
        compiler_params=pltpu.CompilerParams(vmem_limit_bytes=24 * MIB),
        name="attend",
    )(lists, near, keys, in_hbm(values), queries, *others)
    partial = [from_quarter(partial[mask], mask) for mask in (2, 3, 1)] + [partial[0]]
    merged = pl.pallas_call(
        merge_kernel,
        out_shape=jax.ShapeDtypeStruct((groups, local_rows, width), jnp.bfloat16),
        in_specs=[vmem] * CTX,
        out_specs=vmem,
        compiler_params=pltpu.CompilerParams(vmem_limit_bytes=4 * MIB),
        name="merge",
    )(*partial)
    if groups > 1:
        merged = over_seq(merged, same_member)
    return merged.transpose(1, 0, 2).reshape(local_rows, groups * width)


def solution(mesh):
    return jax.shard_map(
        body,
        mesh=mesh,
        in_specs=(
            P(("seq", "ctx"), None),
            P(("seq", "ctx"), None),
            P(("seq", "ctx"), None),
            P("seq", "ctx", None),
            P("seq", "ctx", None),
            P("seq", None, "ctx", None),
            P("seq", None, "ctx"),
        ),
        out_specs=P(("seq", "ctx"), None),
        check_vma=False,
    )
```

```python
import math

import jax
import jax.numpy as jnp
from jax import lax
from jax.experimental import pallas as pl
from jax.experimental.pallas import tpu as pltpu
from jax.sharding import PartitionSpec as P

HEADS_PER_GROUP = 8
TILE_QUERY_ROWS = 64
KROWS = 128
KQ = 12
LANES = 128
CTX = 4
NEAR = 2 * KROWS // TILE_QUERY_ROWS
AT_ONCE = 4
SLOTS_AT_ONCE = 4
LIST_ROWS = 8
COUNTS_AT = 16
MIB = 1024 * 1024
LOG2E = 1.4426950408889634


def nt(a, b):
    return lax.dot_general(a, b, (((1,), (1,)), ((), ())), preferred_element_type=jnp.float32)


def pack_kernel(*refs):
    sources, out_ref, targets = refs[:4], refs[4], refs[5:9]
    scratch, sems = refs[9:]
    copies = [
        pltpu.make_async_copy(source, target, sems.at[i])
        for i, (source, target) in enumerate(zip(sources, targets))
    ]
    for copy in copies:
        copy.start()
    keys, values, ids, counts = targets
    members, groups, _, _ = out_ref.shape
    local_rows = keys.shape[1]
    blocks = ids.shape[1]
    scratch[...] = jnp.zeros_like(scratch)
    for copy in copies:
        copy.wait()
    scratch[0:1, COUNTS_AT : COUNTS_AT + blocks] = counts[...].astype(jnp.float32)
    for member in range(members):
        for group in range(groups):
            block = group * members + member
            scratch[0:1, :KQ] = ids[0, block].astype(jnp.float32)
            out_ref[member, group, :local_rows] = keys[group]
            out_ref[member, group, local_rows : 2 * local_rows] = values[group]
            out_ref[member, group, 2 * local_rows :] = scratch[...].astype(jnp.bfloat16)


def fetch_kernel(*refs):
    count = len(refs) // 2
    copies = [
        pltpu.make_async_copy(refs[i], refs[count + i], refs[-1].at[i]) for i in range(count)
    ]
    for copy in copies:
        copy.start()
    for copy in copies:
        copy.wait()


def attend_kernel(lists, near_ref, k_ref, v_hbm, *refs):
    q_refs, out_refs = refs[:CTX], refs[CTX : 2 * CTX]
    s_scr, m_scr, l_scr, v_ref, sem = refs[2 * CTX :]
    v_copy = pltpu.make_async_copy(v_hbm, v_ref, sem)
    v_copy.start()
    groups, local_rows, _ = q_refs[0].shape
    member = lax.rem(lax.axis_index("seq"), HEADS_PER_GROUP)
    quarter = lax.axis_index("ctx")
    rows = TILE_QUERY_ROWS
    head_size = k_ref.shape[2]
    scale = LOG2E / math.sqrt(head_size)
    shift, mask = local_rows.bit_length() - 1, local_rows - 1
    lane = lax.broadcasted_iota(jnp.int32, (rows, LANES), 1)
    sublane = lax.broadcasted_iota(jnp.int32, (rows, LANES), 0)

    def one_block(group):
        block = group * HEADS_PER_GROUP + member
        near = []
        for back in range(NEAR):
            place = jnp.maximum(group - jnp.where(member < back, 1, 0), 0)
            near.append(near_ref[lax.rem(member - back + HEADS_PER_GROUP, HEADS_PER_GROUP), place])
        near_k = jnp.concatenate([one[:local_rows] for one in near] * 2, axis=0)
        near_v = jnp.concatenate([one[local_rows : 2 * local_rows] for one in near] * 2, axis=0)
        position = (block - (lane >> shift)) * rows + quarter * local_rows + (lane & mask)
        token = block * rows + ((sublane >> shift) ^ quarter) * local_rows + (sublane & mask)
        oldest = jnp.maximum((block * rows // KROWS - 1) * KROWS, 0)
        near_ok = (lane < rows) & (position <= token) & (position >= oldest)

        def columns_of(head):
            return pl.ds(pl.multiple_of(head * head_size, LANES), head_size)

        def scores(head):
            count = lists[head, group, COUNTS_AT + block]
            q = jnp.concatenate([q_ref[group, :, columns_of(head)] for q_ref in q_refs], axis=0)
            s = jnp.where(near_ok, nt(q, near_k), -jnp.inf)
            s_scr[head, KQ] = s
            high = s
            for slot in range(0, KQ, SLOTS_AT_ONCE):
                keys = [k_ref[lists[head, group, slot + i]] for i in range(SLOTS_AT_ONCE)]
                several = nt(q, jnp.concatenate(keys, axis=0))
                for i in range(SLOTS_AT_ONCE):
                    s = several[:, i * KROWS : (i + 1) * KROWS]
                    s = jnp.where(slot + i < count, s, -jnp.inf)
                    s_scr[head, slot + i] = s
                    high = jnp.maximum(high, s)
            m_scr[head] = high

        def sums(head):
            top = m_scr[head]
            total = jnp.exp2(s_scr[head, KQ] * scale - top)
            acc = jnp.dot(total.astype(jnp.bfloat16), near_v, preferred_element_type=jnp.float32)
            for slot in range(0, KQ, SLOTS_AT_ONCE):
                weights = []
                for part in range(slot, slot + SLOTS_AT_ONCE):
                    p = jnp.exp2(s_scr[head, part] * scale - top)
                    total = total + p
                    weights.append(p.astype(jnp.bfloat16))
                values = [v_ref[lists[head, group, slot + i]] for i in range(SLOTS_AT_ONCE)]
                acc = acc + jnp.dot(
                    jnp.concatenate(weights, axis=1),
                    jnp.concatenate(values, axis=0),
                    preferred_element_type=jnp.float32,
                )
            acc = acc.astype(jnp.bfloat16)
            for part, out_ref in enumerate(out_refs):
                out_ref[group, :, columns_of(head)] = acc[
                    part * local_rows : (part + 1) * local_rows
                ]
            l_scr[head] = total

        def in_steps(step):
            def several(turn, carry):
                for i in range(AT_ONCE):
                    step(turn * AT_ONCE + i)
                return carry

            lax.fori_loop(0, HEADS_PER_GROUP // AT_ONCE, several, 0)

        in_steps(scores)
        for head in range(HEADS_PER_GROUP):
            top = jnp.max(m_scr[head], axis=1, keepdims=True) * scale
            m_scr[head] = jnp.broadcast_to(top, (rows, LANES))
        if groups == 1:
            v_copy.wait()
        else:
            pl.when(group == 0)(v_copy.wait)
        in_steps(sums)
        stats = jnp.zeros((rows, LANES), jnp.float32)
        for head in range(HEADS_PER_GROUP):
            total = jnp.sum(l_scr[head], axis=1, keepdims=True)
            stats = jnp.where(lane == head, m_scr[head], stats)
            stats = jnp.where(lane == head + HEADS_PER_GROUP, total, stats)
        packed = jnp.zeros((rows, LANES), jnp.float32)
        for step in range(3):
            part = stats.astype(jnp.bfloat16).astype(jnp.float32)
            stats = stats - part
            by = step * 2 * HEADS_PER_GROUP
            packed = packed + (pltpu.roll(part, by, 1) if by else part)
        packed = packed.astype(jnp.bfloat16)
        width = HEADS_PER_GROUP * head_size
        for part, out_ref in enumerate(out_refs):
            out_ref[group, :, width:] = packed[part * local_rows : (part + 1) * local_rows]

    if groups == 1:
        one_block(0)
    else:
        pl.loop(0, groups)(one_block)


def merge_kernel(*refs):
    in_refs, out_ref = refs[:-1], refs[-1]
    groups, local_rows, full = in_refs[0].shape
    width = full - LANES
    head_size = width // HEADS_PER_GROUP

    def one_block(group):
        stats = []
        for in_ref in in_refs:
            packed = in_ref[group, :, width:].astype(jnp.float32)
            one = packed
            for step in (1, 2):
                one = one + pltpu.roll(packed, LANES - step * 2 * HEADS_PER_GROUP, 1)
            stats.append(one)
        top = stats[0]
        for one in stats[1:]:
            top = jnp.maximum(top, one)
        factors = [jnp.exp2(one - top) for one in stats]
        total = jnp.zeros((local_rows, LANES), jnp.float32)
        for one, factor in zip(stats, factors):
            total = total + pltpu.roll(one, LANES - HEADS_PER_GROUP, 1) * factor
        inverse = 1.0 / total
        factors = [factor * inverse for factor in factors]
        for head in range(HEADS_PER_GROUP):
            columns = slice(head * head_size, (head + 1) * head_size)
            mixed = jnp.zeros((local_rows, head_size), jnp.float32)
            for in_ref, factor in zip(in_refs, factors):
                mixed = mixed + in_ref[group, :, columns].astype(jnp.float32) * (
                    factor[:, head : head + 1]
                )
            out_ref[group, :, columns] = mixed.astype(jnp.bfloat16)

    if groups == 1:
        one_block(0)
    else:
        pl.loop(0, groups)(one_block)


def from_quarter(value, mask):
    return lax.ppermute(value, "ctx", [(device, device ^ mask) for device in range(CTX)])


def body(
    queries, new_token_keys, new_token_values, cache_keys, cache_values, block_ids, block_counts
):
    seq_count = lax.axis_size("seq")
    head_size = cache_keys.shape[2]
    local_rows = queries.shape[0]
    blocks = block_ids.shape[1]
    groups = seq_count // HEADS_PER_GROUP
    width = HEADS_PER_GROUP * head_size
    assert lax.axis_size("ctx") == CTX and cache_keys.shape[0] == 1
    assert local_rows * CTX == TILE_QUERY_ROWS and blocks <= LANES - COUNTS_AT
    assert head_size == LANES and local_rows & (local_rows - 1) == 0
    same_group = same_member = None
    if groups > 1:
        same_group = [
            [g * HEADS_PER_GROUP + r for r in range(HEADS_PER_GROUP)] for g in range(groups)
        ]
        same_member = [
            [g * HEADS_PER_GROUP + r for g in range(groups)] for r in range(HEADS_PER_GROUP)
        ]

    def over_seq(pieces, members):
        return lax.all_to_all(
            pieces, "seq", split_axis=0, concat_axis=0, tiled=True, axis_index_groups=members
        )

    def in_hbm(value):
        return pltpu.with_memory_space_constraint(value, pltpu.HBM)

    def to_groups(rows):
        pieces = rows.reshape(local_rows, groups, -1).transpose(1, 0, 2)
        return pieces if groups == 1 else over_seq(pieces, same_member)

    vmem = pl.BlockSpec(memory_space=pltpu.VMEM)
    hbm = pl.BlockSpec(memory_space=pltpu.HBM)
    smem = pl.BlockSpec(memory_space=pltpu.SMEM)
    queries = to_groups(queries)
    others = [from_quarter(queries, mask) for mask in range(1, CTX)]
    small = (
        to_groups(new_token_keys),
        to_groups(new_token_values),
        block_ids,
        block_counts.reshape(1, blocks),
    )
    packed = pl.pallas_call(
        pack_kernel,
        out_shape=jax.ShapeDtypeStruct(
            (HEADS_PER_GROUP, groups, 2 * local_rows + LIST_ROWS, LANES), jnp.bfloat16
        ),
        in_specs=[hbm] * 4,
        out_specs=vmem,
        scratch_shapes=[pltpu.VMEM(one.shape, one.dtype) for one in small]
        + [pltpu.VMEM((LIST_ROWS, LANES), jnp.float32), pltpu.SemaphoreType.DMA((4,))],
        compiler_params=pltpu.CompilerParams(vmem_limit_bytes=4 * MIB),
        cost_estimate=pl.CostEstimate(flops=0, bytes_accessed=12 * MIB, transcendentals=0),
        name="pack",
    )(*[in_hbm(one) for one in small])
    large = (queries, cache_keys.reshape(-1, KROWS, head_size))
    queries, keys = pl.pallas_call(
        fetch_kernel,
        out_shape=[jax.ShapeDtypeStruct(one.shape, one.dtype) for one in large],
        in_specs=[hbm] * 2,
        out_specs=[vmem] * 2,
        scratch_shapes=[pltpu.SemaphoreType.DMA((2,))],
        compiler_params=pltpu.CompilerParams(vmem_limit_bytes=4 * MIB),
        cost_estimate=pl.CostEstimate(flops=0, bytes_accessed=4 * MIB, transcendentals=0),
        name="fetch",
    )(*[in_hbm(one) for one in large])
    near = over_seq(packed, same_group)
    lists = near[:, :, 2 * local_rows].astype(jnp.int32)
    tile = (TILE_QUERY_ROWS, KROWS)
    values = cache_values.reshape(-1, KROWS, head_size)
    partial = pl.pallas_call(
        attend_kernel,
        out_shape=[
            jax.ShapeDtypeStruct((groups, local_rows, width + LANES), jnp.bfloat16)
        ] * CTX,
        in_specs=[smem, vmem, vmem, hbm] + [vmem] * CTX,
        out_specs=[vmem] * CTX,
        scratch_shapes=[
            pltpu.VMEM((HEADS_PER_GROUP, KQ + 1) + tile, jnp.float32),
            pltpu.VMEM((HEADS_PER_GROUP,) + tile, jnp.float32),
            pltpu.VMEM((HEADS_PER_GROUP,) + tile, jnp.float32),
            pltpu.VMEM(values.shape, values.dtype),
            pltpu.SemaphoreType.DMA,
        ],
        compiler_params=pltpu.CompilerParams(vmem_limit_bytes=24 * MIB),
        name="attend",
    )(lists, near, keys, in_hbm(values), queries, *others)
    partial = [from_quarter(partial[mask], mask) for mask in (2, 3, 1)] + [partial[0]]
    merged = pl.pallas_call(
        merge_kernel,
        out_shape=jax.ShapeDtypeStruct((groups, local_rows, width), jnp.bfloat16),
        in_specs=[vmem] * CTX,
        out_specs=vmem,
        compiler_params=pltpu.CompilerParams(vmem_limit_bytes=4 * MIB),
        name="merge",
    )(*partial)
    if groups > 1:
        merged = over_seq(merged, same_member)
    return merged.transpose(1, 0, 2).reshape(local_rows, groups * width)


def solution(mesh):
    return jax.shard_map(
        body,
        mesh=mesh,
        in_specs=(
            P(("seq", "ctx"), None),
            P(("seq", "ctx"), None),
            P(("seq", "ctx"), None),
            P("seq", "ctx", None),
            P("seq", "ctx", None),
            P("seq", None, "ctx", None),
            P("seq", None, "ctx"),
        ),
        out_specs=P(("seq", "ctx"), None),
        check_vma=False,
    )
```

```python
import math

import jax
import jax.numpy as jnp
from jax import lax
from jax.experimental import pallas as pl
from jax.experimental.pallas import tpu as pltpu
from jax.sharding import PartitionSpec as P

HEADS_PER_GROUP = 8
TILE_QUERY_ROWS = 64
KROWS = 128
KQ = 12
LANES = 128
CTX = 4
NEAR = 2 * KROWS // TILE_QUERY_ROWS
AT_ONCE = 4
SLOTS_AT_ONCE = 4
COUNTS_AT = 16
MIB = 1024 * 1024
LOG2E = 1.4426950408889634


def nt(a, b):
    return lax.dot_general(a, b, (((1,), (1,)), ((), ())), preferred_element_type=jnp.float32)


def pack_kernel(*refs):
    sources, (lists, pairs), targets, sems = refs[:4], refs[4:6], refs[6:10], refs[10]
    copies = [
        pltpu.make_async_copy(source, target, sems.at[i])
        for i, (source, target) in enumerate(zip(sources, targets))
    ]
    for copy in copies:
        copy.start()
    keys, values, ids, counts = targets
    members, groups = lists.shape[:2]
    blocks, head_size = ids.shape[1], keys.shape[2]
    lists[...] = jnp.zeros_like(lists)
    for copy in copies:
        copy.wait()
    pairs[:, :, :head_size] = keys[...]
    pairs[:, :, head_size:] = values[...]
    for member in range(members):
        for group in range(groups):
            lists[member, group, :, :KQ] = ids[0, group * members + member]
            lists[member, group, :, COUNTS_AT : COUNTS_AT + blocks] = counts[...]


def fetch_kernel(*refs):
    count = len(refs) // 2
    copies = [
        pltpu.make_async_copy(refs[i], refs[count + i], refs[-1].at[i]) for i in range(count)
    ]
    for copy in copies:
        copy.start()
    for copy in copies:
        copy.wait()


def attend_kernel(lists, k_ref, v_hbm, *refs):
    near_refs, refs = refs[:NEAR], refs[NEAR:]
    q_refs, out_refs = refs[:CTX], refs[CTX : 2 * CTX]
    s_scr, m_scr, l_scr, v_ref, sem = refs[2 * CTX :]
    v_copy = pltpu.make_async_copy(v_hbm, v_ref, sem)
    v_copy.start()
    groups, local_rows, _ = q_refs[0].shape
    member = lax.rem(lax.axis_index("seq"), HEADS_PER_GROUP)
    quarter = lax.axis_index("ctx")
    rows = TILE_QUERY_ROWS
    head_size = k_ref.shape[2]
    scale = LOG2E / math.sqrt(head_size)
    shift, mask = local_rows.bit_length() - 1, local_rows - 1
    lane = lax.broadcasted_iota(jnp.int32, (rows, LANES), 1)
    sublane = lax.broadcasted_iota(jnp.int32, (rows, LANES), 0)

    def one_block(group):
        block = group * HEADS_PER_GROUP + member
        near = []
        for back, near_ref in enumerate(near_refs):
            near.append(near_ref[jnp.maximum(group - jnp.where(member < back, 1, 0), 0)])
        near = jnp.concatenate(near + near, axis=0)
        near_k, near_v = near[:, :head_size], near[:, head_size:]
        position = (block - (lane >> shift)) * rows + quarter * local_rows + (lane & mask)
        token = block * rows + ((sublane >> shift) ^ quarter) * local_rows + (sublane & mask)
        oldest = jnp.maximum((block * rows // KROWS - 1) * KROWS, 0)
        near_ok = (lane < rows) & (position <= token) & (position >= oldest)

        def columns_of(head):
            return pl.ds(pl.multiple_of(head * head_size, LANES), head_size)

        def scores(head):
            count = lists[head, group, 0, COUNTS_AT + block]
            q = jnp.concatenate([q_ref[group, :, columns_of(head)] for q_ref in q_refs], axis=0)
            s = jnp.where(near_ok, nt(q, near_k), -jnp.inf)
            s_scr[head, KQ] = s
            high = s
            for slot in range(0, KQ, SLOTS_AT_ONCE):
                keys = [k_ref[lists[head, group, 0, slot + i]] for i in range(SLOTS_AT_ONCE)]
                several = nt(q, jnp.concatenate(keys, axis=0))
                for i in range(SLOTS_AT_ONCE):
                    s = several[:, i * KROWS : (i + 1) * KROWS]
                    s = jnp.where(slot + i < count, s, -jnp.inf)
                    s_scr[head, slot + i] = s
                    high = jnp.maximum(high, s)
            m_scr[head] = high

        def sums(head):
            top = m_scr[head]
            total = jnp.exp2(s_scr[head, KQ] * scale - top)
            acc = jnp.dot(total.astype(jnp.bfloat16), near_v, preferred_element_type=jnp.float32)
            for slot in range(0, KQ, SLOTS_AT_ONCE):
                weights = []
                for part in range(slot, slot + SLOTS_AT_ONCE):
                    p = jnp.exp2(s_scr[head, part] * scale - top)
                    total = total + p
                    weights.append(p.astype(jnp.bfloat16))
                values = [v_ref[lists[head, group, 0, slot + i]] for i in range(SLOTS_AT_ONCE)]
                acc = acc + jnp.dot(
                    jnp.concatenate(weights, axis=1),
                    jnp.concatenate(values, axis=0),
                    preferred_element_type=jnp.float32,
                )
            acc = acc.astype(jnp.bfloat16)
            for part, out_ref in enumerate(out_refs):
                out_ref[group, :, columns_of(head)] = acc[
                    part * local_rows : (part + 1) * local_rows
                ]
            l_scr[head] = total

        def in_steps(step):
            def several(turn, carry):
                for i in range(AT_ONCE):
                    step(turn * AT_ONCE + i)
                return carry

            lax.fori_loop(0, HEADS_PER_GROUP // AT_ONCE, several, 0)

        in_steps(scores)
        for head in range(HEADS_PER_GROUP):
            top = jnp.max(m_scr[head], axis=1, keepdims=True) * scale
            m_scr[head] = jnp.broadcast_to(top, (rows, LANES))
        if groups == 1:
            v_copy.wait()
        else:
            pl.when(group == 0)(v_copy.wait)
        in_steps(sums)
        stats = jnp.zeros((rows, LANES), jnp.float32)
        for head in range(HEADS_PER_GROUP):
            total = jnp.sum(l_scr[head], axis=1, keepdims=True)
            stats = jnp.where(lane == head, m_scr[head], stats)
            stats = jnp.where(lane == head + HEADS_PER_GROUP, total, stats)
        packed = jnp.zeros((rows, LANES), jnp.float32)
        for step in range(3):
            part = stats.astype(jnp.bfloat16).astype(jnp.float32)
            stats = stats - part
            by = step * 2 * HEADS_PER_GROUP
            packed = packed + (pltpu.roll(part, by, 1) if by else part)
        packed = packed.astype(jnp.bfloat16)
        width = HEADS_PER_GROUP * head_size
        for part, out_ref in enumerate(out_refs):
            out_ref[group, :, width:] = packed[part * local_rows : (part + 1) * local_rows]

    if groups == 1:
        one_block(0)
    else:
        pl.loop(0, groups)(one_block)


def merge_kernel(*refs):
    in_refs, out_ref = refs[:-1], refs[-1]
    groups, local_rows, full = in_refs[0].shape
    width = full - LANES
    head_size = width // HEADS_PER_GROUP

    def one_block(group):
        stats = []
        for in_ref in in_refs:
            packed = in_ref[group, :, width:].astype(jnp.float32)
            one = packed
            for step in (1, 2):
                one = one + pltpu.roll(packed, LANES - step * 2 * HEADS_PER_GROUP, 1)
            stats.append(one)
        top = stats[0]
        for one in stats[1:]:
            top = jnp.maximum(top, one)
        factors = [jnp.exp2(one - top) for one in stats]
        total = jnp.zeros((local_rows, LANES), jnp.float32)
        for one, factor in zip(stats, factors):
            total = total + pltpu.roll(one, LANES - HEADS_PER_GROUP, 1) * factor
        inverse = 1.0 / total
        factors = [factor * inverse for factor in factors]
        for head in range(HEADS_PER_GROUP):
            columns = slice(head * head_size, (head + 1) * head_size)
            mixed = jnp.zeros((local_rows, head_size), jnp.float32)
            for in_ref, factor in zip(in_refs, factors):
                mixed = mixed + in_ref[group, :, columns].astype(jnp.float32) * (
                    factor[:, head : head + 1]
                )
            out_ref[group, :, columns] = mixed.astype(jnp.bfloat16)

    if groups == 1:
        one_block(0)
    else:
        pl.loop(0, groups)(one_block)


def from_member(value, back, seq_count):
    pairs = []
    for device in range(seq_count):
        member = device % HEADS_PER_GROUP
        target = device - member + (member + back) % HEADS_PER_GROUP
        if target > device or seq_count > HEADS_PER_GROUP:
            pairs.append((device, target))
    return lax.ppermute(value, "seq", pairs)


def from_quarter(value, mask):
    return lax.ppermute(value, "ctx", [(device, device ^ mask) for device in range(CTX)])


def body(
    queries, new_token_keys, new_token_values, cache_keys, cache_values, block_ids, block_counts
):
    seq_count = lax.axis_size("seq")
    head_size = cache_keys.shape[2]
    local_rows = queries.shape[0]
    blocks = block_ids.shape[1]
    groups = seq_count // HEADS_PER_GROUP
    width = HEADS_PER_GROUP * head_size
    assert lax.axis_size("ctx") == CTX and cache_keys.shape[0] == 1
    assert local_rows * CTX == TILE_QUERY_ROWS and blocks <= LANES - COUNTS_AT
    assert head_size == LANES and local_rows & (local_rows - 1) == 0
    same_group = same_member = None
    if groups > 1:
        same_group = [
            [g * HEADS_PER_GROUP + r for r in range(HEADS_PER_GROUP)] for g in range(groups)
        ]
        same_member = [
            [g * HEADS_PER_GROUP + r for g in range(groups)] for r in range(HEADS_PER_GROUP)
        ]

    def over_seq(pieces, members):
        return lax.all_to_all(
            pieces, "seq", split_axis=0, concat_axis=0, tiled=True, axis_index_groups=members
        )

    def in_hbm(value):
        return pltpu.with_memory_space_constraint(value, pltpu.HBM)

    def to_groups(rows):
        pieces = rows.reshape(local_rows, groups, -1).transpose(1, 0, 2)
        return pieces if groups == 1 else over_seq(pieces, same_member)

    vmem = pl.BlockSpec(memory_space=pltpu.VMEM)
    hbm = pl.BlockSpec(memory_space=pltpu.HBM)
    smem = pl.BlockSpec(memory_space=pltpu.SMEM)
    queries = to_groups(queries)
    others = [from_quarter(queries, mask) for mask in range(1, CTX)]
    small = (
        to_groups(new_token_keys),
        to_groups(new_token_values),
        block_ids,
        block_counts.reshape(1, blocks),
    )
    lists, pairs = pl.pallas_call(
        pack_kernel,
        out_shape=[
            jax.ShapeDtypeStruct((HEADS_PER_GROUP, groups, 1, LANES), jnp.int32),
            jax.ShapeDtypeStruct((groups, local_rows, 2 * head_size), jnp.bfloat16),
        ],
        in_specs=[hbm] * 4,
        out_specs=[vmem] * 2,
        scratch_shapes=[pltpu.VMEM(one.shape, one.dtype) for one in small]
        + [pltpu.SemaphoreType.DMA((4,))],
        compiler_params=pltpu.CompilerParams(vmem_limit_bytes=4 * MIB),
        cost_estimate=pl.CostEstimate(flops=0, bytes_accessed=MIB, transcendentals=0),
        name="pack",
    )(*[in_hbm(one) for one in small])
    lists = over_seq(lists, same_group)
    near = [pairs] + [from_member(pairs, back, seq_count) for back in range(1, NEAR)]
    large = (queries, cache_keys.reshape(-1, KROWS, head_size))
    queries, keys = pl.pallas_call(
        fetch_kernel,
        out_shape=[jax.ShapeDtypeStruct(one.shape, one.dtype) for one in large],
        in_specs=[hbm] * 2,
        out_specs=[vmem] * 2,
        scratch_shapes=[pltpu.SemaphoreType.DMA((2,))],
        compiler_params=pltpu.CompilerParams(vmem_limit_bytes=4 * MIB),
        cost_estimate=pl.CostEstimate(flops=0, bytes_accessed=4 * MIB, transcendentals=0),
        name="fetch",
    )(*[in_hbm(one) for one in large])
    tile = (TILE_QUERY_ROWS, KROWS)
    values = cache_values.reshape(-1, KROWS, head_size)
    partial = pl.pallas_call(
        attend_kernel,
        out_shape=[
            jax.ShapeDtypeStruct((groups, local_rows, width + LANES), jnp.bfloat16)
        ] * CTX,
        in_specs=[smem, vmem, hbm] + [vmem] * (NEAR + CTX),
        out_specs=[vmem] * CTX,
        scratch_shapes=[
            pltpu.VMEM((HEADS_PER_GROUP, KQ + 1) + tile, jnp.float32),
            pltpu.VMEM((HEADS_PER_GROUP,) + tile, jnp.float32),
            pltpu.VMEM((HEADS_PER_GROUP,) + tile, jnp.float32),
            pltpu.VMEM(values.shape, values.dtype),
            pltpu.SemaphoreType.DMA,
        ],
        compiler_params=pltpu.CompilerParams(vmem_limit_bytes=24 * MIB),
        name="attend",
    )(lists, keys, in_hbm(values), *near, queries, *others)
    partial = [from_quarter(partial[mask], mask) for mask in (2, 3, 1)] + [partial[0]]
    merged = pl.pallas_call(
        merge_kernel,
        out_shape=jax.ShapeDtypeStruct((groups, local_rows, width), jnp.bfloat16),
        in_specs=[vmem] * CTX,
        out_specs=vmem,
        compiler_params=pltpu.CompilerParams(vmem_limit_bytes=4 * MIB),
        name="merge",
    )(*partial)
    if groups > 1:
        merged = over_seq(merged, same_member)
    return merged.transpose(1, 0, 2).reshape(local_rows, groups * width)


def solution(mesh):
    return jax.shard_map(
        body,
        mesh=mesh,
        in_specs=(
            P(("seq", "ctx"), None),
            P(("seq", "ctx"), None),
            P(("seq", "ctx"), None),
            P("seq", "ctx", None),
            P("seq", "ctx", None),
            P("seq", None, "ctx", None),
            P("seq", None, "ctx"),
        ),
        out_specs=P(("seq", "ctx"), None),
        check_vma=False,
    )
```

```python
import math

import jax
import jax.numpy as jnp
from jax import lax
from jax.experimental import pallas as pl
from jax.experimental.pallas import tpu as pltpu
from jax.sharding import PartitionSpec as P

HEADS_PER_GROUP = 8
TILE_QUERY_ROWS = 64
KROWS = 128
KQ = 12
LANES = 128
CTX = 4
NEAR = 2 * KROWS // TILE_QUERY_ROWS
AT_ONCE = 4
SLOTS_AT_ONCE = 4
LIST_ROWS = 8
COUNTS_AT = 16
MIB = 1024 * 1024
LOG2E = 1.4426950408889634


def nt(a, b):
    return lax.dot_general(a, b, (((1,), (1,)), ((), ())), preferred_element_type=jnp.float32)


def pack_kernel(*refs):
    sources, out_ref, targets = refs[:4], refs[4], refs[5:9]
    scratch, sems = refs[9:]
    copies = [
        pltpu.make_async_copy(source, target, sems.at[i])
        for i, (source, target) in enumerate(zip(sources, targets))
    ]
    for copy in copies:
        copy.start()
    keys, values, ids, counts = targets
    members, groups, _, _ = out_ref.shape
    local_rows = keys.shape[1]
    blocks = ids.shape[1]
    scratch[...] = jnp.zeros_like(scratch)
    for copy in copies:
        copy.wait()
    for member in range(members):
        for group in range(groups):
            row = scratch.at[member * groups + group]
            row[0:1, :KQ] = ids[0, group * members + member].astype(jnp.float32)
            row[0:1, COUNTS_AT : COUNTS_AT + blocks] = counts[...].astype(jnp.float32)
            out_ref[member, group, :local_rows] = keys[group]
            out_ref[member, group, local_rows : 2 * local_rows] = values[group]
    for member in range(members):
        for group in range(groups):
            row = scratch[member * groups + group]
            out_ref[member, group, 2 * local_rows :] = row.astype(jnp.bfloat16)


def fetch_kernel(*refs):
    count = len(refs) // 2
    copies = []
    for i in range(count):
        source, target = refs[i], refs[count + i]
        part = source.at[pl.ds(0, target.shape[0])]
        copies.append(pltpu.make_async_copy(part, target, refs[-1].at[i]))
    for copy in copies:
        copy.start()
    for copy in copies:
        copy.wait()


def attend_kernel(lists, near_ref, k_ref, v_hbm, v_early, *refs):
    q_refs, out_refs = refs[:CTX], refs[CTX : 2 * CTX]
    s_scr, m_scr, l_scr, v_ref, sem = refs[2 * CTX :]
    early = v_early.shape[0]
    late = pl.ds(early, v_hbm.shape[0] - early)
    v_copies = [
        pltpu.make_async_copy(v_hbm.at[late], v_ref.at[late], sem.at[0]),
        pltpu.make_async_copy(v_early, v_ref.at[pl.ds(0, early)], sem.at[1]),
    ]
    for v_copy in v_copies:
        v_copy.start()
    groups, local_rows, _ = q_refs[0].shape
    member = lax.rem(lax.axis_index("seq"), HEADS_PER_GROUP)
    quarter = lax.axis_index("ctx")
    rows = TILE_QUERY_ROWS
    head_size = k_ref.shape[2]
    scale = LOG2E / math.sqrt(head_size)
    shift, mask = local_rows.bit_length() - 1, local_rows - 1
    lane = lax.broadcasted_iota(jnp.int32, (rows, LANES), 1)
    sublane = lax.broadcasted_iota(jnp.int32, (rows, LANES), 0)

    def one_block(group):
        block = group * HEADS_PER_GROUP + member
        near = []
        for back in range(NEAR):
            place = jnp.maximum(group - jnp.where(member < back, 1, 0), 0)
            near.append(near_ref[lax.rem(member - back + HEADS_PER_GROUP, HEADS_PER_GROUP), place])
        near_k = jnp.concatenate([one[:local_rows] for one in near] * 2, axis=0)
        near_v = jnp.concatenate([one[local_rows : 2 * local_rows] for one in near] * 2, axis=0)
        position = (block - (lane >> shift)) * rows + quarter * local_rows + (lane & mask)
        token = block * rows + ((sublane >> shift) ^ quarter) * local_rows + (sublane & mask)
        oldest = jnp.maximum((block * rows // KROWS - 1) * KROWS, 0)
        near_ok = (lane < rows) & (position <= token) & (position >= oldest)

        def columns_of(head):
            return pl.ds(pl.multiple_of(head * head_size, LANES), head_size)

        def scores(head):
            count = lists[head, group, COUNTS_AT + block]
            q = jnp.concatenate([q_ref[group, :, columns_of(head)] for q_ref in q_refs], axis=0)
            s = jnp.where(near_ok, nt(q, near_k), -jnp.inf)
            s_scr[head, KQ] = s
            high = s
            for slot in range(0, KQ, SLOTS_AT_ONCE):
                keys = [k_ref[lists[head, group, slot + i]] for i in range(SLOTS_AT_ONCE)]
                several = nt(q, jnp.concatenate(keys, axis=0))
                for i in range(SLOTS_AT_ONCE):
                    s = several[:, i * KROWS : (i + 1) * KROWS]
                    s = jnp.where(slot + i < count, s, -jnp.inf)
                    s_scr[head, slot + i] = s
                    high = jnp.maximum(high, s)
            m_scr[head] = high

        def sums(head):
            top = m_scr[head]
            total = jnp.exp2(s_scr[head, KQ] * scale - top)
            acc = jnp.dot(total.astype(jnp.bfloat16), near_v, preferred_element_type=jnp.float32)
            for slot in range(0, KQ, SLOTS_AT_ONCE):
                weights = []
                for part in range(slot, slot + SLOTS_AT_ONCE):
                    p = jnp.exp2(s_scr[head, part] * scale - top)
                    total = total + p
                    weights.append(p.astype(jnp.bfloat16))
                values = [v_ref[lists[head, group, slot + i]] for i in range(SLOTS_AT_ONCE)]
                acc = acc + jnp.dot(
                    jnp.concatenate(weights, axis=1),
                    jnp.concatenate(values, axis=0),
                    preferred_element_type=jnp.float32,
                )
            acc = acc.astype(jnp.bfloat16)
            for part, out_ref in enumerate(out_refs):
                out_ref[group, :, columns_of(head)] = acc[
                    part * local_rows : (part + 1) * local_rows
                ]
            l_scr[head] = total

        def in_steps(step):
            def several(turn, carry):
                for i in range(AT_ONCE):
                    step(turn * AT_ONCE + i)
                return carry

            lax.fori_loop(0, HEADS_PER_GROUP // AT_ONCE, several, 0)

        in_steps(scores)
        for head in range(HEADS_PER_GROUP):
            top = jnp.max(m_scr[head], axis=1, keepdims=True) * scale
            m_scr[head] = jnp.broadcast_to(top, (rows, LANES))
        for v_copy in v_copies:
            if groups == 1:
                v_copy.wait()
            else:
                pl.when(group == 0)(v_copy.wait)
        in_steps(sums)
        stats = jnp.zeros((rows, LANES), jnp.float32)
        for head in range(HEADS_PER_GROUP):
            total = jnp.sum(l_scr[head], axis=1, keepdims=True)
            stats = jnp.where(lane == head, m_scr[head], stats)
            stats = jnp.where(lane == head + HEADS_PER_GROUP, total, stats)
        packed = jnp.zeros((rows, LANES), jnp.float32)
        for step in range(3):
            part = stats.astype(jnp.bfloat16).astype(jnp.float32)
            stats = stats - part
            by = step * 2 * HEADS_PER_GROUP
            packed = packed + (pltpu.roll(part, by, 1) if by else part)
        packed = packed.astype(jnp.bfloat16)
        width = HEADS_PER_GROUP * head_size
        for part, out_ref in enumerate(out_refs):
            out_ref[group, :, width:] = packed[part * local_rows : (part + 1) * local_rows]

    if groups == 1:
        one_block(0)
    else:
        pl.loop(0, groups)(one_block)


def merge_kernel(*refs):
    in_refs, out_ref = refs[:-1], refs[-1]
    groups, local_rows, full = in_refs[0].shape
    width = full - LANES
    head_size = width // HEADS_PER_GROUP

    def one_block(group):
        stats = []
        for in_ref in in_refs:
            packed = in_ref[group, :, width:].astype(jnp.float32)
            one = packed
            for step in (1, 2):
                one = one + pltpu.roll(packed, LANES - step * 2 * HEADS_PER_GROUP, 1)
            stats.append(one)
        top = stats[0]
        for one in stats[1:]:
            top = jnp.maximum(top, one)
        factors = [jnp.exp2(one - top) for one in stats]
        total = jnp.zeros((local_rows, LANES), jnp.float32)
        for one, factor in zip(stats, factors):
            total = total + pltpu.roll(one, LANES - HEADS_PER_GROUP, 1) * factor
        inverse = 1.0 / total
        factors = [factor * inverse for factor in factors]
        for head in range(HEADS_PER_GROUP):
            columns = slice(head * head_size, (head + 1) * head_size)
            mixed = jnp.zeros((local_rows, head_size), jnp.float32)
            for in_ref, factor in zip(in_refs, factors):
                mixed = mixed + in_ref[group, :, columns].astype(jnp.float32) * (
                    factor[:, head : head + 1]
                )
            out_ref[group, :, columns] = mixed.astype(jnp.bfloat16)

    if groups == 1:
        one_block(0)
    else:
        pl.loop(0, groups)(one_block)


def from_quarter(value, mask):
    return lax.ppermute(value, "ctx", [(device, device ^ mask) for device in range(CTX)])


def body(
    queries, new_token_keys, new_token_values, cache_keys, cache_values, block_ids, block_counts
):
    seq_count = lax.axis_size("seq")
    head_size = cache_keys.shape[2]
    local_rows = queries.shape[0]
    blocks = block_ids.shape[1]
    groups = seq_count // HEADS_PER_GROUP
    width = HEADS_PER_GROUP * head_size
    assert lax.axis_size("ctx") == CTX and cache_keys.shape[0] == 1
    assert local_rows * CTX == TILE_QUERY_ROWS and blocks <= LANES - COUNTS_AT
    assert head_size == LANES and local_rows & (local_rows - 1) == 0
    same_group = same_member = None
    if groups > 1:
        same_group = [
            [g * HEADS_PER_GROUP + r for r in range(HEADS_PER_GROUP)] for g in range(groups)
        ]
        same_member = [
            [g * HEADS_PER_GROUP + r for g in range(groups)] for r in range(HEADS_PER_GROUP)
        ]

    def over_seq(pieces, members):
        return lax.all_to_all(
            pieces, "seq", split_axis=0, concat_axis=0, tiled=True, axis_index_groups=members
        )

    def in_hbm(value):
        return pltpu.with_memory_space_constraint(value, pltpu.HBM)

    def to_groups(rows):
        pieces = rows.reshape(local_rows, groups, -1).transpose(1, 0, 2)
        return pieces if groups == 1 else over_seq(pieces, same_member)

    vmem = pl.BlockSpec(memory_space=pltpu.VMEM)
    hbm = pl.BlockSpec(memory_space=pltpu.HBM)
    smem = pl.BlockSpec(memory_space=pltpu.SMEM)
    queries = to_groups(queries)
    others = [from_quarter(queries, mask) for mask in range(1, CTX)]
    small = (
        to_groups(new_token_keys),
        to_groups(new_token_values),
        block_ids,
        block_counts.reshape(1, blocks),
    )
    packed = pl.pallas_call(
        pack_kernel,
        out_shape=jax.ShapeDtypeStruct(
            (HEADS_PER_GROUP, groups, 2 * local_rows + LIST_ROWS, LANES), jnp.bfloat16
        ),
        in_specs=[hbm] * 4,
        out_specs=vmem,
        scratch_shapes=[pltpu.VMEM(one.shape, one.dtype) for one in small]
        + [
            pltpu.VMEM((HEADS_PER_GROUP * groups, LIST_ROWS, LANES), jnp.float32),
            pltpu.SemaphoreType.DMA((4,)),
        ],
        compiler_params=pltpu.CompilerParams(vmem_limit_bytes=4 * MIB),
        cost_estimate=pl.CostEstimate(flops=0, bytes_accessed=12 * MIB, transcendentals=0),
        name="pack",
    )(*[in_hbm(one) for one in small])
    values = cache_values.reshape(-1, KROWS, head_size)
    early = values.shape[0] * 3 // 8
    large = (queries, cache_keys.reshape(-1, KROWS, head_size), values)
    queries, keys, early_values = pl.pallas_call(
        fetch_kernel,
        out_shape=[jax.ShapeDtypeStruct(one.shape, one.dtype) for one in large[:2]]
        + [jax.ShapeDtypeStruct((early,) + values.shape[1:], values.dtype)],
        in_specs=[hbm] * 3,
        out_specs=[vmem] * 3,
        scratch_shapes=[pltpu.SemaphoreType.DMA((3,))],
        compiler_params=pltpu.CompilerParams(vmem_limit_bytes=4 * MIB),
        cost_estimate=pl.CostEstimate(flops=0, bytes_accessed=4 * MIB, transcendentals=0),
        name="fetch",
    )(*[in_hbm(one) for one in large])
    near = over_seq(packed, same_group)
    lists = near[:, :, 2 * local_rows].astype(jnp.int32)
    tile = (TILE_QUERY_ROWS, KROWS)
    partial = pl.pallas_call(
        attend_kernel,
        out_shape=[
            jax.ShapeDtypeStruct((groups, local_rows, width + LANES), jnp.bfloat16)
        ] * CTX,
        in_specs=[smem, vmem, vmem, hbm] + [vmem] * (1 + CTX),
        out_specs=[vmem] * CTX,
        scratch_shapes=[
            pltpu.VMEM((HEADS_PER_GROUP, KQ + 1) + tile, jnp.float32),
            pltpu.VMEM((HEADS_PER_GROUP,) + tile, jnp.float32),
            pltpu.VMEM((HEADS_PER_GROUP,) + tile, jnp.float32),
            pltpu.VMEM(values.shape, values.dtype),
            pltpu.SemaphoreType.DMA((2,)),
        ],
        compiler_params=pltpu.CompilerParams(vmem_limit_bytes=24 * MIB),
        name="attend",
    )(lists, near, keys, in_hbm(values), early_values, queries, *others)
    partial = [from_quarter(partial[mask], mask) for mask in (2, 3, 1)] + [partial[0]]
    merged = pl.pallas_call(
        merge_kernel,
        out_shape=jax.ShapeDtypeStruct((groups, local_rows, width), jnp.bfloat16),
        in_specs=[vmem] * CTX,
        out_specs=vmem,
        compiler_params=pltpu.CompilerParams(vmem_limit_bytes=4 * MIB),
        name="merge",
    )(*partial)
    if groups > 1:
        merged = over_seq(merged, same_member)
    return merged.transpose(1, 0, 2).reshape(local_rows, groups * width)


def solution(mesh):
    return jax.shard_map(
        body,
        mesh=mesh,
        in_specs=(
            P(("seq", "ctx"), None),
            P(("seq", "ctx"), None),
            P(("seq", "ctx"), None),
            P("seq", "ctx", None),
            P("seq", "ctx", None),
            P("seq", None, "ctx", None),
            P("seq", None, "ctx"),
        ),
        out_specs=P(("seq", "ctx"), None),
        check_vma=False,
    )
```

```python
import math

import jax
import jax.numpy as jnp
from jax import lax
from jax.experimental import pallas as pl
from jax.experimental.pallas import tpu as pltpu
from jax.sharding import PartitionSpec as P

HEADS_PER_GROUP = 8
TILE_QUERY_ROWS = 64
KROWS = 128
KQ = 12
LANES = 128
CTX = 4
NEAR = 2 * KROWS // TILE_QUERY_ROWS
AT_ONCE = 4
SLOTS_AT_ONCE = 12
LIST_ROWS = 8
COUNTS_AT = 16
MIB = 1024 * 1024
LOG2E = 1.4426950408889634


def nt(a, b):
    return lax.dot_general(a, b, (((1,), (1,)), ((), ())), preferred_element_type=jnp.float32)


def pack_kernel(*refs):
    sources, out_ref, targets = refs[:4], refs[4], refs[5:9]
    scratch, sems = refs[9:]
    copies = [
        pltpu.make_async_copy(source, target, sems.at[i])
        for i, (source, target) in enumerate(zip(sources, targets))
    ]
    for copy in copies:
        copy.start()
    keys, values, ids, counts = targets
    members, groups, _, _ = out_ref.shape
    local_rows = keys.shape[1]
    blocks = ids.shape[1]
    scratch[...] = jnp.zeros_like(scratch)
    for copy in copies:
        copy.wait()
    scratch[0:1, COUNTS_AT : COUNTS_AT + blocks] = counts[...].astype(jnp.float32)
    for member in range(members):
        for group in range(groups):
            block = group * members + member
            scratch[0:1, :KQ] = ids[0, block].astype(jnp.float32)
            out_ref[member, group, :local_rows] = keys[group]
            out_ref[member, group, local_rows : 2 * local_rows] = values[group]
            out_ref[member, group, 2 * local_rows :] = scratch[...].astype(jnp.bfloat16)


def fetch_kernel(*refs):
    count = len(refs) // 2
    copies = [
        pltpu.make_async_copy(refs[i], refs[count + i], refs[-1].at[i]) for i in range(count)
    ]
    for copy in copies:
        copy.start()
    for copy in copies:
        copy.wait()


def attend_kernel(lists, near_ref, k_ref, v_hbm, *refs):
    q_refs, out_refs = refs[:CTX], refs[CTX : 2 * CTX]
    s_scr, m_scr, l_scr, v_ref, sem = refs[2 * CTX :]
    v_copy = pltpu.make_async_copy(v_hbm, v_ref, sem)
    v_copy.start()
    groups, local_rows, _ = q_refs[0].shape
    member = lax.rem(lax.axis_index("seq"), HEADS_PER_GROUP)
    quarter = lax.axis_index("ctx")
    rows = TILE_QUERY_ROWS
    head_size = k_ref.shape[2]
    scale = LOG2E / math.sqrt(head_size)
    shift, mask = local_rows.bit_length() - 1, local_rows - 1
    lane = lax.broadcasted_iota(jnp.int32, (rows, LANES), 1)
    sublane = lax.broadcasted_iota(jnp.int32, (rows, LANES), 0)

    def one_block(group):
        block = group * HEADS_PER_GROUP + member
        near = []
        for back in range(NEAR):
            place = jnp.maximum(group - jnp.where(member < back, 1, 0), 0)
            near.append(near_ref[lax.rem(member - back + HEADS_PER_GROUP, HEADS_PER_GROUP), place])
        near_k = jnp.concatenate([one[:local_rows] for one in near] * 2, axis=0)
        near_v = jnp.concatenate([one[local_rows : 2 * local_rows] for one in near] * 2, axis=0)
        position = (block - (lane >> shift)) * rows + quarter * local_rows + (lane & mask)
        token = block * rows + ((sublane >> shift) ^ quarter) * local_rows + (sublane & mask)
        oldest = jnp.maximum((block * rows // KROWS - 1) * KROWS, 0)
        near_ok = (lane < rows) & (position <= token) & (position >= oldest)

        def columns_of(head):
            return pl.ds(pl.multiple_of(head * head_size, LANES), head_size)

        def scores(head):
            count = lists[head, group, COUNTS_AT + block]
            q = jnp.concatenate([q_ref[group, :, columns_of(head)] for q_ref in q_refs], axis=0)
            s = jnp.where(near_ok, nt(q, near_k), -jnp.inf)
            s_scr[head, KQ] = s
            high = s
            for slot in range(0, KQ, SLOTS_AT_ONCE):
                keys = [k_ref[lists[head, group, slot + i]] for i in range(SLOTS_AT_ONCE)]
                several = nt(q, jnp.concatenate(keys, axis=0))
                for i in range(SLOTS_AT_ONCE):
                    s = several[:, i * KROWS : (i + 1) * KROWS]
                    s = jnp.where(slot + i < count, s, -jnp.inf)
                    s_scr[head, slot + i] = s
                    high = jnp.maximum(high, s)
            m_scr[head] = high

        def sums(head):
            top = m_scr[head]
            total = jnp.exp2(s_scr[head, KQ] * scale - top)
            acc = jnp.dot(total.astype(jnp.bfloat16), near_v, preferred_element_type=jnp.float32)
            for slot in range(0, KQ, SLOTS_AT_ONCE):
                weights = []
                for part in range(slot, slot + SLOTS_AT_ONCE):
                    p = jnp.exp2(s_scr[head, part] * scale - top)
                    total = total + p
                    weights.append(p.astype(jnp.bfloat16))
                values = [v_ref[lists[head, group, slot + i]] for i in range(SLOTS_AT_ONCE)]
                acc = acc + jnp.dot(
                    jnp.concatenate(weights, axis=1),
                    jnp.concatenate(values, axis=0),
                    preferred_element_type=jnp.float32,
                )
            acc = acc.astype(jnp.bfloat16)
            for part, out_ref in enumerate(out_refs):
                out_ref[group, :, columns_of(head)] = acc[
                    part * local_rows : (part + 1) * local_rows
                ]
            l_scr[head] = total

        def in_steps(step):
            def several(turn, carry):
                for i in range(AT_ONCE):
                    step(turn * AT_ONCE + i)
                return carry

            lax.fori_loop(0, HEADS_PER_GROUP // AT_ONCE, several, 0)

        in_steps(scores)
        for head in range(HEADS_PER_GROUP):
            top = jnp.max(m_scr[head], axis=1, keepdims=True) * scale
            m_scr[head] = jnp.broadcast_to(top, (rows, LANES))
        if groups == 1:
            v_copy.wait()
        else:
            pl.when(group == 0)(v_copy.wait)
        in_steps(sums)
        stats = jnp.zeros((rows, LANES), jnp.float32)
        for head in range(HEADS_PER_GROUP):
            total = jnp.sum(l_scr[head], axis=1, keepdims=True)
            stats = jnp.where(lane == head, m_scr[head], stats)
            stats = jnp.where(lane == head + HEADS_PER_GROUP, total, stats)
        packed = jnp.zeros((rows, LANES), jnp.float32)
        for step in range(3):
            part = stats.astype(jnp.bfloat16).astype(jnp.float32)
            stats = stats - part
            by = step * 2 * HEADS_PER_GROUP
            packed = packed + (pltpu.roll(part, by, 1) if by else part)
        packed = packed.astype(jnp.bfloat16)
        width = HEADS_PER_GROUP * head_size
        for part, out_ref in enumerate(out_refs):
            out_ref[group, :, width:] = packed[part * local_rows : (part + 1) * local_rows]

    if groups == 1:
        one_block(0)
    else:
        pl.loop(0, groups)(one_block)


def merge_kernel(*refs):
    in_refs, out_ref = refs[:-1], refs[-1]
    groups, local_rows, full = in_refs[0].shape
    width = full - LANES
    head_size = width // HEADS_PER_GROUP

    def one_block(group):
        stats = []
        for in_ref in in_refs:
            packed = in_ref[group, :, width:].astype(jnp.float32)
            one = packed
            for step in (1, 2):
                one = one + pltpu.roll(packed, LANES - step * 2 * HEADS_PER_GROUP, 1)
            stats.append(one)
        top = stats[0]
        for one in stats[1:]:
            top = jnp.maximum(top, one)
        factors = [jnp.exp2(one - top) for one in stats]
        total = jnp.zeros((local_rows, LANES), jnp.float32)
        for one, factor in zip(stats, factors):
            total = total + pltpu.roll(one, LANES - HEADS_PER_GROUP, 1) * factor
        inverse = 1.0 / total
        factors = [factor * inverse for factor in factors]
        for head in range(HEADS_PER_GROUP):
            columns = slice(head * head_size, (head + 1) * head_size)
            mixed = jnp.zeros((local_rows, head_size), jnp.float32)
            for in_ref, factor in zip(in_refs, factors):
                mixed = mixed + in_ref[group, :, columns].astype(jnp.float32) * (
                    factor[:, head : head + 1]
                )
            out_ref[group, :, columns] = mixed.astype(jnp.bfloat16)

    if groups == 1:
        one_block(0)
    else:
        pl.loop(0, groups)(one_block)


def from_quarter(value, mask):
    return lax.ppermute(value, "ctx", [(device, device ^ mask) for device in range(CTX)])


def body(
    queries, new_token_keys, new_token_values, cache_keys, cache_values, block_ids, block_counts
):
    seq_count = lax.axis_size("seq")
    head_size = cache_keys.shape[2]
    local_rows = queries.shape[0]
    blocks = block_ids.shape[1]
    groups = seq_count // HEADS_PER_GROUP
    width = HEADS_PER_GROUP * head_size
    assert lax.axis_size("ctx") == CTX and cache_keys.shape[0] == 1
    assert local_rows * CTX == TILE_QUERY_ROWS and blocks <= LANES - COUNTS_AT
    assert head_size == LANES and local_rows & (local_rows - 1) == 0
    same_group = same_member = None
    if groups > 1:
        same_group = [
            [g * HEADS_PER_GROUP + r for r in range(HEADS_PER_GROUP)] for g in range(groups)
        ]
        same_member = [
            [g * HEADS_PER_GROUP + r for g in range(groups)] for r in range(HEADS_PER_GROUP)
        ]

    def over_seq(pieces, members):
        return lax.all_to_all(
            pieces, "seq", split_axis=0, concat_axis=0, tiled=True, axis_index_groups=members
        )

    def in_hbm(value):
        return pltpu.with_memory_space_constraint(value, pltpu.HBM)

    def to_groups(rows):
        pieces = rows.reshape(local_rows, groups, -1).transpose(1, 0, 2)
        return pieces if groups == 1 else over_seq(pieces, same_member)

    vmem = pl.BlockSpec(memory_space=pltpu.VMEM)
    hbm = pl.BlockSpec(memory_space=pltpu.HBM)
    smem = pl.BlockSpec(memory_space=pltpu.SMEM)
    queries = to_groups(queries)
    others = [from_quarter(queries, mask) for mask in range(1, CTX)]
    small = (
        to_groups(new_token_keys),
        to_groups(new_token_values),
        block_ids,
        block_counts.reshape(1, blocks),
    )
    packed = pl.pallas_call(
        pack_kernel,
        out_shape=jax.ShapeDtypeStruct(
            (HEADS_PER_GROUP, groups, 2 * local_rows + LIST_ROWS, LANES), jnp.bfloat16
        ),
        in_specs=[hbm] * 4,
        out_specs=vmem,
        scratch_shapes=[pltpu.VMEM(one.shape, one.dtype) for one in small]
        + [pltpu.VMEM((LIST_ROWS, LANES), jnp.float32), pltpu.SemaphoreType.DMA((4,))],
        compiler_params=pltpu.CompilerParams(vmem_limit_bytes=4 * MIB),
        cost_estimate=pl.CostEstimate(flops=0, bytes_accessed=12 * MIB, transcendentals=0),
        name="pack",
    )(*[in_hbm(one) for one in small])
    large = (queries, cache_keys.reshape(-1, KROWS, head_size))
    queries, keys = pl.pallas_call(
        fetch_kernel,
        out_shape=[jax.ShapeDtypeStruct(one.shape, one.dtype) for one in large],
        in_specs=[hbm] * 2,
        out_specs=[vmem] * 2,
        scratch_shapes=[pltpu.SemaphoreType.DMA((2,))],
        compiler_params=pltpu.CompilerParams(vmem_limit_bytes=4 * MIB),
        cost_estimate=pl.CostEstimate(flops=0, bytes_accessed=4 * MIB, transcendentals=0),
        name="fetch",
    )(*[in_hbm(one) for one in large])
    near = over_seq(packed, same_group)
    lists = near[:, :, 2 * local_rows].astype(jnp.int32)
    tile = (TILE_QUERY_ROWS, KROWS)
    values = cache_values.reshape(-1, KROWS, head_size)
    partial = pl.pallas_call(
        attend_kernel,
        out_shape=[
            jax.ShapeDtypeStruct((groups, local_rows, width + LANES), jnp.bfloat16)
        ] * CTX,
        in_specs=[smem, vmem, vmem, hbm] + [vmem] * CTX,
        out_specs=[vmem] * CTX,
        scratch_shapes=[
            pltpu.VMEM((HEADS_PER_GROUP, KQ + 1) + tile, jnp.float32),
            pltpu.VMEM((HEADS_PER_GROUP,) + tile, jnp.float32),
            pltpu.VMEM((HEADS_PER_GROUP,) + tile, jnp.float32),
            pltpu.VMEM(values.shape, values.dtype),
            pltpu.SemaphoreType.DMA,
        ],
        compiler_params=pltpu.CompilerParams(vmem_limit_bytes=24 * MIB),
        name="attend",
    )(lists, near, keys, in_hbm(values), queries, *others)
    partial = [from_quarter(partial[mask], mask) for mask in (2, 3, 1)] + [partial[0]]
    merged = pl.pallas_call(
        merge_kernel,
        out_shape=jax.ShapeDtypeStruct((groups, local_rows, width), jnp.bfloat16),
        in_specs=[vmem] * CTX,
        out_specs=vmem,
        compiler_params=pltpu.CompilerParams(vmem_limit_bytes=4 * MIB),
        name="merge",
    )(*partial)
    if groups > 1:
        merged = over_seq(merged, same_member)
    return merged.transpose(1, 0, 2).reshape(local_rows, groups * width)


def solution(mesh):
    return jax.shard_map(
        body,
        mesh=mesh,
        in_specs=(
            P(("seq", "ctx"), None),
            P(("seq", "ctx"), None),
            P(("seq", "ctx"), None),
            P("seq", "ctx", None),
            P("seq", "ctx", None),
            P("seq", None, "ctx", None),
            P("seq", None, "ctx"),
        ),
        out_specs=P(("seq", "ctx"), None),
        check_vma=False,
    )
```

```python
import math

import jax
import jax.numpy as jnp
from jax import lax
from jax.experimental import pallas as pl
from jax.experimental.pallas import tpu as pltpu
from jax.sharding import PartitionSpec as P

HEADS_PER_GROUP = 8
TILE_QUERY_ROWS = 64
KROWS = 128
KQ = 12
LANES = 128
CTX = 4
NEAR = 2 * KROWS // TILE_QUERY_ROWS
AT_ONCE = 4
SLOTS_AT_ONCE = 4
LIST_ROWS = 8
COUNTS_AT = 16
MIB = 1024 * 1024
LOG2E = 1.4426950408889634


def nt(a, b):
    return lax.dot_general(a, b, (((1,), (1,)), ((), ())), preferred_element_type=jnp.float32)


def pack_kernel(*refs):
    sources, out_ref, targets = refs[:4], refs[4], refs[5:9]
    scratch, sems = refs[9:]
    copies = [
        pltpu.make_async_copy(source, target, sems.at[i])
        for i, (source, target) in enumerate(zip(sources, targets))
    ]
    for copy in copies:
        copy.start()
    keys, values, ids, counts = targets
    members, groups, _, _ = out_ref.shape
    local_rows = keys.shape[1]
    blocks = ids.shape[1]
    scratch[...] = jnp.zeros_like(scratch)
    for copy in copies:
        copy.wait()
    scratch[0:1, COUNTS_AT : COUNTS_AT + blocks] = counts[...].astype(jnp.float32)
    for member in range(members):
        for group in range(groups):
            block = group * members + member
            scratch[0:1, :KQ] = ids[0, block].astype(jnp.float32)
            out_ref[place_of(member), group, :local_rows] = keys[group]
            out_ref[place_of(member), group, local_rows : 2 * local_rows] = values[group]
            out_ref[place_of(member), group, 2 * local_rows :] = scratch[...].astype(jnp.bfloat16)


def place_of(member):
    return HEADS_PER_GROUP - 1 - member


def fetch_kernel(*refs):
    count = len(refs) // 2
    copies = [
        pltpu.make_async_copy(refs[i], refs[count + i], refs[-1].at[i]) for i in range(count)
    ]
    for copy in copies:
        copy.start()
    for copy in copies:
        copy.wait()


def attend_kernel(lists, near_ref, k_ref, v_hbm, *refs):
    q_refs, out_refs = refs[:CTX], refs[CTX : 2 * CTX]
    s_scr, m_scr, l_scr, v_ref, sem = refs[2 * CTX :]
    v_copy = pltpu.make_async_copy(v_hbm, v_ref, sem)
    v_copy.start()
    groups, local_rows, _ = q_refs[0].shape
    member = lax.rem(lax.axis_index("seq"), HEADS_PER_GROUP)
    quarter = lax.axis_index("ctx")
    rows = TILE_QUERY_ROWS
    head_size = k_ref.shape[2]
    scale = LOG2E / math.sqrt(head_size)
    shift, mask = local_rows.bit_length() - 1, local_rows - 1
    lane = lax.broadcasted_iota(jnp.int32, (rows, LANES), 1)
    sublane = lax.broadcasted_iota(jnp.int32, (rows, LANES), 0)

    def one_block(group):
        block = group * HEADS_PER_GROUP + member
        near = []
        for back in range(NEAR):
            place = jnp.maximum(group - jnp.where(member < back, 1, 0), 0)
            near.append(near_ref[place_of(lax.rem(member - back + HEADS_PER_GROUP, HEADS_PER_GROUP)), place])
        near_k = jnp.concatenate([one[:local_rows] for one in near] * 2, axis=0)
        near_v = jnp.concatenate([one[local_rows : 2 * local_rows] for one in near] * 2, axis=0)
        position = (block - (lane >> shift)) * rows + quarter * local_rows + (lane & mask)
        token = block * rows + ((sublane >> shift) ^ quarter) * local_rows + (sublane & mask)
        oldest = jnp.maximum((block * rows // KROWS - 1) * KROWS, 0)
        near_ok = (lane < rows) & (position <= token) & (position >= oldest)

        def columns_of(head):
            return pl.ds(pl.multiple_of(head * head_size, LANES), head_size)

        def scores(head):
            count = lists[place_of(head), group, COUNTS_AT + block]
            q = jnp.concatenate([q_ref[group, :, columns_of(head)] for q_ref in q_refs], axis=0)
            s = jnp.where(near_ok, nt(q, near_k), -jnp.inf)
            s_scr[head, KQ] = s
            high = s
            for slot in range(0, KQ, SLOTS_AT_ONCE):
                keys = [k_ref[lists[place_of(head), group, slot + i]] for i in range(SLOTS_AT_ONCE)]
                several = nt(q, jnp.concatenate(keys, axis=0))
                for i in range(SLOTS_AT_ONCE):
                    s = several[:, i * KROWS : (i + 1) * KROWS]
                    s = jnp.where(slot + i < count, s, -jnp.inf)
                    s_scr[head, slot + i] = s
                    high = jnp.maximum(high, s)
            m_scr[head] = high

        def sums(head):
            top = m_scr[head]
            total = jnp.exp2(s_scr[head, KQ] * scale - top)
            acc = jnp.dot(total.astype(jnp.bfloat16), near_v, preferred_element_type=jnp.float32)
            for slot in range(0, KQ, SLOTS_AT_ONCE):
                weights = []
                for part in range(slot, slot + SLOTS_AT_ONCE):
                    p = jnp.exp2(s_scr[head, part] * scale - top)
                    total = total + p
                    weights.append(p.astype(jnp.bfloat16))
                values = [v_ref[lists[place_of(head), group, slot + i]] for i in range(SLOTS_AT_ONCE)]
                acc = acc + jnp.dot(
                    jnp.concatenate(weights, axis=1),
                    jnp.concatenate(values, axis=0),
                    preferred_element_type=jnp.float32,
                )
            acc = acc.astype(jnp.bfloat16)
            for part, out_ref in enumerate(out_refs):
                out_ref[group, :, columns_of(head)] = acc[
                    part * local_rows : (part + 1) * local_rows
                ]
            l_scr[head] = total

        def in_steps(step):
            def several(turn, carry):
                for i in range(AT_ONCE):
                    step(turn * AT_ONCE + i)
                return carry

            lax.fori_loop(0, HEADS_PER_GROUP // AT_ONCE, several, 0)

        in_steps(scores)
        for head in range(HEADS_PER_GROUP):
            top = jnp.max(m_scr[head], axis=1, keepdims=True) * scale
            m_scr[head] = jnp.broadcast_to(top, (rows, LANES))
        if groups == 1:
            v_copy.wait()
        else:
            pl.when(group == 0)(v_copy.wait)
        in_steps(sums)
        stats = jnp.zeros((rows, LANES), jnp.float32)
        for head in range(HEADS_PER_GROUP):
            total = jnp.sum(l_scr[head], axis=1, keepdims=True)
            stats = jnp.where(lane == head, m_scr[head], stats)
            stats = jnp.where(lane == head + HEADS_PER_GROUP, total, stats)
        packed = jnp.zeros((rows, LANES), jnp.float32)
        for step in range(3):
            part = stats.astype(jnp.bfloat16).astype(jnp.float32)
            stats = stats - part
            by = step * 2 * HEADS_PER_GROUP
            packed = packed + (pltpu.roll(part, by, 1) if by else part)
        packed = packed.astype(jnp.bfloat16)
        width = HEADS_PER_GROUP * head_size
        for part, out_ref in enumerate(out_refs):
            out_ref[group, :, width:] = packed[part * local_rows : (part + 1) * local_rows]

    if groups == 1:
        one_block(0)
    else:
        pl.loop(0, groups)(one_block)


def merge_kernel(*refs):
    in_refs, out_ref = refs[:-1], refs[-1]
    groups, local_rows, full = in_refs[0].shape
    width = full - LANES
    head_size = width // HEADS_PER_GROUP

    def one_block(group):
        stats = []
        for in_ref in in_refs:
            packed = in_ref[group, :, width:].astype(jnp.float32)
            one = packed
            for step in (1, 2):
                one = one + pltpu.roll(packed, LANES - step * 2 * HEADS_PER_GROUP, 1)
            stats.append(one)
        top = stats[0]
        for one in stats[1:]:
            top = jnp.maximum(top, one)
        factors = [jnp.exp2(one - top) for one in stats]
        total = jnp.zeros((local_rows, LANES), jnp.float32)
        for one, factor in zip(stats, factors):
            total = total + pltpu.roll(one, LANES - HEADS_PER_GROUP, 1) * factor
        inverse = 1.0 / total
        factors = [factor * inverse for factor in factors]
        for head in range(HEADS_PER_GROUP):
            columns = slice(head * head_size, (head + 1) * head_size)
            mixed = jnp.zeros((local_rows, head_size), jnp.float32)
            for in_ref, factor in zip(in_refs, factors):
                mixed = mixed + in_ref[group, :, columns].astype(jnp.float32) * (
                    factor[:, head : head + 1]
                )
            out_ref[group, :, columns] = mixed.astype(jnp.bfloat16)

    if groups == 1:
        one_block(0)
    else:
        pl.loop(0, groups)(one_block)


def from_quarter(value, mask):
    return lax.ppermute(value, "ctx", [(device, device ^ mask) for device in range(CTX)])


def body(
    queries, new_token_keys, new_token_values, cache_keys, cache_values, block_ids, block_counts
):
    seq_count = lax.axis_size("seq")
    head_size = cache_keys.shape[2]
    local_rows = queries.shape[0]
    blocks = block_ids.shape[1]
    groups = seq_count // HEADS_PER_GROUP
    width = HEADS_PER_GROUP * head_size
    assert lax.axis_size("ctx") == CTX and cache_keys.shape[0] == 1
    assert local_rows * CTX == TILE_QUERY_ROWS and blocks <= LANES - COUNTS_AT
    assert head_size == LANES and local_rows & (local_rows - 1) == 0
    same_group = [
        [g * HEADS_PER_GROUP + place_of(place) for place in range(HEADS_PER_GROUP)]
        for g in range(groups)
    ]
    if groups > 1:
        same_member = [
            [g * HEADS_PER_GROUP + r for g in range(groups)] for r in range(HEADS_PER_GROUP)
        ]

    def over_seq(pieces, members):
        return lax.all_to_all(
            pieces, "seq", split_axis=0, concat_axis=0, tiled=True, axis_index_groups=members
        )

    def in_hbm(value):
        return pltpu.with_memory_space_constraint(value, pltpu.HBM)

    def to_groups(rows):
        pieces = rows.reshape(local_rows, groups, -1).transpose(1, 0, 2)
        return pieces if groups == 1 else over_seq(pieces, same_member)

    vmem = pl.BlockSpec(memory_space=pltpu.VMEM)
    hbm = pl.BlockSpec(memory_space=pltpu.HBM)
    smem = pl.BlockSpec(memory_space=pltpu.SMEM)
    queries = to_groups(queries)
    others = [from_quarter(queries, mask) for mask in range(1, CTX)]
    small = (
        to_groups(new_token_keys),
        to_groups(new_token_values),
        block_ids,
        block_counts.reshape(1, blocks),
    )
    packed = pl.pallas_call(
        pack_kernel,
        out_shape=jax.ShapeDtypeStruct(
            (HEADS_PER_GROUP, groups, 2 * local_rows + LIST_ROWS, LANES), jnp.bfloat16
        ),
        in_specs=[hbm] * 4,
        out_specs=vmem,
        scratch_shapes=[pltpu.VMEM(one.shape, one.dtype) for one in small]
        + [pltpu.VMEM((LIST_ROWS, LANES), jnp.float32), pltpu.SemaphoreType.DMA((4,))],
        compiler_params=pltpu.CompilerParams(vmem_limit_bytes=4 * MIB),
        cost_estimate=pl.CostEstimate(flops=0, bytes_accessed=12 * MIB, transcendentals=0),
        name="pack",
    )(*[in_hbm(one) for one in small])
    large = (queries, cache_keys.reshape(-1, KROWS, head_size))
    queries, keys = pl.pallas_call(
        fetch_kernel,
        out_shape=[jax.ShapeDtypeStruct(one.shape, one.dtype) for one in large],
        in_specs=[hbm] * 2,
        out_specs=[vmem] * 2,
        scratch_shapes=[pltpu.SemaphoreType.DMA((2,))],
        compiler_params=pltpu.CompilerParams(vmem_limit_bytes=4 * MIB),
        cost_estimate=pl.CostEstimate(flops=0, bytes_accessed=4 * MIB, transcendentals=0),
        name="fetch",
    )(*[in_hbm(one) for one in large])
    near = over_seq(packed, same_group)
    lists = near[:, :, 2 * local_rows].astype(jnp.int32)
    tile = (TILE_QUERY_ROWS, KROWS)
    values = cache_values.reshape(-1, KROWS, head_size)
    partial = pl.pallas_call(
        attend_kernel,
        out_shape=[
            jax.ShapeDtypeStruct((groups, local_rows, width + LANES), jnp.bfloat16)
        ] * CTX,
        in_specs=[smem, vmem, vmem, hbm] + [vmem] * CTX,
        out_specs=[vmem] * CTX,
        scratch_shapes=[
            pltpu.VMEM((HEADS_PER_GROUP, KQ + 1) + tile, jnp.float32),
            pltpu.VMEM((HEADS_PER_GROUP,) + tile, jnp.float32),
            pltpu.VMEM((HEADS_PER_GROUP,) + tile, jnp.float32),
            pltpu.VMEM(values.shape, values.dtype),
            pltpu.SemaphoreType.DMA,
        ],
        compiler_params=pltpu.CompilerParams(vmem_limit_bytes=24 * MIB),
        name="attend",
    )(lists, near, keys, in_hbm(values), queries, *others)
    partial = [from_quarter(partial[mask], mask) for mask in (2, 3, 1)] + [partial[0]]
    merged = pl.pallas_call(
        merge_kernel,
        out_shape=jax.ShapeDtypeStruct((groups, local_rows, width), jnp.bfloat16),
        in_specs=[vmem] * CTX,
        out_specs=vmem,
        compiler_params=pltpu.CompilerParams(vmem_limit_bytes=4 * MIB),
        name="merge",
    )(*partial)
    if groups > 1:
        merged = over_seq(merged, same_member)
    return merged.transpose(1, 0, 2).reshape(local_rows, groups * width)


def solution(mesh):
    return jax.shard_map(
        body,
        mesh=mesh,
        in_specs=(
            P(("seq", "ctx"), None),
            P(("seq", "ctx"), None),
            P(("seq", "ctx"), None),
            P("seq", "ctx", None),
            P("seq", "ctx", None),
            P("seq", None, "ctx", None),
            P("seq", None, "ctx"),
        ),
        out_specs=P(("seq", "ctx"), None),
        check_vma=False,
    )
```

```python
import math

import jax
import jax.numpy as jnp
from jax import lax
from jax.experimental import pallas as pl
from jax.experimental.pallas import tpu as pltpu
from jax.sharding import PartitionSpec as P

HEADS_PER_GROUP = 8
TILE_QUERY_ROWS = 64
KROWS = 128
KQ = 12
LANES = 128
CTX = 4
NEAR = 2 * KROWS // TILE_QUERY_ROWS
AT_ONCE = 4
SLOTS_AT_ONCE = 4
LIST_ROWS = 8
COUNTS_AT = 16
MIB = 1024 * 1024
LOG2E = 1.4426950408889634


def nt(a, b):
    return lax.dot_general(a, b, (((1,), (1,)), ((), ())), preferred_element_type=jnp.float32)


def pack_kernel(*refs):
    sources, out_ref, targets = refs[:4], refs[4], refs[5:9]
    scratch, sems = refs[9:]
    copies = [
        pltpu.make_async_copy(source, target, sems.at[i])
        for i, (source, target) in enumerate(zip(sources, targets))
    ]
    for copy in copies:
        copy.start()
    keys, values, ids, counts = targets
    members, groups, _, _ = out_ref.shape
    local_rows = keys.shape[1]
    blocks = ids.shape[1]
    scratch[...] = jnp.zeros_like(scratch)
    for copy in copies:
        copy.wait()
    scratch[0:1, COUNTS_AT : COUNTS_AT + blocks] = counts[...].astype(jnp.float32)
    for member in range(members):
        for group in range(groups):
            block = group * members + member
            scratch[0:1, :KQ] = ids[0, block].astype(jnp.float32)
            out_ref[place_of(member), group, :local_rows] = keys[group]
            out_ref[place_of(member), group, local_rows : 2 * local_rows] = values[group]
            out_ref[place_of(member), group, 2 * local_rows :] = scratch[...].astype(jnp.bfloat16)


def place_of(member):
    half = HEADS_PER_GROUP // 2
    if isinstance(member, int):
        return 2 * (member - half) if member >= half else HEADS_PER_GROUP - 1 - 2 * member
    return jnp.where(member >= half, 2 * (member - half), HEADS_PER_GROUP - 1 - 2 * member)


def fetch_kernel(*refs):
    count = len(refs) // 2
    copies = [
        pltpu.make_async_copy(refs[i], refs[count + i], refs[-1].at[i]) for i in range(count)
    ]
    for copy in copies:
        copy.start()
    for copy in copies:
        copy.wait()


def attend_kernel(lists, near_ref, k_ref, v_hbm, *refs):
    q_refs, out_refs = refs[:CTX], refs[CTX : 2 * CTX]
    s_scr, m_scr, l_scr, v_ref, sem = refs[2 * CTX :]
    v_copy = pltpu.make_async_copy(v_hbm, v_ref, sem)
    v_copy.start()
    groups, local_rows, _ = q_refs[0].shape
    member = lax.rem(lax.axis_index("seq"), HEADS_PER_GROUP)
    quarter = lax.axis_index("ctx")
    rows = TILE_QUERY_ROWS
    head_size = k_ref.shape[2]
    scale = LOG2E / math.sqrt(head_size)
    shift, mask = local_rows.bit_length() - 1, local_rows - 1
    lane = lax.broadcasted_iota(jnp.int32, (rows, LANES), 1)
    sublane = lax.broadcasted_iota(jnp.int32, (rows, LANES), 0)

    def one_block(group):
        block = group * HEADS_PER_GROUP + member
        near = []
        for back in range(NEAR):
            place = jnp.maximum(group - jnp.where(member < back, 1, 0), 0)
            near.append(near_ref[place_of(lax.rem(member - back + HEADS_PER_GROUP, HEADS_PER_GROUP)), place])
        near_k = jnp.concatenate([one[:local_rows] for one in near] * 2, axis=0)
        near_v = jnp.concatenate([one[local_rows : 2 * local_rows] for one in near] * 2, axis=0)
        position = (block - (lane >> shift)) * rows + quarter * local_rows + (lane & mask)
        token = block * rows + ((sublane >> shift) ^ quarter) * local_rows + (sublane & mask)
        oldest = jnp.maximum((block * rows // KROWS - 1) * KROWS, 0)
        near_ok = (lane < rows) & (position <= token) & (position >= oldest)

        def columns_of(head):
            return pl.ds(pl.multiple_of(head * head_size, LANES), head_size)

        def scores(head):
            count = lists[place_of(head), group, COUNTS_AT + block]
            q = jnp.concatenate([q_ref[group, :, columns_of(head)] for q_ref in q_refs], axis=0)
            s = jnp.where(near_ok, nt(q, near_k), -jnp.inf)
            s_scr[head, KQ] = s
            high = s
            for slot in range(0, KQ, SLOTS_AT_ONCE):
                keys = [k_ref[lists[place_of(head), group, slot + i]] for i in range(SLOTS_AT_ONCE)]
                several = nt(q, jnp.concatenate(keys, axis=0))
                for i in range(SLOTS_AT_ONCE):
                    s = several[:, i * KROWS : (i + 1) * KROWS]
                    s = jnp.where(slot + i < count, s, -jnp.inf)
                    s_scr[head, slot + i] = s
                    high = jnp.maximum(high, s)
            m_scr[head] = high

        def sums(head):
            top = m_scr[head]
            total = jnp.exp2(s_scr[head, KQ] * scale - top)
            acc = jnp.dot(total.astype(jnp.bfloat16), near_v, preferred_element_type=jnp.float32)
            for slot in range(0, KQ, SLOTS_AT_ONCE):
                weights = []
                for part in range(slot, slot + SLOTS_AT_ONCE):
                    p = jnp.exp2(s_scr[head, part] * scale - top)
                    total = total + p
                    weights.append(p.astype(jnp.bfloat16))
                values = [v_ref[lists[place_of(head), group, slot + i]] for i in range(SLOTS_AT_ONCE)]
                acc = acc + jnp.dot(
                    jnp.concatenate(weights, axis=1),
                    jnp.concatenate(values, axis=0),
                    preferred_element_type=jnp.float32,
                )
            acc = acc.astype(jnp.bfloat16)
            for part, out_ref in enumerate(out_refs):
                out_ref[group, :, columns_of(head)] = acc[
                    part * local_rows : (part + 1) * local_rows
                ]
            l_scr[head] = total

        def in_steps(step):
            def several(turn, carry):
                for i in range(AT_ONCE):
                    step(turn * AT_ONCE + i)
                return carry

            lax.fori_loop(0, HEADS_PER_GROUP // AT_ONCE, several, 0)

        in_steps(scores)
        for head in range(HEADS_PER_GROUP):
            top = jnp.max(m_scr[head], axis=1, keepdims=True) * scale
            m_scr[head] = jnp.broadcast_to(top, (rows, LANES))
        if groups == 1:
            v_copy.wait()
        else:
            pl.when(group == 0)(v_copy.wait)
        in_steps(sums)
        stats = jnp.zeros((rows, LANES), jnp.float32)
        for head in range(HEADS_PER_GROUP):
            total = jnp.sum(l_scr[head], axis=1, keepdims=True)
            stats = jnp.where(lane == head, m_scr[head], stats)
            stats = jnp.where(lane == head + HEADS_PER_GROUP, total, stats)
        packed = jnp.zeros((rows, LANES), jnp.float32)
        for step in range(3):
            part = stats.astype(jnp.bfloat16).astype(jnp.float32)
            stats = stats - part
            by = step * 2 * HEADS_PER_GROUP
            packed = packed + (pltpu.roll(part, by, 1) if by else part)
        packed = packed.astype(jnp.bfloat16)
        width = HEADS_PER_GROUP * head_size
        for part, out_ref in enumerate(out_refs):
            out_ref[group, :, width:] = packed[part * local_rows : (part + 1) * local_rows]

    if groups == 1:
        one_block(0)
    else:
        pl.loop(0, groups)(one_block)


def merge_kernel(*refs):
    in_refs, out_ref = refs[:-1], refs[-1]
    groups, local_rows, full = in_refs[0].shape
    width = full - LANES
    head_size = width // HEADS_PER_GROUP

    def one_block(group):
        stats = []
        for in_ref in in_refs:
            packed = in_ref[group, :, width:].astype(jnp.float32)
            one = packed
            for step in (1, 2):
                one = one + pltpu.roll(packed, LANES - step * 2 * HEADS_PER_GROUP, 1)
            stats.append(one)
        top = stats[0]
        for one in stats[1:]:
            top = jnp.maximum(top, one)
        factors = [jnp.exp2(one - top) for one in stats]
        total = jnp.zeros((local_rows, LANES), jnp.float32)
        for one, factor in zip(stats, factors):
            total = total + pltpu.roll(one, LANES - HEADS_PER_GROUP, 1) * factor
        inverse = 1.0 / total
        factors = [factor * inverse for factor in factors]
        for head in range(HEADS_PER_GROUP):
            columns = slice(head * head_size, (head + 1) * head_size)
            mixed = jnp.zeros((local_rows, head_size), jnp.float32)
            for in_ref, factor in zip(in_refs, factors):
                mixed = mixed + in_ref[group, :, columns].astype(jnp.float32) * (
                    factor[:, head : head + 1]
                )
            out_ref[group, :, columns] = mixed.astype(jnp.bfloat16)

    if groups == 1:
        one_block(0)
    else:
        pl.loop(0, groups)(one_block)


def from_quarter(value, mask):
    return lax.ppermute(value, "ctx", [(device, device ^ mask) for device in range(CTX)])


def body(
    queries, new_token_keys, new_token_values, cache_keys, cache_values, block_ids, block_counts
):
    seq_count = lax.axis_size("seq")
    head_size = cache_keys.shape[2]
    local_rows = queries.shape[0]
    blocks = block_ids.shape[1]
    groups = seq_count // HEADS_PER_GROUP
    width = HEADS_PER_GROUP * head_size
    assert lax.axis_size("ctx") == CTX and cache_keys.shape[0] == 1
    assert local_rows * CTX == TILE_QUERY_ROWS and blocks <= LANES - COUNTS_AT
    assert head_size == LANES and local_rows & (local_rows - 1) == 0
    order = sorted(range(HEADS_PER_GROUP), key=place_of)
    same_group = [[g * HEADS_PER_GROUP + member for member in order] for g in range(groups)]
    if groups > 1:
        same_member = [
            [g * HEADS_PER_GROUP + r for g in range(groups)] for r in range(HEADS_PER_GROUP)
        ]

    def over_seq(pieces, members):
        return lax.all_to_all(
            pieces, "seq", split_axis=0, concat_axis=0, tiled=True, axis_index_groups=members
        )

    def in_hbm(value):
        return pltpu.with_memory_space_constraint(value, pltpu.HBM)

    def to_groups(rows):
        pieces = rows.reshape(local_rows, groups, -1).transpose(1, 0, 2)
        return pieces if groups == 1 else over_seq(pieces, same_member)

    vmem = pl.BlockSpec(memory_space=pltpu.VMEM)
    hbm = pl.BlockSpec(memory_space=pltpu.HBM)
    smem = pl.BlockSpec(memory_space=pltpu.SMEM)
    queries = to_groups(queries)
    others = [from_quarter(queries, mask) for mask in range(1, CTX)]
    small = (
        to_groups(new_token_keys),
        to_groups(new_token_values),
        block_ids,
        block_counts.reshape(1, blocks),
    )
    packed = pl.pallas_call(
        pack_kernel,
        out_shape=jax.ShapeDtypeStruct(
            (HEADS_PER_GROUP, groups, 2 * local_rows + LIST_ROWS, LANES), jnp.bfloat16
        ),
        in_specs=[hbm] * 4,
        out_specs=vmem,
        scratch_shapes=[pltpu.VMEM(one.shape, one.dtype) for one in small]
        + [pltpu.VMEM((LIST_ROWS, LANES), jnp.float32), pltpu.SemaphoreType.DMA((4,))],
        compiler_params=pltpu.CompilerParams(vmem_limit_bytes=4 * MIB),
        cost_estimate=pl.CostEstimate(flops=0, bytes_accessed=12 * MIB, transcendentals=0),
        name="pack",
    )(*[in_hbm(one) for one in small])
    large = (queries, cache_keys.reshape(-1, KROWS, head_size))
    queries, keys = pl.pallas_call(
        fetch_kernel,
        out_shape=[jax.ShapeDtypeStruct(one.shape, one.dtype) for one in large],
        in_specs=[hbm] * 2,
        out_specs=[vmem] * 2,
        scratch_shapes=[pltpu.SemaphoreType.DMA((2,))],
        compiler_params=pltpu.CompilerParams(vmem_limit_bytes=4 * MIB),
        cost_estimate=pl.CostEstimate(flops=0, bytes_accessed=4 * MIB, transcendentals=0),
        name="fetch",
    )(*[in_hbm(one) for one in large])
    near = over_seq(packed, same_group)
    lists = near[:, :, 2 * local_rows].astype(jnp.int32)
    tile = (TILE_QUERY_ROWS, KROWS)
    values = cache_values.reshape(-1, KROWS, head_size)
    partial = pl.pallas_call(
        attend_kernel,
        out_shape=[
            jax.ShapeDtypeStruct((groups, local_rows, width + LANES), jnp.bfloat16)
        ] * CTX,
        in_specs=[smem, vmem, vmem, hbm] + [vmem] * CTX,
        out_specs=[vmem] * CTX,
        scratch_shapes=[
            pltpu.VMEM((HEADS_PER_GROUP, KQ + 1) + tile, jnp.float32),
            pltpu.VMEM((HEADS_PER_GROUP,) + tile, jnp.float32),
            pltpu.VMEM((HEADS_PER_GROUP,) + tile, jnp.float32),
            pltpu.VMEM(values.shape, values.dtype),
            pltpu.SemaphoreType.DMA,
        ],
        compiler_params=pltpu.CompilerParams(vmem_limit_bytes=24 * MIB),
        name="attend",
    )(lists, near, keys, in_hbm(values), queries, *others)
    partial = [from_quarter(partial[mask], mask) for mask in (2, 3, 1)] + [partial[0]]
    merged = pl.pallas_call(
        merge_kernel,
        out_shape=jax.ShapeDtypeStruct((groups, local_rows, width), jnp.bfloat16),
        in_specs=[vmem] * CTX,
        out_specs=vmem,
        compiler_params=pltpu.CompilerParams(vmem_limit_bytes=4 * MIB),
        name="merge",
    )(*partial)
    if groups > 1:
        merged = over_seq(merged, same_member)
    return merged.transpose(1, 0, 2).reshape(local_rows, groups * width)


def solution(mesh):
    return jax.shard_map(
        body,
        mesh=mesh,
        in_specs=(
            P(("seq", "ctx"), None),
            P(("seq", "ctx"), None),
            P(("seq", "ctx"), None),
            P("seq", "ctx", None),
            P("seq", "ctx", None),
            P("seq", None, "ctx", None),
            P("seq", None, "ctx"),
        ),
        out_specs=P(("seq", "ctx"), None),
        check_vma=False,
    )
```

```python
import math

import jax
import jax.numpy as jnp
from jax import lax
from jax.experimental import pallas as pl
from jax.experimental.pallas import tpu as pltpu
from jax.sharding import PartitionSpec as P

HEADS_PER_GROUP = 8
TILE_QUERY_ROWS = 64
KROWS = 128
KQ = 12
LANES = 128
CTX = 4
NEAR = 2 * KROWS // TILE_QUERY_ROWS
AT_ONCE = 4
MEETING_ORDER = (5, 7, 4, 3, 6, 2, 1, 0)
SLOTS_AT_ONCE = 4
LIST_ROWS = 8
COUNTS_AT = 16
MIB = 1024 * 1024
LOG2E = 1.4426950408889634


def nt(a, b):
    return lax.dot_general(a, b, (((1,), (1,)), ((), ())), preferred_element_type=jnp.float32)


def pack_kernel(*refs):
    sources, out_ref, targets = refs[:4], refs[4], refs[5:9]
    scratch, sems = refs[9:]
    copies = [
        pltpu.make_async_copy(source, target, sems.at[i])
        for i, (source, target) in enumerate(zip(sources, targets))
    ]
    for copy in copies:
        copy.start()
    keys, values, ids, counts = targets
    members, groups, _, _ = out_ref.shape
    local_rows = keys.shape[1]
    blocks = ids.shape[1]
    scratch[...] = jnp.zeros_like(scratch)
    for copy in copies:
        copy.wait()
    scratch[0:1, COUNTS_AT : COUNTS_AT + blocks] = counts[...].astype(jnp.float32)
    for member in range(members):
        for group in range(groups):
            block = group * members + member
            scratch[0:1, :KQ] = ids[0, block].astype(jnp.float32)
            out_ref[place_of(member), group, :local_rows] = keys[group]
            out_ref[place_of(member), group, local_rows : 2 * local_rows] = values[group]
            out_ref[place_of(member), group, 2 * local_rows :] = scratch[...].astype(jnp.bfloat16)


def place_of(member):
    if isinstance(member, int):
        return MEETING_ORDER.index(member)
    return sum(jnp.where(member == one, place, 0) for place, one in enumerate(MEETING_ORDER))


def fetch_kernel(*refs):
    count = len(refs) // 2
    copies = [
        pltpu.make_async_copy(refs[i], refs[count + i], refs[-1].at[i]) for i in range(count)
    ]
    for copy in copies:
        copy.start()
    for copy in copies:
        copy.wait()


def attend_kernel(lists, near_ref, k_ref, v_hbm, *refs):
    q_refs, out_refs = refs[:CTX], refs[CTX : 2 * CTX]
    s_scr, m_scr, l_scr, v_ref, sem = refs[2 * CTX :]
    v_copy = pltpu.make_async_copy(v_hbm, v_ref, sem)
    v_copy.start()
    groups, local_rows, _ = q_refs[0].shape
    member = lax.rem(lax.axis_index("seq"), HEADS_PER_GROUP)
    quarter = lax.axis_index("ctx")
    rows = TILE_QUERY_ROWS
    head_size = k_ref.shape[2]
    scale = LOG2E / math.sqrt(head_size)
    shift, mask = local_rows.bit_length() - 1, local_rows - 1
    lane = lax.broadcasted_iota(jnp.int32, (rows, LANES), 1)
    sublane = lax.broadcasted_iota(jnp.int32, (rows, LANES), 0)

    def one_block(group):
        block = group * HEADS_PER_GROUP + member
        near = []
        for back in range(NEAR):
            place = jnp.maximum(group - jnp.where(member < back, 1, 0), 0)
            near.append(near_ref[place_of(lax.rem(member - back + HEADS_PER_GROUP, HEADS_PER_GROUP)), place])
        near_k = jnp.concatenate([one[:local_rows] for one in near] * 2, axis=0)
        near_v = jnp.concatenate([one[local_rows : 2 * local_rows] for one in near] * 2, axis=0)
        position = (block - (lane >> shift)) * rows + quarter * local_rows + (lane & mask)
        token = block * rows + ((sublane >> shift) ^ quarter) * local_rows + (sublane & mask)
        oldest = jnp.maximum((block * rows // KROWS - 1) * KROWS, 0)
        near_ok = (lane < rows) & (position <= token) & (position >= oldest)

        def columns_of(head):
            return pl.ds(pl.multiple_of(head * head_size, LANES), head_size)

        def scores(head):
            count = lists[place_of(head), group, COUNTS_AT + block]
            q = jnp.concatenate([q_ref[group, :, columns_of(head)] for q_ref in q_refs], axis=0)
            s = jnp.where(near_ok, nt(q, near_k), -jnp.inf)
            s_scr[head, KQ] = s
            high = s
            for slot in range(0, KQ, SLOTS_AT_ONCE):
                keys = [k_ref[lists[place_of(head), group, slot + i]] for i in range(SLOTS_AT_ONCE)]
                several = nt(q, jnp.concatenate(keys, axis=0))
                for i in range(SLOTS_AT_ONCE):
                    s = several[:, i * KROWS : (i + 1) * KROWS]
                    s = jnp.where(slot + i < count, s, -jnp.inf)
                    s_scr[head, slot + i] = s
                    high = jnp.maximum(high, s)
            m_scr[head] = high

        def sums(head):
            top = m_scr[head]
            total = jnp.exp2(s_scr[head, KQ] * scale - top)
            acc = jnp.dot(total.astype(jnp.bfloat16), near_v, preferred_element_type=jnp.float32)
            for slot in range(0, KQ, SLOTS_AT_ONCE):
                weights = []
                for part in range(slot, slot + SLOTS_AT_ONCE):
                    p = jnp.exp2(s_scr[head, part] * scale - top)
                    total = total + p
                    weights.append(p.astype(jnp.bfloat16))
                values = [v_ref[lists[place_of(head), group, slot + i]] for i in range(SLOTS_AT_ONCE)]
                acc = acc + jnp.dot(
                    jnp.concatenate(weights, axis=1),
                    jnp.concatenate(values, axis=0),
                    preferred_element_type=jnp.float32,
                )
            acc = acc.astype(jnp.bfloat16)
            for part, out_ref in enumerate(out_refs):
                out_ref[group, :, columns_of(head)] = acc[
                    part * local_rows : (part + 1) * local_rows
                ]
            l_scr[head] = total

        def in_steps(step):
            def several(turn, carry):
                for i in range(AT_ONCE):
                    step(turn * AT_ONCE + i)
                return carry

            lax.fori_loop(0, HEADS_PER_GROUP // AT_ONCE, several, 0)

        in_steps(scores)
        for head in range(HEADS_PER_GROUP):
            top = jnp.max(m_scr[head], axis=1, keepdims=True) * scale
            m_scr[head] = jnp.broadcast_to(top, (rows, LANES))
        if groups == 1:
            v_copy.wait()
        else:
            pl.when(group == 0)(v_copy.wait)
        in_steps(sums)
        stats = jnp.zeros((rows, LANES), jnp.float32)
        for head in range(HEADS_PER_GROUP):
            total = jnp.sum(l_scr[head], axis=1, keepdims=True)
            stats = jnp.where(lane == head, m_scr[head], stats)
            stats = jnp.where(lane == head + HEADS_PER_GROUP, total, stats)
        packed = jnp.zeros((rows, LANES), jnp.float32)
        for step in range(3):
            part = stats.astype(jnp.bfloat16).astype(jnp.float32)
            stats = stats - part
            by = step * 2 * HEADS_PER_GROUP
            packed = packed + (pltpu.roll(part, by, 1) if by else part)
        packed = packed.astype(jnp.bfloat16)
        width = HEADS_PER_GROUP * head_size
        for part, out_ref in enumerate(out_refs):
            out_ref[group, :, width:] = packed[part * local_rows : (part + 1) * local_rows]

    if groups == 1:
        one_block(0)
    else:
        pl.loop(0, groups)(one_block)


def merge_kernel(*refs):
    in_refs, out_ref = refs[:-1], refs[-1]
    groups, local_rows, full = in_refs[0].shape
    width = full - LANES
    head_size = width // HEADS_PER_GROUP

    def one_block(group):
        stats = []
        for in_ref in in_refs:
            packed = in_ref[group, :, width:].astype(jnp.float32)
            one = packed
            for step in (1, 2):
                one = one + pltpu.roll(packed, LANES - step * 2 * HEADS_PER_GROUP, 1)
            stats.append(one)
        top = stats[0]
        for one in stats[1:]:
            top = jnp.maximum(top, one)
        factors = [jnp.exp2(one - top) for one in stats]
        total = jnp.zeros((local_rows, LANES), jnp.float32)
        for one, factor in zip(stats, factors):
            total = total + pltpu.roll(one, LANES - HEADS_PER_GROUP, 1) * factor
        inverse = 1.0 / total
        factors = [factor * inverse for factor in factors]
        for head in range(HEADS_PER_GROUP):
            columns = slice(head * head_size, (head + 1) * head_size)
            mixed = jnp.zeros((local_rows, head_size), jnp.float32)
            for in_ref, factor in zip(in_refs, factors):
                mixed = mixed + in_ref[group, :, columns].astype(jnp.float32) * (
                    factor[:, head : head + 1]
                )
            out_ref[group, :, columns] = mixed.astype(jnp.bfloat16)

    if groups == 1:
        one_block(0)
    else:
        pl.loop(0, groups)(one_block)


def from_quarter(value, mask):
    return lax.ppermute(value, "ctx", [(device, device ^ mask) for device in range(CTX)])


def body(
    queries, new_token_keys, new_token_values, cache_keys, cache_values, block_ids, block_counts
):
    seq_count = lax.axis_size("seq")
    head_size = cache_keys.shape[2]
    local_rows = queries.shape[0]
    blocks = block_ids.shape[1]
    groups = seq_count // HEADS_PER_GROUP
    width = HEADS_PER_GROUP * head_size
    assert lax.axis_size("ctx") == CTX and cache_keys.shape[0] == 1
    assert local_rows * CTX == TILE_QUERY_ROWS and blocks <= LANES - COUNTS_AT
    assert head_size == LANES and local_rows & (local_rows - 1) == 0
    same_group = [[g * HEADS_PER_GROUP + member for member in MEETING_ORDER] for g in range(groups)]
    if groups > 1:
        same_member = [
            [g * HEADS_PER_GROUP + r for g in range(groups)] for r in range(HEADS_PER_GROUP)
        ]

    def over_seq(pieces, members):
        return lax.all_to_all(
            pieces, "seq", split_axis=0, concat_axis=0, tiled=True, axis_index_groups=members
        )

    def in_hbm(value):
        return pltpu.with_memory_space_constraint(value, pltpu.HBM)

    def to_groups(rows):
        pieces = rows.reshape(local_rows, groups, -1).transpose(1, 0, 2)
        return pieces if groups == 1 else over_seq(pieces, same_member)

    vmem = pl.BlockSpec(memory_space=pltpu.VMEM)
    hbm = pl.BlockSpec(memory_space=pltpu.HBM)
    smem = pl.BlockSpec(memory_space=pltpu.SMEM)
    queries = to_groups(queries)
    others = [from_quarter(queries, mask) for mask in range(1, CTX)]
    small = (
        to_groups(new_token_keys),
        to_groups(new_token_values),
        block_ids,
        block_counts.reshape(1, blocks),
    )
    packed = pl.pallas_call(
        pack_kernel,
        out_shape=jax.ShapeDtypeStruct(
            (HEADS_PER_GROUP, groups, 2 * local_rows + LIST_ROWS, LANES), jnp.bfloat16
        ),
        in_specs=[hbm] * 4,
        out_specs=vmem,
        scratch_shapes=[pltpu.VMEM(one.shape, one.dtype) for one in small]
        + [pltpu.VMEM((LIST_ROWS, LANES), jnp.float32), pltpu.SemaphoreType.DMA((4,))],
        compiler_params=pltpu.CompilerParams(vmem_limit_bytes=4 * MIB),
        cost_estimate=pl.CostEstimate(flops=0, bytes_accessed=12 * MIB, transcendentals=0),
        name="pack",
    )(*[in_hbm(one) for one in small])
    large = (queries, cache_keys.reshape(-1, KROWS, head_size))
    queries, keys = pl.pallas_call(
        fetch_kernel,
        out_shape=[jax.ShapeDtypeStruct(one.shape, one.dtype) for one in large],
        in_specs=[hbm] * 2,
        out_specs=[vmem] * 2,
        scratch_shapes=[pltpu.SemaphoreType.DMA((2,))],
        compiler_params=pltpu.CompilerParams(vmem_limit_bytes=4 * MIB),
        cost_estimate=pl.CostEstimate(flops=0, bytes_accessed=4 * MIB, transcendentals=0),
        name="fetch",
    )(*[in_hbm(one) for one in large])
    near = over_seq(packed, same_group)
    lists = near[:, :, 2 * local_rows].astype(jnp.int32)
    tile = (TILE_QUERY_ROWS, KROWS)
    values = cache_values.reshape(-1, KROWS, head_size)
    partial = pl.pallas_call(
        attend_kernel,
        out_shape=[
            jax.ShapeDtypeStruct((groups, local_rows, width + LANES), jnp.bfloat16)
        ] * CTX,
        in_specs=[smem, vmem, vmem, hbm] + [vmem] * CTX,
        out_specs=[vmem] * CTX,
        scratch_shapes=[
            pltpu.VMEM((HEADS_PER_GROUP, KQ + 1) + tile, jnp.float32),
            pltpu.VMEM((HEADS_PER_GROUP,) + tile, jnp.float32),
            pltpu.VMEM((HEADS_PER_GROUP,) + tile, jnp.float32),
            pltpu.VMEM(values.shape, values.dtype),
            pltpu.SemaphoreType.DMA,
        ],
        compiler_params=pltpu.CompilerParams(vmem_limit_bytes=24 * MIB),
        name="attend",
    )(lists, near, keys, in_hbm(values), queries, *others)
    partial = [from_quarter(partial[mask], mask) for mask in (2, 3, 1)] + [partial[0]]
    merged = pl.pallas_call(
        merge_kernel,
        out_shape=jax.ShapeDtypeStruct((groups, local_rows, width), jnp.bfloat16),
        in_specs=[vmem] * CTX,
        out_specs=vmem,
        compiler_params=pltpu.CompilerParams(vmem_limit_bytes=4 * MIB),
        name="merge",
    )(*partial)
    if groups > 1:
        merged = over_seq(merged, same_member)
    return merged.transpose(1, 0, 2).reshape(local_rows, groups * width)


def solution(mesh):
    return jax.shard_map(
        body,
        mesh=mesh,
        in_specs=(
            P(("seq", "ctx"), None),
            P(("seq", "ctx"), None),
            P(("seq", "ctx"), None),
            P("seq", "ctx", None),
            P("seq", "ctx", None),
            P("seq", None, "ctx", None),
            P("seq", None, "ctx"),
        ),
        out_specs=P(("seq", "ctx"), None),
        check_vma=False,
    )
```

```python
import math

import jax
import jax.numpy as jnp
from jax import lax
from jax.experimental import pallas as pl
from jax.experimental.pallas import tpu as pltpu
from jax.sharding import PartitionSpec as P

HEADS_PER_GROUP = 8
TILE_QUERY_ROWS = 64
KROWS = 128
KQ = 12
LANES = 128
CTX = 4
NEAR = 2 * KROWS // TILE_QUERY_ROWS
AT_ONCE = 4
MEETING_ORDER = (4, 0, 1, 2, 3, 5, 6, 7)
SLOTS_AT_ONCE = 4
LIST_ROWS = 8
COUNTS_AT = 16
MIB = 1024 * 1024
LOG2E = 1.4426950408889634


def nt(a, b):
    return lax.dot_general(a, b, (((1,), (1,)), ((), ())), preferred_element_type=jnp.float32)


def pack_kernel(*refs):
    sources, out_ref, targets = refs[:4], refs[4], refs[5:9]
    scratch, sems = refs[9:]
    copies = [
        pltpu.make_async_copy(source, target, sems.at[i])
        for i, (source, target) in enumerate(zip(sources, targets))
    ]
    for copy in copies:
        copy.start()
    keys, values, ids, counts = targets
    members, groups, _, _ = out_ref.shape
    local_rows = keys.shape[1]
    blocks = ids.shape[1]
    scratch[...] = jnp.zeros_like(scratch)
    for copy in copies:
        copy.wait()
    scratch[0:1, COUNTS_AT : COUNTS_AT + blocks] = counts[...].astype(jnp.float32)
    for member in range(members):
        for group in range(groups):
            block = group * members + member
            scratch[0:1, :KQ] = ids[0, block].astype(jnp.float32)
            out_ref[place_of(member), group, :local_rows] = keys[group]
            out_ref[place_of(member), group, local_rows : 2 * local_rows] = values[group]
            out_ref[place_of(member), group, 2 * local_rows :] = scratch[...].astype(jnp.bfloat16)


def place_of(member):
    if isinstance(member, int):
        return MEETING_ORDER.index(member)
    return sum(jnp.where(member == one, place, 0) for place, one in enumerate(MEETING_ORDER))


def fetch_kernel(*refs):
    count = len(refs) // 2
    copies = [
        pltpu.make_async_copy(refs[i], refs[count + i], refs[-1].at[i]) for i in range(count)
    ]
    for copy in copies:
        copy.start()
    for copy in copies:
        copy.wait()


def attend_kernel(lists, near_ref, k_ref, v_hbm, *refs):
    q_refs, out_refs = refs[:CTX], refs[CTX : 2 * CTX]
    s_scr, m_scr, l_scr, v_ref, sem = refs[2 * CTX :]
    v_copy = pltpu.make_async_copy(v_hbm, v_ref, sem)
    v_copy.start()
    groups, local_rows, _ = q_refs[0].shape
    member = lax.rem(lax.axis_index("seq"), HEADS_PER_GROUP)
    quarter = lax.axis_index("ctx")
    rows = TILE_QUERY_ROWS
    head_size = k_ref.shape[2]
    scale = LOG2E / math.sqrt(head_size)
    shift, mask = local_rows.bit_length() - 1, local_rows - 1
    lane = lax.broadcasted_iota(jnp.int32, (rows, LANES), 1)
    sublane = lax.broadcasted_iota(jnp.int32, (rows, LANES), 0)

    def one_block(group):
        block = group * HEADS_PER_GROUP + member
        near = []
        for back in range(NEAR):
            place = jnp.maximum(group - jnp.where(member < back, 1, 0), 0)
            near.append(near_ref[place_of(lax.rem(member - back + HEADS_PER_GROUP, HEADS_PER_GROUP)), place])
        near_k = jnp.concatenate([one[:local_rows] for one in near] * 2, axis=0)
        near_v = jnp.concatenate([one[local_rows : 2 * local_rows] for one in near] * 2, axis=0)
        position = (block - (lane >> shift)) * rows + quarter * local_rows + (lane & mask)
        token = block * rows + ((sublane >> shift) ^ quarter) * local_rows + (sublane & mask)
        oldest = jnp.maximum((block * rows // KROWS - 1) * KROWS, 0)
        near_ok = (lane < rows) & (position <= token) & (position >= oldest)

        def columns_of(head):
            return pl.ds(pl.multiple_of(head * head_size, LANES), head_size)

        def scores(head):
            count = lists[place_of(head), group, COUNTS_AT + block]
            q = jnp.concatenate([q_ref[group, :, columns_of(head)] for q_ref in q_refs], axis=0)
            s = jnp.where(near_ok, nt(q, near_k), -jnp.inf)
            s_scr[head, KQ] = s
            high = s
            for slot in range(0, KQ, SLOTS_AT_ONCE):
                keys = [k_ref[lists[place_of(head), group, slot + i]] for i in range(SLOTS_AT_ONCE)]
                several = nt(q, jnp.concatenate(keys, axis=0))
                for i in range(SLOTS_AT_ONCE):
                    s = several[:, i * KROWS : (i + 1) * KROWS]
                    s = jnp.where(slot + i < count, s, -jnp.inf)
                    s_scr[head, slot + i] = s
                    high = jnp.maximum(high, s)
            m_scr[head] = high

        def sums(head):
            top = m_scr[head]
            total = jnp.exp2(s_scr[head, KQ] * scale - top)
            acc = jnp.dot(total.astype(jnp.bfloat16), near_v, preferred_element_type=jnp.float32)
            for slot in range(0, KQ, SLOTS_AT_ONCE):
                weights = []
                for part in range(slot, slot + SLOTS_AT_ONCE):
                    p = jnp.exp2(s_scr[head, part] * scale - top)
                    total = total + p
                    weights.append(p.astype(jnp.bfloat16))
                values = [v_ref[lists[place_of(head), group, slot + i]] for i in range(SLOTS_AT_ONCE)]
                acc = acc + jnp.dot(
                    jnp.concatenate(weights, axis=1),
                    jnp.concatenate(values, axis=0),
                    preferred_element_type=jnp.float32,
                )
            acc = acc.astype(jnp.bfloat16)
            for part, out_ref in enumerate(out_refs):
                out_ref[group, :, columns_of(head)] = acc[
                    part * local_rows : (part + 1) * local_rows
                ]
            l_scr[head] = total

        def in_steps(step):
            def several(turn, carry):
                for i in range(AT_ONCE):
                    step(turn * AT_ONCE + i)
                return carry

            lax.fori_loop(0, HEADS_PER_GROUP // AT_ONCE, several, 0)

        in_steps(scores)
        for head in range(HEADS_PER_GROUP):
            top = jnp.max(m_scr[head], axis=1, keepdims=True) * scale
            m_scr[head] = jnp.broadcast_to(top, (rows, LANES))
        if groups == 1:
            v_copy.wait()
        else:
            pl.when(group == 0)(v_copy.wait)
        in_steps(sums)
        stats = jnp.zeros((rows, LANES), jnp.float32)
        for head in range(HEADS_PER_GROUP):
            total = jnp.sum(l_scr[head], axis=1, keepdims=True)
            stats = jnp.where(lane == head, m_scr[head], stats)
            stats = jnp.where(lane == head + HEADS_PER_GROUP, total, stats)
        packed = jnp.zeros((rows, LANES), jnp.float32)
        for step in range(3):
            part = stats.astype(jnp.bfloat16).astype(jnp.float32)
            stats = stats - part
            by = step * 2 * HEADS_PER_GROUP
            packed = packed + (pltpu.roll(part, by, 1) if by else part)
        packed = packed.astype(jnp.bfloat16)
        width = HEADS_PER_GROUP * head_size
        for part, out_ref in enumerate(out_refs):
            out_ref[group, :, width:] = packed[part * local_rows : (part + 1) * local_rows]

    if groups == 1:
        one_block(0)
    else:
        pl.loop(0, groups)(one_block)


def merge_kernel(*refs):
    in_refs, out_ref = refs[:-1], refs[-1]
    groups, local_rows, full = in_refs[0].shape
    width = full - LANES
    head_size = width // HEADS_PER_GROUP

    def one_block(group):
        stats = []
        for in_ref in in_refs:
            packed = in_ref[group, :, width:].astype(jnp.float32)
            one = packed
            for step in (1, 2):
                one = one + pltpu.roll(packed, LANES - step * 2 * HEADS_PER_GROUP, 1)
            stats.append(one)
        top = stats[0]
        for one in stats[1:]:
            top = jnp.maximum(top, one)
        factors = [jnp.exp2(one - top) for one in stats]
        total = jnp.zeros((local_rows, LANES), jnp.float32)
        for one, factor in zip(stats, factors):
            total = total + pltpu.roll(one, LANES - HEADS_PER_GROUP, 1) * factor
        inverse = 1.0 / total
        factors = [factor * inverse for factor in factors]
        for head in range(HEADS_PER_GROUP):
            columns = slice(head * head_size, (head + 1) * head_size)
            mixed = jnp.zeros((local_rows, head_size), jnp.float32)
            for in_ref, factor in zip(in_refs, factors):
                mixed = mixed + in_ref[group, :, columns].astype(jnp.float32) * (
                    factor[:, head : head + 1]
                )
            out_ref[group, :, columns] = mixed.astype(jnp.bfloat16)

    if groups == 1:
        one_block(0)
    else:
        pl.loop(0, groups)(one_block)


def from_quarter(value, mask):
    return lax.ppermute(value, "ctx", [(device, device ^ mask) for device in range(CTX)])


def body(
    queries, new_token_keys, new_token_values, cache_keys, cache_values, block_ids, block_counts
):
    seq_count = lax.axis_size("seq")
    head_size = cache_keys.shape[2]
    local_rows = queries.shape[0]
    blocks = block_ids.shape[1]
    groups = seq_count // HEADS_PER_GROUP
    width = HEADS_PER_GROUP * head_size
    assert lax.axis_size("ctx") == CTX and cache_keys.shape[0] == 1
    assert local_rows * CTX == TILE_QUERY_ROWS and blocks <= LANES - COUNTS_AT
    assert head_size == LANES and local_rows & (local_rows - 1) == 0
    same_group = [[g * HEADS_PER_GROUP + member for member in MEETING_ORDER] for g in range(groups)]
    if groups > 1:
        same_member = [
            [g * HEADS_PER_GROUP + r for g in range(groups)] for r in range(HEADS_PER_GROUP)
        ]

    def over_seq(pieces, members):
        return lax.all_to_all(
            pieces, "seq", split_axis=0, concat_axis=0, tiled=True, axis_index_groups=members
        )

    def in_hbm(value):
        return pltpu.with_memory_space_constraint(value, pltpu.HBM)

    def to_groups(rows):
        pieces = rows.reshape(local_rows, groups, -1).transpose(1, 0, 2)
        return pieces if groups == 1 else over_seq(pieces, same_member)

    vmem = pl.BlockSpec(memory_space=pltpu.VMEM)
    hbm = pl.BlockSpec(memory_space=pltpu.HBM)
    smem = pl.BlockSpec(memory_space=pltpu.SMEM)
    queries = to_groups(queries)
    others = [from_quarter(queries, mask) for mask in range(1, CTX)]
    small = (
        to_groups(new_token_keys),
        to_groups(new_token_values),
        block_ids,
        block_counts.reshape(1, blocks),
    )
    packed = pl.pallas_call(
        pack_kernel,
        out_shape=jax.ShapeDtypeStruct(
            (HEADS_PER_GROUP, groups, 2 * local_rows + LIST_ROWS, LANES), jnp.bfloat16
        ),
        in_specs=[hbm] * 4,
        out_specs=vmem,
        scratch_shapes=[pltpu.VMEM(one.shape, one.dtype) for one in small]
        + [pltpu.VMEM((LIST_ROWS, LANES), jnp.float32), pltpu.SemaphoreType.DMA((4,))],
        compiler_params=pltpu.CompilerParams(vmem_limit_bytes=4 * MIB),
        cost_estimate=pl.CostEstimate(flops=0, bytes_accessed=12 * MIB, transcendentals=0),
        name="pack",
    )(*[in_hbm(one) for one in small])
    large = (queries, cache_keys.reshape(-1, KROWS, head_size))
    queries, keys = pl.pallas_call(
        fetch_kernel,
        out_shape=[jax.ShapeDtypeStruct(one.shape, one.dtype) for one in large],
        in_specs=[hbm] * 2,
        out_specs=[vmem] * 2,
        scratch_shapes=[pltpu.SemaphoreType.DMA((2,))],
        compiler_params=pltpu.CompilerParams(vmem_limit_bytes=4 * MIB),
        cost_estimate=pl.CostEstimate(flops=0, bytes_accessed=4 * MIB, transcendentals=0),
        name="fetch",
    )(*[in_hbm(one) for one in large])
    near = over_seq(packed, same_group)
    lists = near[:, :, 2 * local_rows].astype(jnp.int32)
    tile = (TILE_QUERY_ROWS, KROWS)
    values = cache_values.reshape(-1, KROWS, head_size)
    partial = pl.pallas_call(
        attend_kernel,
        out_shape=[
            jax.ShapeDtypeStruct((groups, local_rows, width + LANES), jnp.bfloat16)
        ] * CTX,
        in_specs=[smem, vmem, vmem, hbm] + [vmem] * CTX,
        out_specs=[vmem] * CTX,
        scratch_shapes=[
            pltpu.VMEM((HEADS_PER_GROUP, KQ + 1) + tile, jnp.float32),
            pltpu.VMEM((HEADS_PER_GROUP,) + tile, jnp.float32),
            pltpu.VMEM((HEADS_PER_GROUP,) + tile, jnp.float32),
            pltpu.VMEM(values.shape, values.dtype),
            pltpu.SemaphoreType.DMA,
        ],
        compiler_params=pltpu.CompilerParams(vmem_limit_bytes=24 * MIB),
        name="attend",
    )(lists, near, keys, in_hbm(values), queries, *others)
    partial = [from_quarter(partial[mask], mask) for mask in (3, 2, 1)] + [partial[0]]
    merged = pl.pallas_call(
        merge_kernel,
        out_shape=jax.ShapeDtypeStruct((groups, local_rows, width), jnp.bfloat16),
        in_specs=[vmem] * CTX,
        out_specs=vmem,
        compiler_params=pltpu.CompilerParams(vmem_limit_bytes=4 * MIB),
        name="merge",
    )(*partial)
    if groups > 1:
        merged = over_seq(merged, same_member)
    return merged.transpose(1, 0, 2).reshape(local_rows, groups * width)


def solution(mesh):
    return jax.shard_map(
        body,
        mesh=mesh,
        in_specs=(
            P(("seq", "ctx"), None),
            P(("seq", "ctx"), None),
            P(("seq", "ctx"), None),
            P("seq", "ctx", None),
            P("seq", "ctx", None),
            P("seq", None, "ctx", None),
            P("seq", None, "ctx"),
        ),
        out_specs=P(("seq", "ctx"), None),
        check_vma=False,
    )
```

```python
import math

import jax
import jax.numpy as jnp
from jax import lax
from jax.experimental import pallas as pl
from jax.experimental.pallas import tpu as pltpu
from jax.sharding import PartitionSpec as P

HEADS_PER_GROUP = 8
TILE_QUERY_ROWS = 64
KROWS = 128
KQ = 12
LANES = 128
CTX = 4
NEAR = 2 * KROWS // TILE_QUERY_ROWS
AT_ONCE = 4
MEETING_ORDER = (4, 0, 1, 2, 3, 5, 6, 7)
SLOTS_AT_ONCE = 4
LIST_ROWS = 8
COUNTS_AT = 16
MIB = 1024 * 1024
LOG2E = 1.4426950408889634


def nt(a, b):
    return lax.dot_general(a, b, (((1,), (1,)), ((), ())), preferred_element_type=jnp.float32)


def pack_kernel(*refs):
    sources, out_ref, targets = refs[:4], refs[4], refs[5:9]
    scratch, sems = refs[9:]
    copies = [
        pltpu.make_async_copy(source, target, sems.at[i])
        for i, (source, target) in enumerate(zip(sources, targets))
    ]
    for copy in copies:
        copy.start()
    keys, values, ids, counts = targets
    members, groups, _, _ = out_ref.shape
    local_rows = keys.shape[1]
    blocks = ids.shape[1]
    scratch[...] = jnp.zeros_like(scratch)
    for copy in copies:
        copy.wait()
    scratch[0:1, COUNTS_AT : COUNTS_AT + blocks] = counts[...].astype(jnp.float32)
    for member in range(members):
        for group in range(groups):
            block = group * members + member
            scratch[0:1, :KQ] = ids[0, block].astype(jnp.float32)
            out_ref[place_of(member), group, :local_rows] = keys[group]
            out_ref[place_of(member), group, local_rows : 2 * local_rows] = values[group]
            out_ref[place_of(member), group, 2 * local_rows :] = scratch[...].astype(jnp.bfloat16)


def place_of(member):
    if isinstance(member, int):
        return MEETING_ORDER.index(member)
    return sum(jnp.where(member == one, place, 0) for place, one in enumerate(MEETING_ORDER))


def fetch_kernel(*refs):
    count = len(refs) // 2
    copies = [
        pltpu.make_async_copy(refs[i], refs[count + i], refs[-1].at[i]) for i in range(count)
    ]
    for copy in copies:
        copy.start()
    for copy in copies:
        copy.wait()


def attend_kernel(lists, near_ref, k_ref, v_hbm, *refs):
    q_refs, out_refs = refs[:CTX], refs[CTX : 2 * CTX]
    s_scr, m_scr, l_scr, v_ref, sem = refs[2 * CTX :]
    v_copy = pltpu.make_async_copy(v_hbm, v_ref, sem)
    v_copy.start()
    groups, local_rows, _ = q_refs[0].shape
    member = lax.rem(lax.axis_index("seq"), HEADS_PER_GROUP)
    quarter = lax.axis_index("ctx")
    rows = TILE_QUERY_ROWS
    head_size = k_ref.shape[2]
    scale = LOG2E / math.sqrt(head_size)
    shift, mask = local_rows.bit_length() - 1, local_rows - 1
    lane = lax.broadcasted_iota(jnp.int32, (rows, LANES), 1)
    sublane = lax.broadcasted_iota(jnp.int32, (rows, LANES), 0)

    def one_block(group):
        block = group * HEADS_PER_GROUP + member
        near = []
        for back in range(NEAR):
            place = jnp.maximum(group - jnp.where(member < back, 1, 0), 0)
            near.append(near_ref[place_of(lax.rem(member - back + HEADS_PER_GROUP, HEADS_PER_GROUP)), place])
        near_k = jnp.concatenate([one[:local_rows] for one in near] * 2, axis=0)
        near_v = jnp.concatenate([one[local_rows : 2 * local_rows] for one in near] * 2, axis=0)
        position = (block - (lane >> shift)) * rows + quarter * local_rows + (lane & mask)
        token = block * rows + ((sublane >> shift) ^ quarter) * local_rows + (sublane & mask)
        oldest = jnp.maximum((block * rows // KROWS - 1) * KROWS, 0)
        near_ok = (lane < rows) & (position <= token) & (position >= oldest)

        def columns_of(head):
            return pl.ds(pl.multiple_of(head * head_size, LANES), head_size)

        def scores(head):
            count = lists[place_of(head), group, COUNTS_AT + block]
            q = jnp.concatenate([q_ref[group, :, columns_of(head)] for q_ref in q_refs], axis=0)
            s = jnp.where(near_ok, nt(q, near_k), -jnp.inf)
            s_scr[head, KQ] = s
            high = s
            for slot in range(0, KQ, SLOTS_AT_ONCE):
                keys = [k_ref[lists[place_of(head), group, slot + i]] for i in range(SLOTS_AT_ONCE)]
                several = nt(q, jnp.concatenate(keys, axis=0))
                for i in range(SLOTS_AT_ONCE):
                    s = several[:, i * KROWS : (i + 1) * KROWS]
                    s = jnp.where(slot + i < count, s, -jnp.inf)
                    s_scr[head, slot + i] = s
                    high = jnp.maximum(high, s)
            m_scr[head] = high

        def sums(head):
            top = m_scr[head]
            total = jnp.exp2(s_scr[head, KQ] * scale - top)
            acc = jnp.dot(total.astype(jnp.bfloat16), near_v, preferred_element_type=jnp.float32)
            for slot in range(0, KQ, SLOTS_AT_ONCE):
                weights = []
                for part in range(slot, slot + SLOTS_AT_ONCE):
                    p = jnp.exp2(s_scr[head, part] * scale - top)
                    total = total + p
                    weights.append(p.astype(jnp.bfloat16))
                values = [v_ref[lists[place_of(head), group, slot + i]] for i in range(SLOTS_AT_ONCE)]
                acc = acc + jnp.dot(
                    jnp.concatenate(weights, axis=1),
                    jnp.concatenate(values, axis=0),
                    preferred_element_type=jnp.float32,
                )
            acc = acc.astype(jnp.bfloat16)
            for part, out_ref in enumerate(out_refs):
                out_ref[group, :, columns_of(head)] = acc[
                    part * local_rows : (part + 1) * local_rows
                ]
            l_scr[head] = total

        def in_steps(step):
            def several(turn, carry):
                for i in range(AT_ONCE):
                    step(turn * AT_ONCE + i)
                return carry

            lax.fori_loop(0, HEADS_PER_GROUP // AT_ONCE, several, 0)

        in_steps(scores)
        for head in range(HEADS_PER_GROUP):
            top = jnp.max(m_scr[head], axis=1, keepdims=True) * scale
            m_scr[head] = jnp.broadcast_to(top, (rows, LANES))
        if groups == 1:
            v_copy.wait()
        else:
            pl.when(group == 0)(v_copy.wait)
        in_steps(sums)
        stats = jnp.zeros((rows, LANES), jnp.float32)
        for head in range(HEADS_PER_GROUP):
            total = jnp.sum(l_scr[head], axis=1, keepdims=True)
            stats = jnp.where(lane == head, m_scr[head], stats)
            stats = jnp.where(lane == head + HEADS_PER_GROUP, total, stats)
        packed = jnp.zeros((rows, LANES), jnp.float32)
        for step in range(3):
            part = stats.astype(jnp.bfloat16).astype(jnp.float32)
            stats = stats - part
            by = step * 2 * HEADS_PER_GROUP
            packed = packed + (pltpu.roll(part, by, 1) if by else part)
        packed = packed.astype(jnp.bfloat16)
        width = HEADS_PER_GROUP * head_size
        for part, out_ref in enumerate(out_refs):
            out_ref[group, :, width:] = packed[part * local_rows : (part + 1) * local_rows]

    if groups == 1:
        one_block(0)
    else:
        pl.loop(0, groups)(one_block)


def merge_kernel(*refs):
    in_refs, out_ref = refs[:-1], refs[-1]
    groups, local_rows, full = in_refs[0].shape
    width = full - LANES
    head_size = width // HEADS_PER_GROUP

    def one_block(group):
        stats = []
        for in_ref in in_refs:
            packed = in_ref[group, :, width:].astype(jnp.float32)
            one = packed
            for step in (1, 2):
                one = one + pltpu.roll(packed, LANES - step * 2 * HEADS_PER_GROUP, 1)
            stats.append(one)
        top = stats[0]
        for one in stats[1:]:
            top = jnp.maximum(top, one)
        factors = [jnp.exp2(one - top) for one in stats]
        total = jnp.zeros((local_rows, LANES), jnp.float32)
        for one, factor in zip(stats, factors):
            total = total + pltpu.roll(one, LANES - HEADS_PER_GROUP, 1) * factor
        inverse = 1.0 / total
        factors = [factor * inverse for factor in factors]
        for head in range(HEADS_PER_GROUP):
            columns = slice(head * head_size, (head + 1) * head_size)
            mixed = jnp.zeros((local_rows, head_size), jnp.float32)
            for in_ref, factor in zip(in_refs, factors):
                mixed = mixed + in_ref[group, :, columns].astype(jnp.float32) * (
                    factor[:, head : head + 1]
                )
            out_ref[group, :, columns] = mixed.astype(jnp.bfloat16)

    if groups == 1:
        one_block(0)
    else:
        pl.loop(0, groups)(one_block)


def from_quarter(value, mask):
    return lax.ppermute(value, "ctx", [(device, device ^ mask) for device in reversed(range(CTX))])


def body(
    queries, new_token_keys, new_token_values, cache_keys, cache_values, block_ids, block_counts
):
    seq_count = lax.axis_size("seq")
    head_size = cache_keys.shape[2]
    local_rows = queries.shape[0]
    blocks = block_ids.shape[1]
    groups = seq_count // HEADS_PER_GROUP
    width = HEADS_PER_GROUP * head_size
    assert lax.axis_size("ctx") == CTX and cache_keys.shape[0] == 1
    assert local_rows * CTX == TILE_QUERY_ROWS and blocks <= LANES - COUNTS_AT
    assert head_size == LANES and local_rows & (local_rows - 1) == 0
    same_group = [[g * HEADS_PER_GROUP + member for member in MEETING_ORDER] for g in range(groups)]
    if groups > 1:
        same_member = [
            [g * HEADS_PER_GROUP + r for g in range(groups)] for r in range(HEADS_PER_GROUP)
        ]

    def over_seq(pieces, members):
        return lax.all_to_all(
            pieces, "seq", split_axis=0, concat_axis=0, tiled=True, axis_index_groups=members
        )

    def in_hbm(value):
        return pltpu.with_memory_space_constraint(value, pltpu.HBM)

    def to_groups(rows):
        pieces = rows.reshape(local_rows, groups, -1).transpose(1, 0, 2)
        return pieces if groups == 1 else over_seq(pieces, same_member)

    vmem = pl.BlockSpec(memory_space=pltpu.VMEM)
    hbm = pl.BlockSpec(memory_space=pltpu.HBM)
    smem = pl.BlockSpec(memory_space=pltpu.SMEM)
    queries = to_groups(queries)
    others = [from_quarter(queries, mask) for mask in range(1, CTX)]
    small = (
        to_groups(new_token_keys),
        to_groups(new_token_values),
        block_ids,
        block_counts.reshape(1, blocks),
    )
    packed = pl.pallas_call(
        pack_kernel,
        out_shape=jax.ShapeDtypeStruct(
            (HEADS_PER_GROUP, groups, 2 * local_rows + LIST_ROWS, LANES), jnp.bfloat16
        ),
        in_specs=[hbm] * 4,
        out_specs=vmem,
        scratch_shapes=[pltpu.VMEM(one.shape, one.dtype) for one in small]
        + [pltpu.VMEM((LIST_ROWS, LANES), jnp.float32), pltpu.SemaphoreType.DMA((4,))],
        compiler_params=pltpu.CompilerParams(vmem_limit_bytes=4 * MIB),
        cost_estimate=pl.CostEstimate(flops=0, bytes_accessed=12 * MIB, transcendentals=0),
        name="pack",
    )(*[in_hbm(one) for one in small])
    large = (queries, cache_keys.reshape(-1, KROWS, head_size))
    queries, keys = pl.pallas_call(
        fetch_kernel,
        out_shape=[jax.ShapeDtypeStruct(one.shape, one.dtype) for one in large],
        in_specs=[hbm] * 2,
        out_specs=[vmem] * 2,
        scratch_shapes=[pltpu.SemaphoreType.DMA((2,))],
        compiler_params=pltpu.CompilerParams(vmem_limit_bytes=4 * MIB),
        cost_estimate=pl.CostEstimate(flops=0, bytes_accessed=4 * MIB, transcendentals=0),
        name="fetch",
    )(*[in_hbm(one) for one in large])
    near = over_seq(packed, same_group)
    lists = near[:, :, 2 * local_rows].astype(jnp.int32)
    tile = (TILE_QUERY_ROWS, KROWS)
    values = cache_values.reshape(-1, KROWS, head_size)
    partial = pl.pallas_call(
        attend_kernel,
        out_shape=[
            jax.ShapeDtypeStruct((groups, local_rows, width + LANES), jnp.bfloat16)
        ] * CTX,
        in_specs=[smem, vmem, vmem, hbm] + [vmem] * CTX,
        out_specs=[vmem] * CTX,
        scratch_shapes=[
            pltpu.VMEM((HEADS_PER_GROUP, KQ + 1) + tile, jnp.float32),
            pltpu.VMEM((HEADS_PER_GROUP,) + tile, jnp.float32),
            pltpu.VMEM((HEADS_PER_GROUP,) + tile, jnp.float32),
            pltpu.VMEM(values.shape, values.dtype),
            pltpu.SemaphoreType.DMA,
        ],
        compiler_params=pltpu.CompilerParams(vmem_limit_bytes=24 * MIB),
        name="attend",
    )(lists, near, keys, in_hbm(values), queries, *others)
    partial = [from_quarter(partial[mask], mask) for mask in (3, 2, 1)] + [partial[0]]
    merged = pl.pallas_call(
        merge_kernel,
        out_shape=jax.ShapeDtypeStruct((groups, local_rows, width), jnp.bfloat16),
        in_specs=[vmem] * CTX,
        out_specs=vmem,
        compiler_params=pltpu.CompilerParams(vmem_limit_bytes=4 * MIB),
        name="merge",
    )(*partial)
    if groups > 1:
        merged = over_seq(merged, same_member)
    return merged.transpose(1, 0, 2).reshape(local_rows, groups * width)


def solution(mesh):
    return jax.shard_map(
        body,
        mesh=mesh,
        in_specs=(
            P(("seq", "ctx"), None),
            P(("seq", "ctx"), None),
            P(("seq", "ctx"), None),
            P("seq", "ctx", None),
            P("seq", "ctx", None),
            P("seq", None, "ctx", None),
            P("seq", None, "ctx"),
        ),
        out_specs=P(("seq", "ctx"), None),
        check_vma=False,
    )
```

```python
import math

import jax
import jax.numpy as jnp
from jax import lax
from jax.experimental import pallas as pl
from jax.experimental.pallas import tpu as pltpu
from jax.sharding import PartitionSpec as P

HEADS_PER_GROUP = 8
TILE_QUERY_ROWS = 64
KROWS = 128
KQ = 12
LANES = 128
CTX = 4
NEAR = 2 * KROWS // TILE_QUERY_ROWS
AT_ONCE = 4
MEETING_ORDERS = ((4, 0, 1, 2, 3, 5, 6, 7), (6, 0, 1, 2, 3, 4, 5, 7))
SLOTS_AT_ONCE = 4
LIST_ROWS = 8
COUNTS_AT = 16
MIB = 1024 * 1024
LOG2E = 1.4426950408889634


def nt(a, b):
    return lax.dot_general(a, b, (((1,), (1,)), ((), ())), preferred_element_type=jnp.float32)


def pack_kernel(*refs):
    sources, out_ref, targets = refs[:4], refs[4], refs[5:9]
    scratch, sems = refs[9:]
    copies = [
        pltpu.make_async_copy(source, target, sems.at[i])
        for i, (source, target) in enumerate(zip(sources, targets))
    ]
    for copy in copies:
        copy.start()
    keys, values, ids, counts = targets
    members, groups, _, _ = out_ref.shape
    local_rows = keys.shape[1]
    blocks = ids.shape[1]
    scratch[...] = jnp.zeros_like(scratch)
    for copy in copies:
        copy.wait()
    scratch[0:1, COUNTS_AT : COUNTS_AT + blocks] = counts[...].astype(jnp.float32)
    quarter = lax.axis_index("ctx")
    for member in range(members):
        place = place_of(member, quarter)
        for group in range(groups):
            block = group * members + member
            scratch[0:1, :KQ] = ids[0, block].astype(jnp.float32)
            out_ref[place, group, :local_rows] = keys[group]
            out_ref[place, group, local_rows : 2 * local_rows] = values[group]
            out_ref[place, group, 2 * local_rows :] = scratch[...].astype(jnp.bfloat16)


def place_of(member, quarter):
    odd = lax.rem(quarter, 2) == 1
    places = []
    for order in MEETING_ORDERS:
        if isinstance(member, int):
            places.append(jnp.int32(order.index(member)))
        else:
            places.append(sum(jnp.where(member == one, i, 0) for i, one in enumerate(order)))
    return jnp.where(odd, places[1], places[0])


def fetch_kernel(*refs):
    count = len(refs) // 2
    copies = [
        pltpu.make_async_copy(refs[i], refs[count + i], refs[-1].at[i]) for i in range(count)
    ]
    for copy in copies:
        copy.start()
    for copy in copies:
        copy.wait()


def attend_kernel(lists, near_ref, k_ref, v_hbm, *refs):
    q_refs, out_refs = refs[:CTX], refs[CTX : 2 * CTX]
    s_scr, m_scr, l_scr, v_ref, sem = refs[2 * CTX :]
    v_copy = pltpu.make_async_copy(v_hbm, v_ref, sem)
    v_copy.start()
    groups, local_rows, _ = q_refs[0].shape
    member = lax.rem(lax.axis_index("seq"), HEADS_PER_GROUP)
    quarter = lax.axis_index("ctx")
    rows = TILE_QUERY_ROWS
    head_size = k_ref.shape[2]
    scale = LOG2E / math.sqrt(head_size)
    shift, mask = local_rows.bit_length() - 1, local_rows - 1
    lane = lax.broadcasted_iota(jnp.int32, (rows, LANES), 1)
    sublane = lax.broadcasted_iota(jnp.int32, (rows, LANES), 0)

    def one_block(group):
        block = group * HEADS_PER_GROUP + member
        near = []
        for back in range(NEAR):
            place = jnp.maximum(group - jnp.where(member < back, 1, 0), 0)
            source = lax.rem(member - back + HEADS_PER_GROUP, HEADS_PER_GROUP)
            near.append(near_ref[place_of(source, quarter), place])
        near_k = jnp.concatenate([one[:local_rows] for one in near] * 2, axis=0)
        near_v = jnp.concatenate([one[local_rows : 2 * local_rows] for one in near] * 2, axis=0)
        position = (block - (lane >> shift)) * rows + quarter * local_rows + (lane & mask)
        token = block * rows + ((sublane >> shift) ^ quarter) * local_rows + (sublane & mask)
        oldest = jnp.maximum((block * rows // KROWS - 1) * KROWS, 0)
        near_ok = (lane < rows) & (position <= token) & (position >= oldest)

        def columns_of(head):
            return pl.ds(pl.multiple_of(head * head_size, LANES), head_size)

        def scores(head):
            place = place_of(head, quarter)
            count = lists[place, group, COUNTS_AT + block]
            q = jnp.concatenate([q_ref[group, :, columns_of(head)] for q_ref in q_refs], axis=0)
            s = jnp.where(near_ok, nt(q, near_k), -jnp.inf)
            s_scr[head, KQ] = s
            high = s
            for slot in range(0, KQ, SLOTS_AT_ONCE):
                keys = [k_ref[lists[place, group, slot + i]] for i in range(SLOTS_AT_ONCE)]
                several = nt(q, jnp.concatenate(keys, axis=0))
                for i in range(SLOTS_AT_ONCE):
                    s = several[:, i * KROWS : (i + 1) * KROWS]
                    s = jnp.where(slot + i < count, s, -jnp.inf)
                    s_scr[head, slot + i] = s
                    high = jnp.maximum(high, s)
            m_scr[head] = high

        def sums(head):
            place = place_of(head, quarter)
            top = m_scr[head]
            total = jnp.exp2(s_scr[head, KQ] * scale - top)
            acc = jnp.dot(total.astype(jnp.bfloat16), near_v, preferred_element_type=jnp.float32)
            for slot in range(0, KQ, SLOTS_AT_ONCE):
                weights = []
                for part in range(slot, slot + SLOTS_AT_ONCE):
                    p = jnp.exp2(s_scr[head, part] * scale - top)
                    total = total + p
                    weights.append(p.astype(jnp.bfloat16))
                values = [v_ref[lists[place, group, slot + i]] for i in range(SLOTS_AT_ONCE)]
                acc = acc + jnp.dot(
                    jnp.concatenate(weights, axis=1),
                    jnp.concatenate(values, axis=0),
                    preferred_element_type=jnp.float32,
                )
            acc = acc.astype(jnp.bfloat16)
            for part, out_ref in enumerate(out_refs):
                out_ref[group, :, columns_of(head)] = acc[
                    part * local_rows : (part + 1) * local_rows
                ]
            l_scr[head] = total

        def in_steps(step):
            def several(turn, carry):
                for i in range(AT_ONCE):
                    step(turn * AT_ONCE + i)
                return carry

            lax.fori_loop(0, HEADS_PER_GROUP // AT_ONCE, several, 0)

        in_steps(scores)
        for head in range(HEADS_PER_GROUP):
            top = jnp.max(m_scr[head], axis=1, keepdims=True) * scale
            m_scr[head] = jnp.broadcast_to(top, (rows, LANES))
        if groups == 1:
            v_copy.wait()
        else:
            pl.when(group == 0)(v_copy.wait)
        in_steps(sums)
        stats = jnp.zeros((rows, LANES), jnp.float32)
        for head in range(HEADS_PER_GROUP):
            total = jnp.sum(l_scr[head], axis=1, keepdims=True)
            stats = jnp.where(lane == head, m_scr[head], stats)
            stats = jnp.where(lane == head + HEADS_PER_GROUP, total, stats)
        packed = jnp.zeros((rows, LANES), jnp.float32)
        for step in range(3):
            part = stats.astype(jnp.bfloat16).astype(jnp.float32)
            stats = stats - part
            by = step * 2 * HEADS_PER_GROUP
            packed = packed + (pltpu.roll(part, by, 1) if by else part)
        packed = packed.astype(jnp.bfloat16)
        width = HEADS_PER_GROUP * head_size
        for part, out_ref in enumerate(out_refs):
            out_ref[group, :, width:] = packed[part * local_rows : (part + 1) * local_rows]

    if groups == 1:
        one_block(0)
    else:
        pl.loop(0, groups)(one_block)


def merge_kernel(*refs):
    in_refs, out_ref = refs[:-1], refs[-1]
    groups, local_rows, full = in_refs[0].shape
    width = full - LANES
    head_size = width // HEADS_PER_GROUP

    def one_block(group):
        stats = []
        for in_ref in in_refs:
            packed = in_ref[group, :, width:].astype(jnp.float32)
            one = packed
            for step in (1, 2):
                one = one + pltpu.roll(packed, LANES - step * 2 * HEADS_PER_GROUP, 1)
            stats.append(one)
        top = stats[0]
        for one in stats[1:]:
            top = jnp.maximum(top, one)
        factors = [jnp.exp2(one - top) for one in stats]
        total = jnp.zeros((local_rows, LANES), jnp.float32)
        for one, factor in zip(stats, factors):
            total = total + pltpu.roll(one, LANES - HEADS_PER_GROUP, 1) * factor
        inverse = 1.0 / total
        factors = [factor * inverse for factor in factors]
        for head in range(HEADS_PER_GROUP):
            columns = slice(head * head_size, (head + 1) * head_size)
            mixed = jnp.zeros((local_rows, head_size), jnp.float32)
            for in_ref, factor in zip(in_refs, factors):
                mixed = mixed + in_ref[group, :, columns].astype(jnp.float32) * (
                    factor[:, head : head + 1]
                )
            out_ref[group, :, columns] = mixed.astype(jnp.bfloat16)

    if groups == 1:
        one_block(0)
    else:
        pl.loop(0, groups)(one_block)


def from_quarter(value, mask):
    return lax.ppermute(value, "ctx", [(device, device ^ mask) for device in range(CTX)])


def body(
    queries, new_token_keys, new_token_values, cache_keys, cache_values, block_ids, block_counts
):
    seq_count = lax.axis_size("seq")
    head_size = cache_keys.shape[2]
    local_rows = queries.shape[0]
    blocks = block_ids.shape[1]
    groups = seq_count // HEADS_PER_GROUP
    width = HEADS_PER_GROUP * head_size
    assert lax.axis_size("ctx") == CTX and cache_keys.shape[0] == 1
    assert local_rows * CTX == TILE_QUERY_ROWS and blocks <= LANES - COUNTS_AT
    assert head_size == LANES and local_rows & (local_rows - 1) == 0
    same_group = []
    for g in range(groups):
        for c in range(CTX):
            order = MEETING_ORDERS[c % 2]
            same_group.append([(g * HEADS_PER_GROUP + member) * CTX + c for member in order])
    if groups > 1:
        same_member = [
            [g * HEADS_PER_GROUP + r for g in range(groups)] for r in range(HEADS_PER_GROUP)
        ]

    def over_seq(pieces, members):
        return lax.all_to_all(
            pieces, "seq", split_axis=0, concat_axis=0, tiled=True, axis_index_groups=members
        )

    def in_hbm(value):
        return pltpu.with_memory_space_constraint(value, pltpu.HBM)

    def to_groups(rows):
        pieces = rows.reshape(local_rows, groups, -1).transpose(1, 0, 2)
        return pieces if groups == 1 else over_seq(pieces, same_member)

    vmem = pl.BlockSpec(memory_space=pltpu.VMEM)
    hbm = pl.BlockSpec(memory_space=pltpu.HBM)
    smem = pl.BlockSpec(memory_space=pltpu.SMEM)
    queries = to_groups(queries)
    others = [from_quarter(queries, mask) for mask in range(1, CTX)]
    small = (
        to_groups(new_token_keys),
        to_groups(new_token_values),
        block_ids,
        block_counts.reshape(1, blocks),
    )
    packed = pl.pallas_call(
        pack_kernel,
        out_shape=jax.ShapeDtypeStruct(
            (HEADS_PER_GROUP, groups, 2 * local_rows + LIST_ROWS, LANES), jnp.bfloat16
        ),
        in_specs=[hbm] * 4,
        out_specs=vmem,
        scratch_shapes=[pltpu.VMEM(one.shape, one.dtype) for one in small]
        + [pltpu.VMEM((LIST_ROWS, LANES), jnp.float32), pltpu.SemaphoreType.DMA((4,))],
        compiler_params=pltpu.CompilerParams(vmem_limit_bytes=4 * MIB),
        cost_estimate=pl.CostEstimate(flops=0, bytes_accessed=12 * MIB, transcendentals=0),
        name="pack",
    )(*[in_hbm(one) for one in small])
    large = (queries, cache_keys.reshape(-1, KROWS, head_size))
    queries, keys = pl.pallas_call(
        fetch_kernel,
        out_shape=[jax.ShapeDtypeStruct(one.shape, one.dtype) for one in large],
        in_specs=[hbm] * 2,
        out_specs=[vmem] * 2,
        scratch_shapes=[pltpu.SemaphoreType.DMA((2,))],
        compiler_params=pltpu.CompilerParams(vmem_limit_bytes=4 * MIB),
        cost_estimate=pl.CostEstimate(flops=0, bytes_accessed=4 * MIB, transcendentals=0),
        name="fetch",
    )(*[in_hbm(one) for one in large])
    near = lax.all_to_all(
        packed,
        ("seq", "ctx"),
        split_axis=0,
        concat_axis=0,
        tiled=True,
        axis_index_groups=same_group,
    )
    lists = near[:, :, 2 * local_rows].astype(jnp.int32)
    tile = (TILE_QUERY_ROWS, KROWS)
    values = cache_values.reshape(-1, KROWS, head_size)
    partial = pl.pallas_call(
        attend_kernel,
        out_shape=[
            jax.ShapeDtypeStruct((groups, local_rows, width + LANES), jnp.bfloat16)
        ] * CTX,
        in_specs=[smem, vmem, vmem, hbm] + [vmem] * CTX,
        out_specs=[vmem] * CTX,
        scratch_shapes=[
            pltpu.VMEM((HEADS_PER_GROUP, KQ + 1) + tile, jnp.float32),
            pltpu.VMEM((HEADS_PER_GROUP,) + tile, jnp.float32),
            pltpu.VMEM((HEADS_PER_GROUP,) + tile, jnp.float32),
            pltpu.VMEM(values.shape, values.dtype),
            pltpu.SemaphoreType.DMA,
        ],
        compiler_params=pltpu.CompilerParams(vmem_limit_bytes=24 * MIB),
        name="attend",
    )(lists, near, keys, in_hbm(values), queries, *others)
    partial = [from_quarter(partial[mask], mask) for mask in (3, 2, 1)] + [partial[0]]
    merged = pl.pallas_call(
        merge_kernel,
        out_shape=jax.ShapeDtypeStruct((groups, local_rows, width), jnp.bfloat16),
        in_specs=[vmem] * CTX,
        out_specs=vmem,
        compiler_params=pltpu.CompilerParams(vmem_limit_bytes=4 * MIB),
        name="merge",
    )(*partial)
    if groups > 1:
        merged = over_seq(merged, same_member)
    return merged.transpose(1, 0, 2).reshape(local_rows, groups * width)


def solution(mesh):
    return jax.shard_map(
        body,
        mesh=mesh,
        in_specs=(
            P(("seq", "ctx"), None),
            P(("seq", "ctx"), None),
            P(("seq", "ctx"), None),
            P("seq", "ctx", None),
            P("seq", "ctx", None),
            P("seq", None, "ctx", None),
            P("seq", None, "ctx"),
        ),
        out_specs=P(("seq", "ctx"), None),
        check_vma=False,
    )
```

```python
import math

import jax
import jax.numpy as jnp
from jax import lax
from jax.experimental import pallas as pl
from jax.experimental.pallas import tpu as pltpu
from jax.sharding import PartitionSpec as P

HEADS_PER_GROUP = 8
TILE_QUERY_ROWS = 64
KROWS = 128
KQ = 12
LANES = 128
CTX = 4
NEAR = 2 * KROWS // TILE_QUERY_ROWS
AT_ONCE = 4
MEETING_ORDERS = ((4, 0, 1, 2, 3, 5, 6, 7), (6, 0, 1, 2, 3, 4, 5, 7))
SLOTS_AT_ONCE = 4
LIST_ROWS = 8
COUNTS_AT = 16
MIB = 1024 * 1024
LOG2E = 1.4426950408889634


def nt(a, b):
    return lax.dot_general(a, b, (((1,), (1,)), ((), ())), preferred_element_type=jnp.float32)


def pack_kernel(*refs):
    sources, (out_ref, q_ref), targets = refs[:5], refs[5:7], refs[7:11]
    scratch, sems = refs[11:]
    copies = [
        pltpu.make_async_copy(source, target, sems.at[i])
        for i, (source, target) in enumerate(zip(sources, targets + (q_ref,)))
    ]
    for copy in copies:
        copy.start()
    keys, values, ids, counts = targets
    members, groups, _, _ = out_ref.shape
    local_rows = keys.shape[1]
    blocks = ids.shape[1]
    scratch[...] = jnp.zeros_like(scratch)
    for copy in copies:
        copy.wait()
    scratch[0:1, COUNTS_AT : COUNTS_AT + blocks] = counts[...].astype(jnp.float32)
    quarter = lax.axis_index("ctx")
    for member in range(members):
        place = place_of(member, quarter)
        for group in range(groups):
            block = group * members + member
            scratch[0:1, :KQ] = ids[0, block].astype(jnp.float32)
            out_ref[place, group, :local_rows] = keys[group]
            out_ref[place, group, local_rows : 2 * local_rows] = values[group]
            out_ref[place, group, 2 * local_rows :] = scratch[...].astype(jnp.bfloat16)


def place_of(member, quarter):
    odd = lax.rem(quarter, 2) == 1
    places = []
    for order in MEETING_ORDERS:
        if isinstance(member, int):
            places.append(jnp.int32(order.index(member)))
        else:
            places.append(sum(jnp.where(member == one, i, 0) for i, one in enumerate(order)))
    return jnp.where(odd, places[1], places[0])


def fetch_kernel(source, target, sem):
    copy = pltpu.make_async_copy(source, target, sem)
    copy.start()
    copy.wait()


def attend_kernel(lists, near_ref, k_ref, v_hbm, *refs):
    own, beside, across = refs[:3]
    q_refs, refs = (own, beside, across.at[0], across.at[1]), refs[3:]
    out_refs, refs = refs[:CTX], refs[CTX:]
    s_scr, m_scr, l_scr, v_ref, sem = refs
    v_copy = pltpu.make_async_copy(v_hbm, v_ref, sem)
    v_copy.start()
    groups, local_rows, _ = q_refs[0].shape
    member = lax.rem(lax.axis_index("seq"), HEADS_PER_GROUP)
    quarter = lax.axis_index("ctx")
    rows = TILE_QUERY_ROWS
    head_size = k_ref.shape[2]
    scale = LOG2E / math.sqrt(head_size)
    shift, mask = local_rows.bit_length() - 1, local_rows - 1
    lane = lax.broadcasted_iota(jnp.int32, (rows, LANES), 1)
    sublane = lax.broadcasted_iota(jnp.int32, (rows, LANES), 0)

    def one_block(group):
        block = group * HEADS_PER_GROUP + member
        near = []
        for back in range(NEAR):
            place = jnp.maximum(group - jnp.where(member < back, 1, 0), 0)
            source = lax.rem(member - back + HEADS_PER_GROUP, HEADS_PER_GROUP)
            near.append(near_ref[place_of(source, quarter), place])
        near_k = jnp.concatenate([one[:local_rows] for one in near] * 2, axis=0)
        near_v = jnp.concatenate([one[local_rows : 2 * local_rows] for one in near] * 2, axis=0)
        position = (block - (lane >> shift)) * rows + quarter * local_rows + (lane & mask)
        token = block * rows + ((sublane >> shift) ^ quarter) * local_rows + (sublane & mask)
        oldest = jnp.maximum((block * rows // KROWS - 1) * KROWS, 0)
        near_ok = (lane < rows) & (position <= token) & (position >= oldest)

        def columns_of(head):
            return pl.ds(pl.multiple_of(head * head_size, LANES), head_size)

        def scores(head):
            place = place_of(head, quarter)
            count = lists[place, group, COUNTS_AT + block]
            q = jnp.concatenate([q_ref[group, :, columns_of(head)] for q_ref in q_refs], axis=0)
            s = jnp.where(near_ok, nt(q, near_k), -jnp.inf)
            s_scr[head, KQ] = s
            high = s
            for slot in range(0, KQ, SLOTS_AT_ONCE):
                keys = [k_ref[lists[place, group, slot + i]] for i in range(SLOTS_AT_ONCE)]
                several = nt(q, jnp.concatenate(keys, axis=0))
                for i in range(SLOTS_AT_ONCE):
                    s = several[:, i * KROWS : (i + 1) * KROWS]
                    s = jnp.where(slot + i < count, s, -jnp.inf)
                    s_scr[head, slot + i] = s
                    high = jnp.maximum(high, s)
            m_scr[head] = high

        def sums(head):
            place = place_of(head, quarter)
            top = m_scr[head]
            total = jnp.exp2(s_scr[head, KQ] * scale - top)
            acc = jnp.dot(total.astype(jnp.bfloat16), near_v, preferred_element_type=jnp.float32)
            for slot in range(0, KQ, SLOTS_AT_ONCE):
                weights = []
                for part in range(slot, slot + SLOTS_AT_ONCE):
                    p = jnp.exp2(s_scr[head, part] * scale - top)
                    total = total + p
                    weights.append(p.astype(jnp.bfloat16))
                values = [v_ref[lists[place, group, slot + i]] for i in range(SLOTS_AT_ONCE)]
                acc = acc + jnp.dot(
                    jnp.concatenate(weights, axis=1),
                    jnp.concatenate(values, axis=0),
                    preferred_element_type=jnp.float32,
                )
            acc = acc.astype(jnp.bfloat16)
            for part, out_ref in enumerate(out_refs):
                out_ref[group, :, columns_of(head)] = acc[
                    part * local_rows : (part + 1) * local_rows
                ]
            l_scr[head] = total

        def in_steps(step):
            def several(turn, carry):
                for i in range(AT_ONCE):
                    step(turn * AT_ONCE + i)
                return carry

            lax.fori_loop(0, HEADS_PER_GROUP // AT_ONCE, several, 0)

        in_steps(scores)
        for head in range(HEADS_PER_GROUP):
            top = jnp.max(m_scr[head], axis=1, keepdims=True) * scale
            m_scr[head] = jnp.broadcast_to(top, (rows, LANES))
        if groups == 1:
            v_copy.wait()
        else:
            pl.when(group == 0)(v_copy.wait)
        in_steps(sums)
        stats = jnp.zeros((rows, LANES), jnp.float32)
        for head in range(HEADS_PER_GROUP):
            total = jnp.sum(l_scr[head], axis=1, keepdims=True)
            stats = jnp.where(lane == head, m_scr[head], stats)
            stats = jnp.where(lane == head + HEADS_PER_GROUP, total, stats)
        packed = jnp.zeros((rows, LANES), jnp.float32)
        for step in range(3):
            part = stats.astype(jnp.bfloat16).astype(jnp.float32)
            stats = stats - part
            by = step * 2 * HEADS_PER_GROUP
            packed = packed + (pltpu.roll(part, by, 1) if by else part)
        packed = packed.astype(jnp.bfloat16)
        width = HEADS_PER_GROUP * head_size
        for part, out_ref in enumerate(out_refs):
            out_ref[group, :, width:] = packed[part * local_rows : (part + 1) * local_rows]

    if groups == 1:
        one_block(0)
    else:
        pl.loop(0, groups)(one_block)


def merge_kernel(*refs):
    in_refs, out_ref = refs[:-1], refs[-1]
    groups, local_rows, full = in_refs[0].shape
    width = full - LANES
    head_size = width // HEADS_PER_GROUP

    def one_block(group):
        stats = []
        for in_ref in in_refs:
            packed = in_ref[group, :, width:].astype(jnp.float32)
            one = packed
            for step in (1, 2):
                one = one + pltpu.roll(packed, LANES - step * 2 * HEADS_PER_GROUP, 1)
            stats.append(one)
        top = stats[0]
        for one in stats[1:]:
            top = jnp.maximum(top, one)
        factors = [jnp.exp2(one - top) for one in stats]
        total = jnp.zeros((local_rows, LANES), jnp.float32)
        for one, factor in zip(stats, factors):
            total = total + pltpu.roll(one, LANES - HEADS_PER_GROUP, 1) * factor
        inverse = 1.0 / total
        factors = [factor * inverse for factor in factors]
        for head in range(HEADS_PER_GROUP):
            columns = slice(head * head_size, (head + 1) * head_size)
            mixed = jnp.zeros((local_rows, head_size), jnp.float32)
            for in_ref, factor in zip(in_refs, factors):
                mixed = mixed + in_ref[group, :, columns].astype(jnp.float32) * (
                    factor[:, head : head + 1]
                )
            out_ref[group, :, columns] = mixed.astype(jnp.bfloat16)

    if groups == 1:
        one_block(0)
    else:
        pl.loop(0, groups)(one_block)


def from_quarter(value, mask):
    return lax.ppermute(value, "ctx", [(device, device ^ mask) for device in range(CTX)])


def body(
    queries, new_token_keys, new_token_values, cache_keys, cache_values, block_ids, block_counts
):
    seq_count = lax.axis_size("seq")
    head_size = cache_keys.shape[2]
    local_rows = queries.shape[0]
    blocks = block_ids.shape[1]
    groups = seq_count // HEADS_PER_GROUP
    width = HEADS_PER_GROUP * head_size
    assert lax.axis_size("ctx") == CTX and cache_keys.shape[0] == 1
    assert local_rows * CTX == TILE_QUERY_ROWS and blocks <= LANES - COUNTS_AT
    assert head_size == LANES and local_rows & (local_rows - 1) == 0
    same_group = []
    for g in range(groups):
        for c in range(CTX):
            order = MEETING_ORDERS[c % 2]
            same_group.append([(g * HEADS_PER_GROUP + member) * CTX + c for member in order])
    if groups > 1:
        same_member = [
            [g * HEADS_PER_GROUP + r for g in range(groups)] for r in range(HEADS_PER_GROUP)
        ]

    def over_seq(pieces, members):
        return lax.all_to_all(
            pieces, "seq", split_axis=0, concat_axis=0, tiled=True, axis_index_groups=members
        )

    def in_hbm(value):
        return pltpu.with_memory_space_constraint(value, pltpu.HBM)

    def to_groups(rows):
        pieces = rows.reshape(local_rows, groups, -1).transpose(1, 0, 2)
        return pieces if groups == 1 else over_seq(pieces, same_member)

    vmem = pl.BlockSpec(memory_space=pltpu.VMEM)
    hbm = pl.BlockSpec(memory_space=pltpu.HBM)
    smem = pl.BlockSpec(memory_space=pltpu.SMEM)
    queries = to_groups(queries)
    beside = from_quarter(queries, 1)
    small = (
        to_groups(new_token_keys),
        to_groups(new_token_values),
        block_ids,
        block_counts.reshape(1, blocks),
    )
    packed, queries = pl.pallas_call(
        pack_kernel,
        out_shape=[
            jax.ShapeDtypeStruct(
                (HEADS_PER_GROUP, groups, 2 * local_rows + LIST_ROWS, LANES), jnp.bfloat16
            ),
            jax.ShapeDtypeStruct(queries.shape, queries.dtype),
        ],
        in_specs=[hbm] * 5,
        out_specs=[vmem] * 2,
        scratch_shapes=[pltpu.VMEM(one.shape, one.dtype) for one in small]
        + [pltpu.VMEM((LIST_ROWS, LANES), jnp.float32), pltpu.SemaphoreType.DMA((5,))],
        compiler_params=pltpu.CompilerParams(vmem_limit_bytes=4 * MIB),
        cost_estimate=pl.CostEstimate(flops=0, bytes_accessed=12 * MIB, transcendentals=0),
        name="pack",
    )(*[in_hbm(one) for one in small + (queries,)])
    across = from_quarter(jnp.stack([queries, beside]), 2)
    near = lax.all_to_all(
        packed,
        ("seq", "ctx"),
        split_axis=0,
        concat_axis=0,
        tiled=True,
        axis_index_groups=same_group,
    )
    lists = near[:, :, 2 * local_rows].astype(jnp.int32)
    keys = cache_keys.reshape(-1, KROWS, head_size)
    keys = pl.pallas_call(
        fetch_kernel,
        out_shape=jax.ShapeDtypeStruct(keys.shape, keys.dtype),
        in_specs=[hbm],
        out_specs=vmem,
        scratch_shapes=[pltpu.SemaphoreType.DMA],
        compiler_params=pltpu.CompilerParams(vmem_limit_bytes=4 * MIB),
        cost_estimate=pl.CostEstimate(flops=0, bytes_accessed=4 * MIB, transcendentals=0),
        name="fetch",
    )(in_hbm(keys))
    tile = (TILE_QUERY_ROWS, KROWS)
    values = cache_values.reshape(-1, KROWS, head_size)
    partial = pl.pallas_call(
        attend_kernel,
        out_shape=[
            jax.ShapeDtypeStruct((groups, local_rows, width + LANES), jnp.bfloat16)
        ] * CTX,
        in_specs=[smem, vmem, vmem, hbm] + [vmem] * 3,
        out_specs=[vmem] * CTX,
        scratch_shapes=[
            pltpu.VMEM((HEADS_PER_GROUP, KQ + 1) + tile, jnp.float32),
            pltpu.VMEM((HEADS_PER_GROUP,) + tile, jnp.float32),
            pltpu.VMEM((HEADS_PER_GROUP,) + tile, jnp.float32),
            pltpu.VMEM(values.shape, values.dtype),
            pltpu.SemaphoreType.DMA,
        ],
        compiler_params=pltpu.CompilerParams(vmem_limit_bytes=24 * MIB),
        name="attend",
    )(lists, near, keys, in_hbm(values), queries, beside, across)
    partial = [from_quarter(partial[mask], mask) for mask in (3, 2, 1)] + [partial[0]]
    merged = pl.pallas_call(
        merge_kernel,
        out_shape=jax.ShapeDtypeStruct((groups, local_rows, width), jnp.bfloat16),
        in_specs=[vmem] * CTX,
        out_specs=vmem,
        compiler_params=pltpu.CompilerParams(vmem_limit_bytes=4 * MIB),
        name="merge",
    )(*partial)
    if groups > 1:
        merged = over_seq(merged, same_member)
    return merged.transpose(1, 0, 2).reshape(local_rows, groups * width)


def solution(mesh):
    return jax.shard_map(
        body,
        mesh=mesh,
        in_specs=(
            P(("seq", "ctx"), None),
            P(("seq", "ctx"), None),
            P(("seq", "ctx"), None),
            P("seq", "ctx", None),
            P("seq", "ctx", None),
            P("seq", None, "ctx", None),
            P("seq", None, "ctx"),
        ),
        out_specs=P(("seq", "ctx"), None),
        check_vma=False,
    )
```

```python
import math

import jax
import jax.numpy as jnp
from jax import lax
from jax.experimental import pallas as pl
from jax.experimental.pallas import tpu as pltpu
from jax.sharding import PartitionSpec as P

HEADS_PER_GROUP = 8
TILE_QUERY_ROWS = 64
KROWS = 128
KQ = 12
LANES = 128
CTX = 4
NEAR = 2 * KROWS // TILE_QUERY_ROWS
AT_ONCE = 4
MEETING_ORDERS = ((4, 0, 1, 2, 3, 5, 6, 7), (2, 0, 1, 3, 4, 5, 6, 7))
SLOTS_AT_ONCE = 4
LIST_ROWS = 8
COUNTS_AT = 16
MIB = 1024 * 1024
LOG2E = 1.4426950408889634


def nt(a, b):
    return lax.dot_general(a, b, (((1,), (1,)), ((), ())), preferred_element_type=jnp.float32)


def pack_kernel(*refs):
    sources, out_ref, targets = refs[:4], refs[4], refs[5:9]
    scratch, sems = refs[9:]
    copies = [
        pltpu.make_async_copy(source, target, sems.at[i])
        for i, (source, target) in enumerate(zip(sources, targets))
    ]
    for copy in copies:
        copy.start()
    keys, values, ids, counts = targets
    members, groups, _, _ = out_ref.shape
    local_rows = keys.shape[1]
    blocks = ids.shape[1]
    scratch[...] = jnp.zeros_like(scratch)
    for copy in copies:
        copy.wait()
    scratch[0:1, COUNTS_AT : COUNTS_AT + blocks] = counts[...].astype(jnp.float32)
    quarter = lax.axis_index("ctx")
    for member in range(members):
        place = place_of(member, quarter)
        for group in range(groups):
            block = group * members + member
            scratch[0:1, :KQ] = ids[0, block].astype(jnp.float32)
            out_ref[place, group, :local_rows] = keys[group]
            out_ref[place, group, local_rows : 2 * local_rows] = values[group]
            out_ref[place, group, 2 * local_rows :] = scratch[...].astype(jnp.bfloat16)


def place_of(member, quarter):
    odd = lax.rem(quarter, 2) == 1
    places = []
    for order in MEETING_ORDERS:
        if isinstance(member, int):
            places.append(jnp.int32(order.index(member)))
        else:
            places.append(sum(jnp.where(member == one, i, 0) for i, one in enumerate(order)))
    return jnp.where(odd, places[1], places[0])


def fetch_kernel(*refs):
    count = len(refs) // 2
    copies = [
        pltpu.make_async_copy(refs[i], refs[count + i], refs[-1].at[i]) for i in range(count)
    ]
    for copy in copies:
        copy.start()
    for copy in copies:
        copy.wait()


def attend_kernel(lists, near_ref, k_ref, v_hbm, *refs):
    q_refs, out_refs = refs[:CTX], refs[CTX : 2 * CTX]
    s_scr, m_scr, l_scr, v_ref, sem = refs[2 * CTX :]
    v_copy = pltpu.make_async_copy(v_hbm, v_ref, sem)
    v_copy.start()
    groups, local_rows, _ = q_refs[0].shape
    member = lax.rem(lax.axis_index("seq"), HEADS_PER_GROUP)
    quarter = lax.axis_index("ctx")
    rows = TILE_QUERY_ROWS
    head_size = k_ref.shape[2]
    scale = LOG2E / math.sqrt(head_size)
    shift, mask = local_rows.bit_length() - 1, local_rows - 1
    lane = lax.broadcasted_iota(jnp.int32, (rows, LANES), 1)
    sublane = lax.broadcasted_iota(jnp.int32, (rows, LANES), 0)

    def one_block(group):
        block = group * HEADS_PER_GROUP + member
        near = []
        for back in range(NEAR):
            place = jnp.maximum(group - jnp.where(member < back, 1, 0), 0)
            source = lax.rem(member - back + HEADS_PER_GROUP, HEADS_PER_GROUP)
            near.append(near_ref[place_of(source, quarter), place])
        near_k = jnp.concatenate([one[:local_rows] for one in near] * 2, axis=0)
        near_v = jnp.concatenate([one[local_rows : 2 * local_rows] for one in near] * 2, axis=0)
        position = (block - (lane >> shift)) * rows + quarter * local_rows + (lane & mask)
        token = block * rows + ((sublane >> shift) ^ quarter) * local_rows + (sublane & mask)
        oldest = jnp.maximum((block * rows // KROWS - 1) * KROWS, 0)
        near_ok = (lane < rows) & (position <= token) & (position >= oldest)

        def columns_of(head):
            return pl.ds(pl.multiple_of(head * head_size, LANES), head_size)

        def scores(head):
            place = place_of(head, quarter)
            count = lists[place, group, COUNTS_AT + block]
            q = jnp.concatenate([q_ref[group, :, columns_of(head)] for q_ref in q_refs], axis=0)
            s = jnp.where(near_ok, nt(q, near_k), -jnp.inf)
            s_scr[head, KQ] = s
            high = s
            for slot in range(0, KQ, SLOTS_AT_ONCE):
                keys = [k_ref[lists[place, group, slot + i]] for i in range(SLOTS_AT_ONCE)]
                several = nt(q, jnp.concatenate(keys, axis=0))
                for i in range(SLOTS_AT_ONCE):
                    s = several[:, i * KROWS : (i + 1) * KROWS]
                    s = jnp.where(slot + i < count, s, -jnp.inf)
                    s_scr[head, slot + i] = s
                    high = jnp.maximum(high, s)
            m_scr[head] = high

        def sums(head):
            place = place_of(head, quarter)
            top = m_scr[head]
            total = jnp.exp2(s_scr[head, KQ] * scale - top)
            acc = jnp.dot(total.astype(jnp.bfloat16), near_v, preferred_element_type=jnp.float32)
            for slot in range(0, KQ, SLOTS_AT_ONCE):
                weights = []
                for part in range(slot, slot + SLOTS_AT_ONCE):
                    p = jnp.exp2(s_scr[head, part] * scale - top)
                    total = total + p
                    weights.append(p.astype(jnp.bfloat16))
                values = [v_ref[lists[place, group, slot + i]] for i in range(SLOTS_AT_ONCE)]
                acc = acc + jnp.dot(
                    jnp.concatenate(weights, axis=1),
                    jnp.concatenate(values, axis=0),
                    preferred_element_type=jnp.float32,
                )
            acc = acc.astype(jnp.bfloat16)
            for part, out_ref in enumerate(out_refs):
                out_ref[group, :, columns_of(head)] = acc[
                    part * local_rows : (part + 1) * local_rows
                ]
            l_scr[head] = total

        def in_steps(step):
            def several(turn, carry):
                for i in range(AT_ONCE):
                    step(turn * AT_ONCE + i)
                return carry

            lax.fori_loop(0, HEADS_PER_GROUP // AT_ONCE, several, 0)

        in_steps(scores)
        for head in range(HEADS_PER_GROUP):
            top = jnp.max(m_scr[head], axis=1, keepdims=True) * scale
            m_scr[head] = jnp.broadcast_to(top, (rows, LANES))
        if groups == 1:
            v_copy.wait()
        else:
            pl.when(group == 0)(v_copy.wait)
        in_steps(sums)
        stats = jnp.zeros((rows, LANES), jnp.float32)
        for head in range(HEADS_PER_GROUP):
            total = jnp.sum(l_scr[head], axis=1, keepdims=True)
            stats = jnp.where(lane == head, m_scr[head], stats)
            stats = jnp.where(lane == head + HEADS_PER_GROUP, total, stats)
        packed = jnp.zeros((rows, LANES), jnp.float32)
        for step in range(3):
            part = stats.astype(jnp.bfloat16).astype(jnp.float32)
            stats = stats - part
            by = step * 2 * HEADS_PER_GROUP
            packed = packed + (pltpu.roll(part, by, 1) if by else part)
        packed = packed.astype(jnp.bfloat16)
        width = HEADS_PER_GROUP * head_size
        for part, out_ref in enumerate(out_refs):
            out_ref[group, :, width:] = packed[part * local_rows : (part + 1) * local_rows]

    if groups == 1:
        one_block(0)
    else:
        pl.loop(0, groups)(one_block)


def merge_kernel(*refs):
    in_refs, out_ref = refs[:-1], refs[-1]
    groups, local_rows, full = in_refs[0].shape
    width = full - LANES
    head_size = width // HEADS_PER_GROUP

    def one_block(group):
        stats = []
        for in_ref in in_refs:
            packed = in_ref[group, :, width:].astype(jnp.float32)
            one = packed
            for step in (1, 2):
                one = one + pltpu.roll(packed, LANES - step * 2 * HEADS_PER_GROUP, 1)
            stats.append(one)
        top = stats[0]
        for one in stats[1:]:
            top = jnp.maximum(top, one)
        factors = [jnp.exp2(one - top) for one in stats]
        total = jnp.zeros((local_rows, LANES), jnp.float32)
        for one, factor in zip(stats, factors):
            total = total + pltpu.roll(one, LANES - HEADS_PER_GROUP, 1) * factor
        inverse = 1.0 / total
        factors = [factor * inverse for factor in factors]
        for head in range(HEADS_PER_GROUP):
            columns = slice(head * head_size, (head + 1) * head_size)
            mixed = jnp.zeros((local_rows, head_size), jnp.float32)
            for in_ref, factor in zip(in_refs, factors):
                mixed = mixed + in_ref[group, :, columns].astype(jnp.float32) * (
                    factor[:, head : head + 1]
                )
            out_ref[group, :, columns] = mixed.astype(jnp.bfloat16)

    if groups == 1:
        one_block(0)
    else:
        pl.loop(0, groups)(one_block)


def from_quarter(value, mask):
    return lax.ppermute(value, "ctx", [(device, device ^ mask) for device in range(CTX)])


def body(
    queries, new_token_keys, new_token_values, cache_keys, cache_values, block_ids, block_counts
):
    seq_count = lax.axis_size("seq")
    head_size = cache_keys.shape[2]
    local_rows = queries.shape[0]
    blocks = block_ids.shape[1]
    groups = seq_count // HEADS_PER_GROUP
    width = HEADS_PER_GROUP * head_size
    assert lax.axis_size("ctx") == CTX and cache_keys.shape[0] == 1
    assert local_rows * CTX == TILE_QUERY_ROWS and blocks <= LANES - COUNTS_AT
    assert head_size == LANES and local_rows & (local_rows - 1) == 0
    same_group = []
    for g in range(groups):
        for c in range(CTX):
            order = MEETING_ORDERS[c % 2]
            same_group.append([(g * HEADS_PER_GROUP + member) * CTX + c for member in order])
    if groups > 1:
        same_member = [
            [g * HEADS_PER_GROUP + r for g in range(groups)] for r in range(HEADS_PER_GROUP)
        ]

    def over_seq(pieces, members):
        return lax.all_to_all(
            pieces, "seq", split_axis=0, concat_axis=0, tiled=True, axis_index_groups=members
        )

    def in_hbm(value):
        return pltpu.with_memory_space_constraint(value, pltpu.HBM)

    def to_groups(rows):
        pieces = rows.reshape(local_rows, groups, -1).transpose(1, 0, 2)
        return pieces if groups == 1 else over_seq(pieces, same_member)

    vmem = pl.BlockSpec(memory_space=pltpu.VMEM)
    hbm = pl.BlockSpec(memory_space=pltpu.HBM)
    smem = pl.BlockSpec(memory_space=pltpu.SMEM)
    queries = to_groups(queries)
    others = [from_quarter(queries, mask) for mask in range(1, CTX)]
    small = (
        to_groups(new_token_keys),
        to_groups(new_token_values),
        block_ids,
        block_counts.reshape(1, blocks),
    )
    packed = pl.pallas_call(
        pack_kernel,
        out_shape=jax.ShapeDtypeStruct(
            (HEADS_PER_GROUP, groups, 2 * local_rows + LIST_ROWS, LANES), jnp.bfloat16
        ),
        in_specs=[hbm] * 4,
        out_specs=vmem,
        scratch_shapes=[pltpu.VMEM(one.shape, one.dtype) for one in small]
        + [pltpu.VMEM((LIST_ROWS, LANES), jnp.float32), pltpu.SemaphoreType.DMA((4,))],
        compiler_params=pltpu.CompilerParams(vmem_limit_bytes=4 * MIB),
        cost_estimate=pl.CostEstimate(flops=0, bytes_accessed=12 * MIB, transcendentals=0),
        name="pack",
    )(*[in_hbm(one) for one in small])
    large = (queries, cache_keys.reshape(-1, KROWS, head_size))
    queries, keys = pl.pallas_call(
        fetch_kernel,
        out_shape=[jax.ShapeDtypeStruct(one.shape, one.dtype) for one in large],
        in_specs=[hbm] * 2,
        out_specs=[vmem] * 2,
        scratch_shapes=[pltpu.SemaphoreType.DMA((2,))],
        compiler_params=pltpu.CompilerParams(vmem_limit_bytes=4 * MIB),
        cost_estimate=pl.CostEstimate(flops=0, bytes_accessed=4 * MIB, transcendentals=0),
        name="fetch",
    )(*[in_hbm(one) for one in large])
    near = lax.all_to_all(
        packed,
        ("seq", "ctx"),
        split_axis=0,
        concat_axis=0,
        tiled=True,
        axis_index_groups=same_group,
    )
    lists = near[:, :, 2 * local_rows].astype(jnp.int32)
    tile = (TILE_QUERY_ROWS, KROWS)
    values = cache_values.reshape(-1, KROWS, head_size)
    partial = pl.pallas_call(
        attend_kernel,
        out_shape=[
            jax.ShapeDtypeStruct((groups, local_rows, width + LANES), jnp.bfloat16)
        ] * CTX,
        in_specs=[smem, vmem, vmem, hbm] + [vmem] * CTX,
        out_specs=[vmem] * CTX,
        scratch_shapes=[
            pltpu.VMEM((HEADS_PER_GROUP, KQ + 1) + tile, jnp.float32),
            pltpu.VMEM((HEADS_PER_GROUP,) + tile, jnp.float32),
            pltpu.VMEM((HEADS_PER_GROUP,) + tile, jnp.float32),
            pltpu.VMEM(values.shape, values.dtype),
            pltpu.SemaphoreType.DMA,
        ],
        compiler_params=pltpu.CompilerParams(vmem_limit_bytes=24 * MIB),
        name="attend",
    )(lists, near, keys, in_hbm(values), queries, *others)
    partial = [from_quarter(partial[mask], mask) for mask in (3, 2, 1)] + [partial[0]]
    merged = pl.pallas_call(
        merge_kernel,
        out_shape=jax.ShapeDtypeStruct((groups, local_rows, width), jnp.bfloat16),
        in_specs=[vmem] * CTX,
        out_specs=vmem,
        compiler_params=pltpu.CompilerParams(vmem_limit_bytes=4 * MIB),
        name="merge",
    )(*partial)
    if groups > 1:
        merged = over_seq(merged, same_member)
    return merged.transpose(1, 0, 2).reshape(local_rows, groups * width)


def solution(mesh):
    return jax.shard_map(
        body,
        mesh=mesh,
        in_specs=(
            P(("seq", "ctx"), None),
            P(("seq", "ctx"), None),
            P(("seq", "ctx"), None),
            P("seq", "ctx", None),
            P("seq", "ctx", None),
            P("seq", None, "ctx", None),
            P("seq", None, "ctx"),
        ),
        out_specs=P(("seq", "ctx"), None),
        check_vma=False,
    )
```

```python
import math

import jax
import jax.numpy as jnp
from jax import lax
from jax.experimental import pallas as pl
from jax.experimental.pallas import tpu as pltpu
from jax.sharding import PartitionSpec as P

HEADS_PER_GROUP = 8
TILE_QUERY_ROWS = 64
KROWS = 128
KQ = 12
LANES = 128
CTX = 4
NEAR = 2 * KROWS // TILE_QUERY_ROWS
AT_ONCE = 4
SLOTS_AT_ONCE = 4
LIST_ROWS = 8
COUNTS_AT = 16
MIB = 1024 * 1024
LOG2E = 1.4426950408889634


def nt(a, b):
    return lax.dot_general(a, b, (((1,), (1,)), ((), ())), preferred_element_type=jnp.float32)


def pack_kernel(*refs):
    sources, out_ref, targets = refs[:4], refs[4], refs[5:9]
    scratch, sems = refs[9:]
    copies = [
        pltpu.make_async_copy(source, target, sems.at[i])
        for i, (source, target) in enumerate(zip(sources, targets))
    ]
    for copy in copies:
        copy.start()
    keys, values, ids, counts = targets
    members, groups, _, _ = out_ref.shape
    local_rows = keys.shape[1]
    blocks = ids.shape[1]
    scratch[...] = jnp.zeros_like(scratch)
    for copy in copies:
        copy.wait()
    scratch[0:1, COUNTS_AT : COUNTS_AT + blocks] = counts[...].astype(jnp.float32)
    for member in range(members):
        for group in range(groups):
            block = group * members + member
            scratch[0:1, :KQ] = ids[0, block].astype(jnp.float32)
            out_ref[place_of(member), group, :local_rows] = keys[group]
            out_ref[place_of(member), group, local_rows : 2 * local_rows] = values[group]
            out_ref[place_of(member), group, 2 * local_rows :] = scratch[...].astype(jnp.bfloat16)


def place_of(member):
    half = HEADS_PER_GROUP // 2
    if isinstance(member, int):
        return 2 * (member - half) if member >= half else HEADS_PER_GROUP - 1 - 2 * member
    return jnp.where(member >= half, 2 * (member - half), HEADS_PER_GROUP - 1 - 2 * member)


def fetch_kernel(*refs):
    count = len(refs) // 2
    copies = [
        pltpu.make_async_copy(refs[i], refs[count + i], refs[-1].at[i]) for i in range(count)
    ]
    for copy in copies:
        copy.start()
    for copy in copies:
        copy.wait()


def attend_kernel(lists, near_ref, k_ref, v_hbm, *refs):
    q_refs, out_refs = refs[:CTX], refs[CTX : 2 * CTX]
    s_scr, m_scr, v_ref, sem = refs[2 * CTX :]
    v_copy = pltpu.make_async_copy(v_hbm, v_ref, sem)
    v_copy.start()
    groups, local_rows, _ = q_refs[0].shape
    member = lax.rem(lax.axis_index("seq"), HEADS_PER_GROUP)
    quarter = lax.axis_index("ctx")
    rows = TILE_QUERY_ROWS
    head_size = k_ref.shape[2]
    scale = LOG2E / math.sqrt(head_size)
    shift, mask = local_rows.bit_length() - 1, local_rows - 1
    lane = lax.broadcasted_iota(jnp.int32, (rows, LANES), 1)
    sublane = lax.broadcasted_iota(jnp.int32, (rows, LANES), 0)

    def one_block(group):
        block = group * HEADS_PER_GROUP + member
        near = []
        for back in range(NEAR):
            place = jnp.maximum(group - jnp.where(member < back, 1, 0), 0)
            near.append(near_ref[place_of(lax.rem(member - back + HEADS_PER_GROUP, HEADS_PER_GROUP)), place])
        near_k = jnp.concatenate([one[:local_rows] for one in near] * 2, axis=0)
        near_v = jnp.concatenate([one[local_rows : 2 * local_rows] for one in near] * 2, axis=0)
        position = (block - (lane >> shift)) * rows + quarter * local_rows + (lane & mask)
        token = block * rows + ((sublane >> shift) ^ quarter) * local_rows + (sublane & mask)
        oldest = jnp.maximum((block * rows // KROWS - 1) * KROWS, 0)
        near_ok = (lane < rows) & (position <= token) & (position >= oldest)

        def columns_of(head):
            return pl.ds(pl.multiple_of(head * head_size, LANES), head_size)

        def scores(head):
            count = lists[place_of(head), group, COUNTS_AT + block]
            q = jnp.concatenate([q_ref[group, :, columns_of(head)] for q_ref in q_refs], axis=0)
            s = jnp.where(near_ok, nt(q, near_k), -jnp.inf)
            s_scr[head, KQ] = s
            high = s
            for slot in range(0, KQ, SLOTS_AT_ONCE):
                keys = [k_ref[lists[place_of(head), group, slot + i]] for i in range(SLOTS_AT_ONCE)]
                several = nt(q, jnp.concatenate(keys, axis=0))
                for i in range(SLOTS_AT_ONCE):
                    s = several[:, i * KROWS : (i + 1) * KROWS]
                    s = jnp.where(slot + i < count, s, -jnp.inf)
                    s_scr[head, slot + i] = s
                    high = jnp.maximum(high, s)
            m_scr[head] = high

        def sums(head, stats):
            top = m_scr[head]
            total = jnp.exp2(s_scr[head, KQ] * scale - top)
            acc = jnp.dot(total.astype(jnp.bfloat16), near_v, preferred_element_type=jnp.float32)
            for slot in range(0, KQ, SLOTS_AT_ONCE):
                weights = []
                for part in range(slot, slot + SLOTS_AT_ONCE):
                    p = jnp.exp2(s_scr[head, part] * scale - top)
                    total = total + p
                    weights.append(p.astype(jnp.bfloat16))
                values = [v_ref[lists[place_of(head), group, slot + i]] for i in range(SLOTS_AT_ONCE)]
                acc = acc + jnp.dot(
                    jnp.concatenate(weights, axis=1),
                    jnp.concatenate(values, axis=0),
                    preferred_element_type=jnp.float32,
                )
            acc = acc.astype(jnp.bfloat16)
            for part, out_ref in enumerate(out_refs):
                out_ref[group, :, columns_of(head)] = acc[
                    part * local_rows : (part + 1) * local_rows
                ]
            total = jnp.sum(total, axis=1, keepdims=True)
            stats = jnp.where(lane == head, top, stats)
            return jnp.where(lane == head + HEADS_PER_GROUP, total, stats)

        def score_step(turn, carry):
            for i in range(AT_ONCE):
                scores(turn * AT_ONCE + i)
            return carry

        def sum_step(turn, stats):
            for i in range(AT_ONCE):
                stats = sums(turn * AT_ONCE + i, stats)
            return stats

        steps = HEADS_PER_GROUP // AT_ONCE
        lax.fori_loop(0, steps, score_step, 0)
        for head in range(HEADS_PER_GROUP):
            top = jnp.max(m_scr[head], axis=1, keepdims=True) * scale
            m_scr[head] = jnp.broadcast_to(top, (rows, LANES))
        if groups == 1:
            v_copy.wait()
        else:
            pl.when(group == 0)(v_copy.wait)
        stats = lax.fori_loop(0, steps, sum_step, jnp.zeros((rows, LANES), jnp.float32))
        packed = jnp.zeros((rows, LANES), jnp.float32)
        for step in range(3):
            part = stats.astype(jnp.bfloat16).astype(jnp.float32)
            stats = stats - part
            by = step * 2 * HEADS_PER_GROUP
            packed = packed + (pltpu.roll(part, by, 1) if by else part)
        packed = packed.astype(jnp.bfloat16)
        width = HEADS_PER_GROUP * head_size
        for part, out_ref in enumerate(out_refs):
            out_ref[group, :, width:] = packed[part * local_rows : (part + 1) * local_rows]

    if groups == 1:
        one_block(0)
    else:
        pl.loop(0, groups)(one_block)


def merge_kernel(*refs):
    in_refs, out_ref = refs[:-1], refs[-1]
    groups, local_rows, full = in_refs[0].shape
    width = full - LANES
    head_size = width // HEADS_PER_GROUP

    def one_block(group):
        stats = []
        for in_ref in in_refs:
            packed = in_ref[group, :, width:].astype(jnp.float32)
            one = packed
            for step in (1, 2):
                one = one + pltpu.roll(packed, LANES - step * 2 * HEADS_PER_GROUP, 1)
            stats.append(one)
        top = stats[0]
        for one in stats[1:]:
            top = jnp.maximum(top, one)
        factors = [jnp.exp2(one - top) for one in stats]
        total = jnp.zeros((local_rows, LANES), jnp.float32)
        for one, factor in zip(stats, factors):
            total = total + pltpu.roll(one, LANES - HEADS_PER_GROUP, 1) * factor
        inverse = 1.0 / total
        factors = [factor * inverse for factor in factors]
        for head in range(HEADS_PER_GROUP):
            columns = slice(head * head_size, (head + 1) * head_size)
            mixed = jnp.zeros((local_rows, head_size), jnp.float32)
            for in_ref, factor in zip(in_refs, factors):
                mixed = mixed + in_ref[group, :, columns].astype(jnp.float32) * (
                    factor[:, head : head + 1]
                )
            out_ref[group, :, columns] = mixed.astype(jnp.bfloat16)

    if groups == 1:
        one_block(0)
    else:
        pl.loop(0, groups)(one_block)


def from_quarter(value, mask):
    return lax.ppermute(value, "ctx", [(device, device ^ mask) for device in range(CTX)])


def body(
    queries, new_token_keys, new_token_values, cache_keys, cache_values, block_ids, block_counts
):
    seq_count = lax.axis_size("seq")
    head_size = cache_keys.shape[2]
    local_rows = queries.shape[0]
    blocks = block_ids.shape[1]
    groups = seq_count // HEADS_PER_GROUP
    width = HEADS_PER_GROUP * head_size
    assert lax.axis_size("ctx") == CTX and cache_keys.shape[0] == 1
    assert local_rows * CTX == TILE_QUERY_ROWS and blocks <= LANES - COUNTS_AT
    assert head_size == LANES and local_rows & (local_rows - 1) == 0
    order = sorted(range(HEADS_PER_GROUP), key=place_of)
    same_group = [[g * HEADS_PER_GROUP + member for member in order] for g in range(groups)]
    if groups > 1:
        same_member = [
            [g * HEADS_PER_GROUP + r for g in range(groups)] for r in range(HEADS_PER_GROUP)
        ]

    def over_seq(pieces, members):
        return lax.all_to_all(
            pieces, "seq", split_axis=0, concat_axis=0, tiled=True, axis_index_groups=members
        )

    def in_hbm(value):
        return pltpu.with_memory_space_constraint(value, pltpu.HBM)

    def to_groups(rows):
        pieces = rows.reshape(local_rows, groups, -1).transpose(1, 0, 2)
        return pieces if groups == 1 else over_seq(pieces, same_member)

    vmem = pl.BlockSpec(memory_space=pltpu.VMEM)
    hbm = pl.BlockSpec(memory_space=pltpu.HBM)
    smem = pl.BlockSpec(memory_space=pltpu.SMEM)
    queries = to_groups(queries)
    others = [from_quarter(queries, mask) for mask in range(1, CTX)]
    small = (
        to_groups(new_token_keys),
        to_groups(new_token_values),
        block_ids,
        block_counts.reshape(1, blocks),
    )
    packed = pl.pallas_call(
        pack_kernel,
        out_shape=jax.ShapeDtypeStruct(
            (HEADS_PER_GROUP, groups, 2 * local_rows + LIST_ROWS, LANES), jnp.bfloat16
        ),
        in_specs=[hbm] * 4,
        out_specs=vmem,
        scratch_shapes=[pltpu.VMEM(one.shape, one.dtype) for one in small]
        + [pltpu.VMEM((LIST_ROWS, LANES), jnp.float32), pltpu.SemaphoreType.DMA((4,))],
        compiler_params=pltpu.CompilerParams(vmem_limit_bytes=4 * MIB),
        cost_estimate=pl.CostEstimate(flops=0, bytes_accessed=12 * MIB, transcendentals=0),
        name="pack",
    )(*[in_hbm(one) for one in small])
    large = (queries, cache_keys.reshape(-1, KROWS, head_size))
    queries, keys = pl.pallas_call(
        fetch_kernel,
        out_shape=[jax.ShapeDtypeStruct(one.shape, one.dtype) for one in large],
        in_specs=[hbm] * 2,
        out_specs=[vmem] * 2,
        scratch_shapes=[pltpu.SemaphoreType.DMA((2,))],
        compiler_params=pltpu.CompilerParams(vmem_limit_bytes=4 * MIB),
        cost_estimate=pl.CostEstimate(flops=0, bytes_accessed=4 * MIB, transcendentals=0),
        name="fetch",
    )(*[in_hbm(one) for one in large])
    near = over_seq(packed, same_group)
    lists = near[:, :, 2 * local_rows].astype(jnp.int32)
    tile = (TILE_QUERY_ROWS, KROWS)
    values = cache_values.reshape(-1, KROWS, head_size)
    partial = pl.pallas_call(
        attend_kernel,
        out_shape=[
            jax.ShapeDtypeStruct((groups, local_rows, width + LANES), jnp.bfloat16)
        ] * CTX,
        in_specs=[smem, vmem, vmem, hbm] + [vmem] * CTX,
        out_specs=[vmem] * CTX,
        scratch_shapes=[
            pltpu.VMEM((HEADS_PER_GROUP, KQ + 1) + tile, jnp.float32),
            pltpu.VMEM((HEADS_PER_GROUP,) + tile, jnp.float32),
            pltpu.VMEM(values.shape, values.dtype),
            pltpu.SemaphoreType.DMA,
        ],
        compiler_params=pltpu.CompilerParams(vmem_limit_bytes=24 * MIB),
        name="attend",
    )(lists, near, keys, in_hbm(values), queries, *others)
    partial = [from_quarter(partial[mask], mask) for mask in (2, 3, 1)] + [partial[0]]
    merged = pl.pallas_call(
        merge_kernel,
        out_shape=jax.ShapeDtypeStruct((groups, local_rows, width), jnp.bfloat16),
        in_specs=[vmem] * CTX,
        out_specs=vmem,
        compiler_params=pltpu.CompilerParams(vmem_limit_bytes=4 * MIB),
        name="merge",
    )(*partial)
    if groups > 1:
        merged = over_seq(merged, same_member)
    return merged.transpose(1, 0, 2).reshape(local_rows, groups * width)


def solution(mesh):
    return jax.shard_map(
        body,
        mesh=mesh,
        in_specs=(
            P(("seq", "ctx"), None),
            P(("seq", "ctx"), None),
            P(("seq", "ctx"), None),
            P("seq", "ctx", None),
            P("seq", "ctx", None),
            P("seq", None, "ctx", None),
            P("seq", None, "ctx"),
        ),
        out_specs=P(("seq", "ctx"), None),
        check_vma=False,
    )
```

```python
import math

import jax
import jax.numpy as jnp
from jax import lax
from jax.experimental import pallas as pl
from jax.experimental.pallas import tpu as pltpu
from jax.sharding import PartitionSpec as P

HEADS_PER_GROUP = 8
TILE_QUERY_ROWS = 64
KROWS = 128
KQ = 12
LANES = 128
CTX = 4
NEAR = 2 * KROWS // TILE_QUERY_ROWS
AT_ONCE = 4
SLOTS_AT_ONCE = 4
LIST_ROWS = 8
COUNTS_AT = 16
MIB = 1024 * 1024
LOG2E = 1.4426950408889634


def nt(a, b):
    return lax.dot_general(a, b, (((1,), (1,)), ((), ())), preferred_element_type=jnp.float32)


def pack_kernel(*refs):
    sources, out_ref, targets = refs[:4], refs[4], refs[5:9]
    scratch, sems = refs[9:]
    copies = [
        pltpu.make_async_copy(source, target, sems.at[i])
        for i, (source, target) in enumerate(zip(sources, targets))
    ]
    for copy in copies:
        copy.start()
    keys, values, ids, counts = targets
    members, groups, _, _ = out_ref.shape
    local_rows = keys.shape[1]
    blocks = ids.shape[1]
    scratch[...] = jnp.zeros_like(scratch)
    for copy in copies:
        copy.wait()
    scratch[0:1, COUNTS_AT : COUNTS_AT + blocks] = counts[...].astype(jnp.float32)
    for member in range(members):
        for group in range(groups):
            block = group * members + member
            scratch[0:1, :KQ] = ids[0, block].astype(jnp.float32)
            out_ref[place_of(member), group, :local_rows] = keys[group]
            out_ref[place_of(member), group, local_rows : 2 * local_rows] = values[group]
            out_ref[place_of(member), group, 2 * local_rows :] = scratch[...].astype(jnp.bfloat16)


def place_of(member):
    half = HEADS_PER_GROUP // 2
    if isinstance(member, int):
        return 2 * (member - half) if member >= half else HEADS_PER_GROUP - 1 - 2 * member
    return jnp.where(member >= half, 2 * (member - half), HEADS_PER_GROUP - 1 - 2 * member)


def fetch_kernel(*refs):
    count = len(refs) // 2
    copies = [
        pltpu.make_async_copy(refs[i], refs[count + i], refs[-1].at[i]) for i in range(count)
    ]
    for copy in copies:
        copy.start()
    for copy in copies:
        copy.wait()


def attend_kernel(lists, near_ref, k_ref, v_hbm, *refs):
    q_refs, out_refs = refs[:CTX], refs[CTX : 2 * CTX]
    s_scr, m_scr, v_ref, sem = refs[2 * CTX :]
    v_copy = pltpu.make_async_copy(v_hbm, v_ref, sem)
    v_copy.start()
    groups, local_rows, _ = q_refs[0].shape
    member = lax.rem(lax.axis_index("seq"), HEADS_PER_GROUP)
    quarter = lax.axis_index("ctx")
    rows = TILE_QUERY_ROWS
    head_size = k_ref.shape[2]
    scale = LOG2E / math.sqrt(head_size)
    shift, mask = local_rows.bit_length() - 1, local_rows - 1
    lane = lax.broadcasted_iota(jnp.int32, (rows, LANES), 1)
    sublane = lax.broadcasted_iota(jnp.int32, (rows, LANES), 0)

    def one_block(group):
        block = group * HEADS_PER_GROUP + member
        near = []
        for back in range(NEAR):
            place = jnp.maximum(group - jnp.where(member < back, 1, 0), 0)
            near.append(near_ref[place_of(lax.rem(member - back + HEADS_PER_GROUP, HEADS_PER_GROUP)), place])
        near_k = jnp.concatenate([one[:local_rows] for one in near] * 2, axis=0)
        near_v = jnp.concatenate([one[local_rows : 2 * local_rows] for one in near] * 2, axis=0)
        position = (block - (lane >> shift)) * rows + quarter * local_rows + (lane & mask)
        token = block * rows + ((sublane >> shift) ^ quarter) * local_rows + (sublane & mask)
        oldest = jnp.maximum((block * rows // KROWS - 1) * KROWS, 0)
        near_ok = (lane < rows) & (position <= token) & (position >= oldest)

        def columns_of(head):
            return pl.ds(pl.multiple_of(head * head_size, LANES), head_size)

        def scores(head):
            count = lists[place_of(head), group, COUNTS_AT + block]
            q = jnp.concatenate([q_ref[group, :, columns_of(head)] for q_ref in q_refs], axis=0)
            s = jnp.where(near_ok, nt(q, near_k), -jnp.inf)
            s_scr[head, KQ] = s
            high = s
            for slot in range(0, KQ, SLOTS_AT_ONCE):
                keys = [k_ref[lists[place_of(head), group, slot + i]] for i in range(SLOTS_AT_ONCE)]
                several = nt(q, jnp.concatenate(keys, axis=0))
                for i in range(SLOTS_AT_ONCE):
                    s = several[:, i * KROWS : (i + 1) * KROWS]
                    s = jnp.where(slot + i < count, s, -jnp.inf)
                    s_scr[head, slot + i] = s
                    high = jnp.maximum(high, s)
            top = jnp.max(high, axis=1, keepdims=True) * scale
            m_scr[head] = jnp.broadcast_to(top, (rows, LANES))

        def sums(head, stats):
            top = m_scr[head]
            total = jnp.exp2(s_scr[head, KQ] * scale - top)
            acc = jnp.dot(total.astype(jnp.bfloat16), near_v, preferred_element_type=jnp.float32)
            for slot in range(0, KQ, SLOTS_AT_ONCE):
                weights = []
                for part in range(slot, slot + SLOTS_AT_ONCE):
                    p = jnp.exp2(s_scr[head, part] * scale - top)
                    total = total + p
                    weights.append(p.astype(jnp.bfloat16))
                values = [v_ref[lists[place_of(head), group, slot + i]] for i in range(SLOTS_AT_ONCE)]
                acc = acc + jnp.dot(
                    jnp.concatenate(weights, axis=1),
                    jnp.concatenate(values, axis=0),
                    preferred_element_type=jnp.float32,
                )
            acc = acc.astype(jnp.bfloat16)
            for part, out_ref in enumerate(out_refs):
                out_ref[group, :, columns_of(head)] = acc[
                    part * local_rows : (part + 1) * local_rows
                ]
            total = jnp.sum(total, axis=1, keepdims=True)
            stats = jnp.where(lane == head, top, stats)
            return jnp.where(lane == head + HEADS_PER_GROUP, total, stats)

        def score_step(turn, carry):
            for i in range(AT_ONCE):
                scores(turn * AT_ONCE + i)
            return carry

        def sum_step(turn, stats):
            for i in range(AT_ONCE):
                stats = sums(turn * AT_ONCE + i, stats)
            return stats

        steps = HEADS_PER_GROUP // AT_ONCE
        lax.fori_loop(0, steps, score_step, 0)
        if groups == 1:
            v_copy.wait()
        else:
            pl.when(group == 0)(v_copy.wait)
        stats = lax.fori_loop(0, steps, sum_step, jnp.zeros((rows, LANES), jnp.float32))
        packed = jnp.zeros((rows, LANES), jnp.float32)
        for step in range(3):
            part = stats.astype(jnp.bfloat16).astype(jnp.float32)
            stats = stats - part
            by = step * 2 * HEADS_PER_GROUP
            packed = packed + (pltpu.roll(part, by, 1) if by else part)
        packed = packed.astype(jnp.bfloat16)
        width = HEADS_PER_GROUP * head_size
        for part, out_ref in enumerate(out_refs):
            out_ref[group, :, width:] = packed[part * local_rows : (part + 1) * local_rows]

    if groups == 1:
        one_block(0)
    else:
        pl.loop(0, groups)(one_block)


def merge_kernel(*refs):
    in_refs, out_ref = refs[:-1], refs[-1]
    groups, local_rows, full = in_refs[0].shape
    width = full - LANES
    head_size = width // HEADS_PER_GROUP

    def one_block(group):
        stats = []
        for in_ref in in_refs:
            packed = in_ref[group, :, width:].astype(jnp.float32)
            one = packed
            for step in (1, 2):
                one = one + pltpu.roll(packed, LANES - step * 2 * HEADS_PER_GROUP, 1)
            stats.append(one)
        top = stats[0]
        for one in stats[1:]:
            top = jnp.maximum(top, one)
        factors = [jnp.exp2(one - top) for one in stats]
        total = jnp.zeros((local_rows, LANES), jnp.float32)
        for one, factor in zip(stats, factors):
            total = total + pltpu.roll(one, LANES - HEADS_PER_GROUP, 1) * factor
        inverse = 1.0 / total
        factors = [factor * inverse for factor in factors]
        for head in range(HEADS_PER_GROUP):
            columns = slice(head * head_size, (head + 1) * head_size)
            mixed = jnp.zeros((local_rows, head_size), jnp.float32)
            for in_ref, factor in zip(in_refs, factors):
                mixed = mixed + in_ref[group, :, columns].astype(jnp.float32) * (
                    factor[:, head : head + 1]
                )
            out_ref[group, :, columns] = mixed.astype(jnp.bfloat16)

    if groups == 1:
        one_block(0)
    else:
        pl.loop(0, groups)(one_block)


def from_quarter(value, mask):
    return lax.ppermute(value, "ctx", [(device, device ^ mask) for device in range(CTX)])


def body(
    queries, new_token_keys, new_token_values, cache_keys, cache_values, block_ids, block_counts
):
    seq_count = lax.axis_size("seq")
    head_size = cache_keys.shape[2]
    local_rows = queries.shape[0]
    blocks = block_ids.shape[1]
    groups = seq_count // HEADS_PER_GROUP
    width = HEADS_PER_GROUP * head_size
    assert lax.axis_size("ctx") == CTX and cache_keys.shape[0] == 1
    assert local_rows * CTX == TILE_QUERY_ROWS and blocks <= LANES - COUNTS_AT
    assert head_size == LANES and local_rows & (local_rows - 1) == 0
    order = sorted(range(HEADS_PER_GROUP), key=place_of)
    same_group = [[g * HEADS_PER_GROUP + member for member in order] for g in range(groups)]
    if groups > 1:
        same_member = [
            [g * HEADS_PER_GROUP + r for g in range(groups)] for r in range(HEADS_PER_GROUP)
        ]

    def over_seq(pieces, members):
        return lax.all_to_all(
            pieces, "seq", split_axis=0, concat_axis=0, tiled=True, axis_index_groups=members
        )

    def in_hbm(value):
        return pltpu.with_memory_space_constraint(value, pltpu.HBM)

    def to_groups(rows):
        pieces = rows.reshape(local_rows, groups, -1).transpose(1, 0, 2)
        return pieces if groups == 1 else over_seq(pieces, same_member)

    vmem = pl.BlockSpec(memory_space=pltpu.VMEM)
    hbm = pl.BlockSpec(memory_space=pltpu.HBM)
    smem = pl.BlockSpec(memory_space=pltpu.SMEM)
    queries = to_groups(queries)
    others = [from_quarter(queries, mask) for mask in range(1, CTX)]
    small = (
        to_groups(new_token_keys),
        to_groups(new_token_values),
        block_ids,
        block_counts.reshape(1, blocks),
    )
    packed = pl.pallas_call(
        pack_kernel,
        out_shape=jax.ShapeDtypeStruct(
            (HEADS_PER_GROUP, groups, 2 * local_rows + LIST_ROWS, LANES), jnp.bfloat16
        ),
        in_specs=[hbm] * 4,
        out_specs=vmem,
        scratch_shapes=[pltpu.VMEM(one.shape, one.dtype) for one in small]
        + [pltpu.VMEM((LIST_ROWS, LANES), jnp.float32), pltpu.SemaphoreType.DMA((4,))],
        compiler_params=pltpu.CompilerParams(vmem_limit_bytes=4 * MIB),
        cost_estimate=pl.CostEstimate(flops=0, bytes_accessed=12 * MIB, transcendentals=0),
        name="pack",
    )(*[in_hbm(one) for one in small])
    large = (queries, cache_keys.reshape(-1, KROWS, head_size))
    queries, keys = pl.pallas_call(
        fetch_kernel,
        out_shape=[jax.ShapeDtypeStruct(one.shape, one.dtype) for one in large],
        in_specs=[hbm] * 2,
        out_specs=[vmem] * 2,
        scratch_shapes=[pltpu.SemaphoreType.DMA((2,))],
        compiler_params=pltpu.CompilerParams(vmem_limit_bytes=4 * MIB),
        cost_estimate=pl.CostEstimate(flops=0, bytes_accessed=4 * MIB, transcendentals=0),
        name="fetch",
    )(*[in_hbm(one) for one in large])
    near = over_seq(packed, same_group)
    lists = near[:, :, 2 * local_rows].astype(jnp.int32)
    tile = (TILE_QUERY_ROWS, KROWS)
    values = cache_values.reshape(-1, KROWS, head_size)
    partial = pl.pallas_call(
        attend_kernel,
        out_shape=[
            jax.ShapeDtypeStruct((groups, local_rows, width + LANES), jnp.bfloat16)
        ] * CTX,
        in_specs=[smem, vmem, vmem, hbm] + [vmem] * CTX,
        out_specs=[vmem] * CTX,
        scratch_shapes=[
            pltpu.VMEM((HEADS_PER_GROUP, KQ + 1) + tile, jnp.float32),
            pltpu.VMEM((HEADS_PER_GROUP,) + tile, jnp.float32),
            pltpu.VMEM(values.shape, values.dtype),
            pltpu.SemaphoreType.DMA,
        ],
        compiler_params=pltpu.CompilerParams(vmem_limit_bytes=24 * MIB),
        name="attend",
    )(lists, near, keys, in_hbm(values), queries, *others)
    partial = [from_quarter(partial[mask], mask) for mask in (2, 3, 1)] + [partial[0]]
    merged = pl.pallas_call(
        merge_kernel,
        out_shape=jax.ShapeDtypeStruct((groups, local_rows, width), jnp.bfloat16),
        in_specs=[vmem] * CTX,
        out_specs=vmem,
        compiler_params=pltpu.CompilerParams(vmem_limit_bytes=4 * MIB),
        name="merge",
    )(*partial)
    if groups > 1:
        merged = over_seq(merged, same_member)
    return merged.transpose(1, 0, 2).reshape(local_rows, groups * width)


def solution(mesh):
    return jax.shard_map(
        body,
        mesh=mesh,
        in_specs=(
            P(("seq", "ctx"), None),
            P(("seq", "ctx"), None),
            P(("seq", "ctx"), None),
            P("seq", "ctx", None),
            P("seq", "ctx", None),
            P("seq", None, "ctx", None),
            P("seq", None, "ctx"),
        ),
        out_specs=P(("seq", "ctx"), None),
        check_vma=False,
    )
```

```python
import math

import jax
import jax.numpy as jnp
from jax import lax
from jax.experimental import pallas as pl
from jax.experimental.pallas import tpu as pltpu
from jax.sharding import PartitionSpec as P

HEADS_PER_GROUP = 8
TILE_QUERY_ROWS = 64
KROWS = 128
KQ = 12
LANES = 128
CTX = 4
NEAR = 2 * KROWS // TILE_QUERY_ROWS
AT_ONCE = 4
SLOTS_AT_ONCE = 4
LIST_ROWS = 8
COUNTS_AT = 16
MIB = 1024 * 1024
LOG2E = 1.4426950408889634


def nt(a, b):
    return lax.dot_general(a, b, (((1,), (1,)), ((), ())), preferred_element_type=jnp.float32)


def pack_kernel(*refs):
    sources, out_ref, targets = refs[:4], refs[4], refs[5:9]
    scratch, sems = refs[9:]
    copies = [
        pltpu.make_async_copy(source, target, sems.at[i])
        for i, (source, target) in enumerate(zip(sources, targets))
    ]
    for copy in copies:
        copy.start()
    keys, values, ids, counts = targets
    members, groups, _, _ = out_ref.shape
    local_rows = keys.shape[1]
    blocks = ids.shape[1]
    scratch[...] = jnp.zeros_like(scratch)
    for copy in copies:
        copy.wait()
    scratch[0:1, COUNTS_AT : COUNTS_AT + blocks] = counts[...].astype(jnp.float32)
    for member in range(members):
        for group in range(groups):
            block = group * members + member
            scratch[0:1, :KQ] = ids[0, block].astype(jnp.float32)
            out_ref[place_of(member), group, :local_rows] = keys[group]
            out_ref[place_of(member), group, local_rows : 2 * local_rows] = values[group]
            out_ref[place_of(member), group, 2 * local_rows :] = scratch[...].astype(jnp.bfloat16)


def place_of(member):
    half = HEADS_PER_GROUP // 2
    if isinstance(member, int):
        return 2 * (member - half) if member >= half else HEADS_PER_GROUP - 1 - 2 * member
    return jnp.where(member >= half, 2 * (member - half), HEADS_PER_GROUP - 1 - 2 * member)


def fetch_kernel(*refs):
    count = len(refs) // 2
    copies = [
        pltpu.make_async_copy(refs[i], refs[count + i], refs[-1].at[i]) for i in range(count)
    ]
    for copy in copies:
        copy.start()
    for copy in copies:
        copy.wait()


def attend_kernel(lists, near_ref, k_ref, v_hbm, *refs):
    q_refs, out_refs = refs[:CTX], refs[CTX : 2 * CTX]
    s_scr, m_scr, v_ref, sem = refs[2 * CTX :]
    v_copy = pltpu.make_async_copy(v_hbm, v_ref, sem)
    v_copy.start()
    groups, local_rows, _ = q_refs[0].shape
    member = lax.rem(lax.axis_index("seq"), HEADS_PER_GROUP)
    quarter = lax.axis_index("ctx")
    rows = TILE_QUERY_ROWS
    head_size = k_ref.shape[2]
    scale = LOG2E / math.sqrt(head_size)
    shift, mask = local_rows.bit_length() - 1, local_rows - 1
    lane = lax.broadcasted_iota(jnp.int32, (rows, LANES), 1)
    sublane = lax.broadcasted_iota(jnp.int32, (rows, LANES), 0)

    def one_block(group):
        block = group * HEADS_PER_GROUP + member
        near = []
        for back in range(NEAR):
            place = jnp.maximum(group - jnp.where(member < back, 1, 0), 0)
            near.append(near_ref[place_of(lax.rem(member - back + HEADS_PER_GROUP, HEADS_PER_GROUP)), place])
        near_k = jnp.concatenate([one[:local_rows] for one in near] * 2, axis=0)
        near_v = jnp.concatenate([one[local_rows : 2 * local_rows] for one in near] * 2, axis=0)
        position = (block - (lane >> shift)) * rows + quarter * local_rows + (lane & mask)
        token = block * rows + ((sublane >> shift) ^ quarter) * local_rows + (sublane & mask)
        oldest = jnp.maximum((block * rows // KROWS - 1) * KROWS, 0)
        near_ok = (lane < rows) & (position <= token) & (position >= oldest)

        def columns_of(head):
            return pl.ds(pl.multiple_of(head * head_size, LANES), head_size)

        def scores(head):
            count = lists[place_of(head), group, COUNTS_AT + block]
            q = jnp.concatenate([q_ref[group, :, columns_of(head)] for q_ref in q_refs], axis=0)
            high = jnp.full((rows, LANES), -jnp.inf, jnp.float32)
            for slot in range(0, KQ, SLOTS_AT_ONCE):
                last = slot + SLOTS_AT_ONCE == KQ
                keys = [k_ref[lists[place_of(head), group, slot + i]] for i in range(SLOTS_AT_ONCE)]
                several = nt(q, jnp.concatenate(keys + [near_k] * last, axis=0))
                for i in range(SLOTS_AT_ONCE + last):
                    s = several[:, i * KROWS : (i + 1) * KROWS]
                    seen = near_ok if i == SLOTS_AT_ONCE else slot + i < count
                    s = jnp.where(seen, s, -jnp.inf)
                    s_scr[head, slot + i] = s
                    high = jnp.maximum(high, s)
            m_scr[head] = high

        def sums(head, stats):
            top = m_scr[head]
            total = jnp.zeros((rows, LANES), jnp.float32)
            acc = jnp.zeros((rows, head_size), jnp.float32)
            for slot in range(0, KQ, SLOTS_AT_ONCE):
                last = slot + SLOTS_AT_ONCE == KQ
                weights = []
                for part in range(slot, slot + SLOTS_AT_ONCE + last):
                    p = jnp.exp2(s_scr[head, part] * scale - top)
                    total = total + p
                    weights.append(p.astype(jnp.bfloat16))
                values = [v_ref[lists[place_of(head), group, slot + i]] for i in range(SLOTS_AT_ONCE)]
                acc = acc + jnp.dot(
                    jnp.concatenate(weights, axis=1),
                    jnp.concatenate(values + [near_v] * last, axis=0),
                    preferred_element_type=jnp.float32,
                )
            acc = acc.astype(jnp.bfloat16)
            for part, out_ref in enumerate(out_refs):
                out_ref[group, :, columns_of(head)] = acc[
                    part * local_rows : (part + 1) * local_rows
                ]
            total = jnp.sum(total, axis=1, keepdims=True)
            stats = jnp.where(lane == head, top, stats)
            return jnp.where(lane == head + HEADS_PER_GROUP, total, stats)

        def score_step(turn, carry):
            for i in range(AT_ONCE):
                scores(turn * AT_ONCE + i)
            return carry

        def sum_step(turn, stats):
            for i in range(AT_ONCE):
                stats = sums(turn * AT_ONCE + i, stats)
            return stats

        steps = HEADS_PER_GROUP // AT_ONCE
        lax.fori_loop(0, steps, score_step, 0)
        for head in range(HEADS_PER_GROUP):
            top = jnp.max(m_scr[head], axis=1, keepdims=True) * scale
            m_scr[head] = jnp.broadcast_to(top, (rows, LANES))
        if groups == 1:
            v_copy.wait()
        else:
            pl.when(group == 0)(v_copy.wait)
        stats = lax.fori_loop(0, steps, sum_step, jnp.zeros((rows, LANES), jnp.float32))
        packed = jnp.zeros((rows, LANES), jnp.float32)
        for step in range(3):
            part = stats.astype(jnp.bfloat16).astype(jnp.float32)
            stats = stats - part
            by = step * 2 * HEADS_PER_GROUP
            packed = packed + (pltpu.roll(part, by, 1) if by else part)
        packed = packed.astype(jnp.bfloat16)
        width = HEADS_PER_GROUP * head_size
        for part, out_ref in enumerate(out_refs):
            out_ref[group, :, width:] = packed[part * local_rows : (part + 1) * local_rows]

    if groups == 1:
        one_block(0)
    else:
        pl.loop(0, groups)(one_block)


def merge_kernel(*refs):
    in_refs, out_ref = refs[:-1], refs[-1]
    groups, local_rows, full = in_refs[0].shape
    width = full - LANES
    head_size = width // HEADS_PER_GROUP

    def one_block(group):
        stats = []
        for in_ref in in_refs:
            packed = in_ref[group, :, width:].astype(jnp.float32)
            one = packed
            for step in (1, 2):
                one = one + pltpu.roll(packed, LANES - step * 2 * HEADS_PER_GROUP, 1)
            stats.append(one)
        top = stats[0]
        for one in stats[1:]:
            top = jnp.maximum(top, one)
        factors = [jnp.exp2(one - top) for one in stats]
        total = jnp.zeros((local_rows, LANES), jnp.float32)
        for one, factor in zip(stats, factors):
            total = total + pltpu.roll(one, LANES - HEADS_PER_GROUP, 1) * factor
        inverse = 1.0 / total
        factors = [factor * inverse for factor in factors]
        for head in range(HEADS_PER_GROUP):
            columns = slice(head * head_size, (head + 1) * head_size)
            mixed = jnp.zeros((local_rows, head_size), jnp.float32)
            for in_ref, factor in zip(in_refs, factors):
                mixed = mixed + in_ref[group, :, columns].astype(jnp.float32) * (
                    factor[:, head : head + 1]
                )
            out_ref[group, :, columns] = mixed.astype(jnp.bfloat16)

    if groups == 1:
        one_block(0)
    else:
        pl.loop(0, groups)(one_block)


def from_quarter(value, mask):
    return lax.ppermute(value, "ctx", [(device, device ^ mask) for device in range(CTX)])


def body(
    queries, new_token_keys, new_token_values, cache_keys, cache_values, block_ids, block_counts
):
    seq_count = lax.axis_size("seq")
    head_size = cache_keys.shape[2]
    local_rows = queries.shape[0]
    blocks = block_ids.shape[1]
    groups = seq_count // HEADS_PER_GROUP
    width = HEADS_PER_GROUP * head_size
    assert lax.axis_size("ctx") == CTX and cache_keys.shape[0] == 1
    assert local_rows * CTX == TILE_QUERY_ROWS and blocks <= LANES - COUNTS_AT
    assert head_size == LANES and local_rows & (local_rows - 1) == 0
    order = sorted(range(HEADS_PER_GROUP), key=place_of)
    same_group = [[g * HEADS_PER_GROUP + member for member in order] for g in range(groups)]
    if groups > 1:
        same_member = [
            [g * HEADS_PER_GROUP + r for g in range(groups)] for r in range(HEADS_PER_GROUP)
        ]

    def over_seq(pieces, members):
        return lax.all_to_all(
            pieces, "seq", split_axis=0, concat_axis=0, tiled=True, axis_index_groups=members
        )

    def in_hbm(value):
        return pltpu.with_memory_space_constraint(value, pltpu.HBM)

    def to_groups(rows):
        pieces = rows.reshape(local_rows, groups, -1).transpose(1, 0, 2)
        return pieces if groups == 1 else over_seq(pieces, same_member)

    vmem = pl.BlockSpec(memory_space=pltpu.VMEM)
    hbm = pl.BlockSpec(memory_space=pltpu.HBM)
    smem = pl.BlockSpec(memory_space=pltpu.SMEM)
    queries = to_groups(queries)
    others = [from_quarter(queries, mask) for mask in range(1, CTX)]
    small = (
        to_groups(new_token_keys),
        to_groups(new_token_values),
        block_ids,
        block_counts.reshape(1, blocks),
    )
    packed = pl.pallas_call(
        pack_kernel,
        out_shape=jax.ShapeDtypeStruct(
            (HEADS_PER_GROUP, groups, 2 * local_rows + LIST_ROWS, LANES), jnp.bfloat16
        ),
        in_specs=[hbm] * 4,
        out_specs=vmem,
        scratch_shapes=[pltpu.VMEM(one.shape, one.dtype) for one in small]
        + [pltpu.VMEM((LIST_ROWS, LANES), jnp.float32), pltpu.SemaphoreType.DMA((4,))],
        compiler_params=pltpu.CompilerParams(vmem_limit_bytes=4 * MIB),
        cost_estimate=pl.CostEstimate(flops=0, bytes_accessed=12 * MIB, transcendentals=0),
        name="pack",
    )(*[in_hbm(one) for one in small])
    large = (queries, cache_keys.reshape(-1, KROWS, head_size))
    queries, keys = pl.pallas_call(
        fetch_kernel,
        out_shape=[jax.ShapeDtypeStruct(one.shape, one.dtype) for one in large],
        in_specs=[hbm] * 2,
        out_specs=[vmem] * 2,
        scratch_shapes=[pltpu.SemaphoreType.DMA((2,))],
        compiler_params=pltpu.CompilerParams(vmem_limit_bytes=4 * MIB),
        cost_estimate=pl.CostEstimate(flops=0, bytes_accessed=4 * MIB, transcendentals=0),
        name="fetch",
    )(*[in_hbm(one) for one in large])
    near = over_seq(packed, same_group)
    lists = near[:, :, 2 * local_rows].astype(jnp.int32)
    tile = (TILE_QUERY_ROWS, KROWS)
    values = cache_values.reshape(-1, KROWS, head_size)
    partial = pl.pallas_call(
        attend_kernel,
        out_shape=[
            jax.ShapeDtypeStruct((groups, local_rows, width + LANES), jnp.bfloat16)
        ] * CTX,
        in_specs=[smem, vmem, vmem, hbm] + [vmem] * CTX,
        out_specs=[vmem] * CTX,
        scratch_shapes=[
            pltpu.VMEM((HEADS_PER_GROUP, KQ + 1) + tile, jnp.float32),
            pltpu.VMEM((HEADS_PER_GROUP,) + tile, jnp.float32),
            pltpu.VMEM(values.shape, values.dtype),
            pltpu.SemaphoreType.DMA,
        ],
        compiler_params=pltpu.CompilerParams(vmem_limit_bytes=24 * MIB),
        name="attend",
    )(lists, near, keys, in_hbm(values), queries, *others)
    partial = [from_quarter(partial[mask], mask) for mask in (2, 3, 1)] + [partial[0]]
    merged = pl.pallas_call(
        merge_kernel,
        out_shape=jax.ShapeDtypeStruct((groups, local_rows, width), jnp.bfloat16),
        in_specs=[vmem] * CTX,
        out_specs=vmem,
        compiler_params=pltpu.CompilerParams(vmem_limit_bytes=4 * MIB),
        name="merge",
    )(*partial)
    if groups > 1:
        merged = over_seq(merged, same_member)
    return merged.transpose(1, 0, 2).reshape(local_rows, groups * width)


def solution(mesh):
    return jax.shard_map(
        body,
        mesh=mesh,
        in_specs=(
            P(("seq", "ctx"), None),
            P(("seq", "ctx"), None),
            P(("seq", "ctx"), None),
            P("seq", "ctx", None),
            P("seq", "ctx", None),
            P("seq", None, "ctx", None),
            P("seq", None, "ctx"),
        ),
        out_specs=P(("seq", "ctx"), None),
        check_vma=False,
    )
```

```python
import math

import jax
import jax.numpy as jnp
from jax import lax
from jax.experimental import pallas as pl
from jax.experimental.pallas import tpu as pltpu
from jax.sharding import PartitionSpec as P

HEADS_PER_GROUP = 8
TILE_QUERY_ROWS = 64
KROWS = 128
KQ = 12
LANES = 128
CTX = 4
NEAR = 2 * KROWS // TILE_QUERY_ROWS
AT_ONCE = 4
MEETING_ORDERS = ((4, 3, 5, 2, 6, 1, 7, 0), (5, 7, 4, 3, 6, 2, 1, 0))
SLOTS_AT_ONCE = 4
LIST_ROWS = 8
COUNTS_AT = 16
MIB = 1024 * 1024
LOG2E = 1.4426950408889634


def nt(a, b):
    return lax.dot_general(a, b, (((1,), (1,)), ((), ())), preferred_element_type=jnp.float32)


def pack_kernel(*refs):
    sources, out_ref, targets = refs[:4], refs[4], refs[5:9]
    scratch, sems = refs[9:]
    copies = [
        pltpu.make_async_copy(source, target, sems.at[i])
        for i, (source, target) in enumerate(zip(sources, targets))
    ]
    for copy in copies:
        copy.start()
    keys, values, ids, counts = targets
    members, groups, _, _ = out_ref.shape
    local_rows = keys.shape[1]
    blocks = ids.shape[1]
    scratch[...] = jnp.zeros_like(scratch)
    for copy in copies:
        copy.wait()
    scratch[0:1, COUNTS_AT : COUNTS_AT + blocks] = counts[...].astype(jnp.float32)
    quarter = lax.axis_index("ctx")
    for member in range(members):
        place = place_of(member, quarter)
        for group in range(groups):
            block = group * members + member
            scratch[0:1, :KQ] = ids[0, block].astype(jnp.float32)
            out_ref[place, group, :local_rows] = keys[group]
            out_ref[place, group, local_rows : 2 * local_rows] = values[group]
            out_ref[place, group, 2 * local_rows :] = scratch[...].astype(jnp.bfloat16)


def place_of(member, quarter):
    second = quarter >= CTX // 2
    places = []
    for order in MEETING_ORDERS:
        if isinstance(member, int):
            places.append(jnp.int32(order.index(member)))
        else:
            places.append(sum(jnp.where(member == one, i, 0) for i, one in enumerate(order)))
    return jnp.where(second, places[1], places[0])


def fetch_kernel(*refs):
    count = len(refs) // 2
    copies = [
        pltpu.make_async_copy(refs[i], refs[count + i], refs[-1].at[i]) for i in range(count)
    ]
    for copy in copies:
        copy.start()
    for copy in copies:
        copy.wait()


def attend_kernel(lists, near_ref, k_ref, v_hbm, *refs):
    q_refs, out_refs = refs[:CTX], refs[CTX : 2 * CTX]
    s_scr, m_scr, v_ref, sem = refs[2 * CTX :]
    v_copy = pltpu.make_async_copy(v_hbm, v_ref, sem)
    v_copy.start()
    groups, local_rows, _ = q_refs[0].shape
    member = lax.rem(lax.axis_index("seq"), HEADS_PER_GROUP)
    quarter = lax.axis_index("ctx")
    rows = TILE_QUERY_ROWS
    head_size = k_ref.shape[2]
    scale = LOG2E / math.sqrt(head_size)
    shift, mask = local_rows.bit_length() - 1, local_rows - 1
    lane = lax.broadcasted_iota(jnp.int32, (rows, LANES), 1)
    sublane = lax.broadcasted_iota(jnp.int32, (rows, LANES), 0)

    def one_block(group):
        block = group * HEADS_PER_GROUP + member
        near = []
        for back in range(NEAR):
            place = jnp.maximum(group - jnp.where(member < back, 1, 0), 0)
            source = lax.rem(member - back + HEADS_PER_GROUP, HEADS_PER_GROUP)
            near.append(near_ref[place_of(source, quarter), place])
        near_k = jnp.concatenate([one[:local_rows] for one in near] * 2, axis=0)
        near_v = jnp.concatenate([one[local_rows : 2 * local_rows] for one in near] * 2, axis=0)
        position = (block - (lane >> shift)) * rows + quarter * local_rows + (lane & mask)
        token = block * rows + ((sublane >> shift) ^ quarter) * local_rows + (sublane & mask)
        oldest = jnp.maximum((block * rows // KROWS - 1) * KROWS, 0)
        near_ok = (lane < rows) & (position <= token) & (position >= oldest)

        def columns_of(head):
            return pl.ds(pl.multiple_of(head * head_size, LANES), head_size)

        def scores(head):
            place = place_of(head, quarter)
            count = lists[place, group, COUNTS_AT + block]
            q = jnp.concatenate([q_ref[group, :, columns_of(head)] for q_ref in q_refs], axis=0)
            s = jnp.where(near_ok, nt(q, near_k), -jnp.inf)
            s_scr[head, KQ] = s
            high = s
            for slot in range(0, KQ, SLOTS_AT_ONCE):
                keys = [k_ref[lists[place, group, slot + i]] for i in range(SLOTS_AT_ONCE)]
                several = nt(q, jnp.concatenate(keys, axis=0))
                for i in range(SLOTS_AT_ONCE):
                    s = several[:, i * KROWS : (i + 1) * KROWS]
                    s = jnp.where(slot + i < count, s, -jnp.inf)
                    s_scr[head, slot + i] = s
                    high = jnp.maximum(high, s)
            m_scr[head] = high

        def sums(head, stats):
            place = place_of(head, quarter)
            top = m_scr[head]
            total = jnp.exp2(s_scr[head, KQ] * scale - top)
            acc = jnp.dot(total.astype(jnp.bfloat16), near_v, preferred_element_type=jnp.float32)
            for slot in range(0, KQ, SLOTS_AT_ONCE):
                weights = []
                for part in range(slot, slot + SLOTS_AT_ONCE):
                    p = jnp.exp2(s_scr[head, part] * scale - top)
                    total = total + p
                    weights.append(p.astype(jnp.bfloat16))
                values = [v_ref[lists[place, group, slot + i]] for i in range(SLOTS_AT_ONCE)]
                acc = acc + jnp.dot(
                    jnp.concatenate(weights, axis=1),
                    jnp.concatenate(values, axis=0),
                    preferred_element_type=jnp.float32,
                )
            acc = acc.astype(jnp.bfloat16)
            for part, out_ref in enumerate(out_refs):
                out_ref[group, :, columns_of(head)] = acc[
                    part * local_rows : (part + 1) * local_rows
                ]
            total = jnp.sum(total, axis=1, keepdims=True)
            stats = jnp.where(lane == head, top, stats)
            return jnp.where(lane == head + HEADS_PER_GROUP, total, stats)

        def score_step(turn, carry):
            for i in range(AT_ONCE):
                scores(turn * AT_ONCE + i)
            return carry

        def sum_step(turn, stats):
            for i in range(AT_ONCE):
                stats = sums(turn * AT_ONCE + i, stats)
            return stats

        steps = HEADS_PER_GROUP // AT_ONCE
        lax.fori_loop(0, steps, score_step, 0)
        for head in range(HEADS_PER_GROUP):
            top = jnp.max(m_scr[head], axis=1, keepdims=True) * scale
            m_scr[head] = jnp.broadcast_to(top, (rows, LANES))
        if groups == 1:
            v_copy.wait()
        else:
            pl.when(group == 0)(v_copy.wait)
        stats = lax.fori_loop(0, steps, sum_step, jnp.zeros((rows, LANES), jnp.float32))
        packed = jnp.zeros((rows, LANES), jnp.float32)
        for step in range(3):
            part = stats.astype(jnp.bfloat16).astype(jnp.float32)
            stats = stats - part
            by = step * 2 * HEADS_PER_GROUP
            packed = packed + (pltpu.roll(part, by, 1) if by else part)
        packed = packed.astype(jnp.bfloat16)
        width = HEADS_PER_GROUP * head_size
        for part, out_ref in enumerate(out_refs):
            out_ref[group, :, width:] = packed[part * local_rows : (part + 1) * local_rows]

    if groups == 1:
        one_block(0)
    else:
        pl.loop(0, groups)(one_block)


def merge_kernel(*refs):
    in_refs, out_ref = refs[:-1], refs[-1]
    groups, local_rows, full = in_refs[0].shape
    width = full - LANES
    head_size = width // HEADS_PER_GROUP

    def one_block(group):
        stats = []
        for in_ref in in_refs:
            packed = in_ref[group, :, width:].astype(jnp.float32)
            one = packed
            for step in (1, 2):
                one = one + pltpu.roll(packed, LANES - step * 2 * HEADS_PER_GROUP, 1)
            stats.append(one)
        top = stats[0]
        for one in stats[1:]:
            top = jnp.maximum(top, one)
        factors = [jnp.exp2(one - top) for one in stats]
        total = jnp.zeros((local_rows, LANES), jnp.float32)
        for one, factor in zip(stats, factors):
            total = total + pltpu.roll(one, LANES - HEADS_PER_GROUP, 1) * factor
        inverse = 1.0 / total
        factors = [factor * inverse for factor in factors]
        for head in range(HEADS_PER_GROUP):
            columns = slice(head * head_size, (head + 1) * head_size)
            mixed = jnp.zeros((local_rows, head_size), jnp.float32)
            for in_ref, factor in zip(in_refs, factors):
                mixed = mixed + in_ref[group, :, columns].astype(jnp.float32) * (
                    factor[:, head : head + 1]
                )
            out_ref[group, :, columns] = mixed.astype(jnp.bfloat16)

    if groups == 1:
        one_block(0)
    else:
        pl.loop(0, groups)(one_block)


def from_quarter(value, mask):
    return lax.ppermute(value, "ctx", [(device, device ^ mask) for device in range(CTX)])


def body(
    queries, new_token_keys, new_token_values, cache_keys, cache_values, block_ids, block_counts
):
    seq_count = lax.axis_size("seq")
    head_size = cache_keys.shape[2]
    local_rows = queries.shape[0]
    blocks = block_ids.shape[1]
    groups = seq_count // HEADS_PER_GROUP
    width = HEADS_PER_GROUP * head_size
    assert lax.axis_size("ctx") == CTX and cache_keys.shape[0] == 1
    assert local_rows * CTX == TILE_QUERY_ROWS and blocks <= LANES - COUNTS_AT
    assert head_size == LANES and local_rows & (local_rows - 1) == 0
    same_group = []
    for g in range(groups):
        for c in range(CTX):
            order = MEETING_ORDERS[c // (CTX // 2)]
            same_group.append([(g * HEADS_PER_GROUP + member) * CTX + c for member in order])
    if groups > 1:
        same_member = [
            [g * HEADS_PER_GROUP + r for g in range(groups)] for r in range(HEADS_PER_GROUP)
        ]

    def over_seq(pieces, members):
        return lax.all_to_all(
            pieces, "seq", split_axis=0, concat_axis=0, tiled=True, axis_index_groups=members
        )

    def in_hbm(value):
        return pltpu.with_memory_space_constraint(value, pltpu.HBM)

    def to_groups(rows):
        pieces = rows.reshape(local_rows, groups, -1).transpose(1, 0, 2)
        return pieces if groups == 1 else over_seq(pieces, same_member)

    vmem = pl.BlockSpec(memory_space=pltpu.VMEM)
    hbm = pl.BlockSpec(memory_space=pltpu.HBM)
    smem = pl.BlockSpec(memory_space=pltpu.SMEM)
    queries = to_groups(queries)
    others = [from_quarter(queries, mask) for mask in range(1, CTX)]
    small = (
        to_groups(new_token_keys),
        to_groups(new_token_values),
        block_ids,
        block_counts.reshape(1, blocks),
    )
    packed = pl.pallas_call(
        pack_kernel,
        out_shape=jax.ShapeDtypeStruct(
            (HEADS_PER_GROUP, groups, 2 * local_rows + LIST_ROWS, LANES), jnp.bfloat16
        ),
        in_specs=[hbm] * 4,
        out_specs=vmem,
        scratch_shapes=[pltpu.VMEM(one.shape, one.dtype) for one in small]
        + [pltpu.VMEM((LIST_ROWS, LANES), jnp.float32), pltpu.SemaphoreType.DMA((4,))],
        compiler_params=pltpu.CompilerParams(vmem_limit_bytes=4 * MIB),
        cost_estimate=pl.CostEstimate(flops=0, bytes_accessed=12 * MIB, transcendentals=0),
        name="pack",
    )(*[in_hbm(one) for one in small])
    large = (queries, cache_keys.reshape(-1, KROWS, head_size))
    queries, keys = pl.pallas_call(
        fetch_kernel,
        out_shape=[jax.ShapeDtypeStruct(one.shape, one.dtype) for one in large],
        in_specs=[hbm] * 2,
        out_specs=[vmem] * 2,
        scratch_shapes=[pltpu.SemaphoreType.DMA((2,))],
        compiler_params=pltpu.CompilerParams(vmem_limit_bytes=4 * MIB),
        cost_estimate=pl.CostEstimate(flops=0, bytes_accessed=4 * MIB, transcendentals=0),
        name="fetch",
    )(*[in_hbm(one) for one in large])
    near = lax.all_to_all(
        packed,
        ("seq", "ctx"),
        split_axis=0,
        concat_axis=0,
        tiled=True,
        axis_index_groups=same_group,
    )
    lists = near[:, :, 2 * local_rows].astype(jnp.int32)
    tile = (TILE_QUERY_ROWS, KROWS)
    values = cache_values.reshape(-1, KROWS, head_size)
    partial = pl.pallas_call(
        attend_kernel,
        out_shape=[
            jax.ShapeDtypeStruct((groups, local_rows, width + LANES), jnp.bfloat16)
        ] * CTX,
        in_specs=[smem, vmem, vmem, hbm] + [vmem] * CTX,
        out_specs=[vmem] * CTX,
        scratch_shapes=[
            pltpu.VMEM((HEADS_PER_GROUP, KQ + 1) + tile, jnp.float32),
            pltpu.VMEM((HEADS_PER_GROUP,) + tile, jnp.float32),
            pltpu.VMEM(values.shape, values.dtype),
            pltpu.SemaphoreType.DMA,
        ],
        compiler_params=pltpu.CompilerParams(vmem_limit_bytes=24 * MIB),
        name="attend",
    )(lists, near, keys, in_hbm(values), queries, *others)
    partial = [from_quarter(partial[mask], mask) for mask in (2, 3, 1)] + [partial[0]]
    merged = pl.pallas_call(
        merge_kernel,
        out_shape=jax.ShapeDtypeStruct((groups, local_rows, width), jnp.bfloat16),
        in_specs=[vmem] * CTX,
        out_specs=vmem,
        compiler_params=pltpu.CompilerParams(vmem_limit_bytes=4 * MIB),
        name="merge",
    )(*partial)
    if groups > 1:
        merged = over_seq(merged, same_member)
    return merged.transpose(1, 0, 2).reshape(local_rows, groups * width)


def solution(mesh):
    return jax.shard_map(
        body,
        mesh=mesh,
        in_specs=(
            P(("seq", "ctx"), None),
            P(("seq", "ctx"), None),
            P(("seq", "ctx"), None),
            P("seq", "ctx", None),
            P("seq", "ctx", None),
            P("seq", None, "ctx", None),
            P("seq", None, "ctx"),
        ),
        out_specs=P(("seq", "ctx"), None),
        check_vma=False,
    )
```

```python
import math

import jax
import jax.numpy as jnp
from jax import lax
from jax.experimental import pallas as pl
from jax.experimental.pallas import tpu as pltpu
from jax.sharding import PartitionSpec as P

HEADS_PER_GROUP = 8
TILE_QUERY_ROWS = 64
KROWS = 128
KQ = 12
LANES = 128
CTX = 4
NEAR = 2 * KROWS // TILE_QUERY_ROWS
AT_ONCE = 4
SLOTS_AT_ONCE = 6
LIST_ROWS = 8
COUNTS_AT = 16
MIB = 1024 * 1024
LOG2E = 1.4426950408889634


def nt(a, b):
    return lax.dot_general(a, b, (((1,), (1,)), ((), ())), preferred_element_type=jnp.float32)


def pack_kernel(*refs):
    sources, out_ref, targets = refs[:4], refs[4], refs[5:9]
    scratch, sems = refs[9:]
    copies = [
        pltpu.make_async_copy(source, target, sems.at[i])
        for i, (source, target) in enumerate(zip(sources, targets))
    ]
    for copy in copies:
        copy.start()
    keys, values, ids, counts = targets
    members, groups, _, _ = out_ref.shape
    local_rows = keys.shape[1]
    blocks = ids.shape[1]
    scratch[...] = jnp.zeros_like(scratch)
    for copy in copies:
        copy.wait()
    scratch[0:1, COUNTS_AT : COUNTS_AT + blocks] = counts[...].astype(jnp.float32)
    for member in range(members):
        for group in range(groups):
            block = group * members + member
            scratch[0:1, :KQ] = ids[0, block].astype(jnp.float32)
            out_ref[place_of(member), group, :local_rows] = keys[group]
            out_ref[place_of(member), group, local_rows : 2 * local_rows] = values[group]
            out_ref[place_of(member), group, 2 * local_rows :] = scratch[...].astype(jnp.bfloat16)


def place_of(member):
    half = HEADS_PER_GROUP // 2
    if isinstance(member, int):
        return 2 * (member - half) if member >= half else HEADS_PER_GROUP - 1 - 2 * member
    return jnp.where(member >= half, 2 * (member - half), HEADS_PER_GROUP - 1 - 2 * member)


def fetch_kernel(*refs):
    count = len(refs) // 2
    copies = [
        pltpu.make_async_copy(refs[i], refs[count + i], refs[-1].at[i]) for i in range(count)
    ]
    for copy in copies:
        copy.start()
    for copy in copies:
        copy.wait()


def attend_kernel(lists, near_ref, k_ref, v_hbm, *refs):
    q_refs, out_refs = refs[:CTX], refs[CTX : 2 * CTX]
    s_scr, m_scr, v_ref, sem = refs[2 * CTX :]
    v_copy = pltpu.make_async_copy(v_hbm, v_ref, sem)
    v_copy.start()
    groups, local_rows, _ = q_refs[0].shape
    member = lax.rem(lax.axis_index("seq"), HEADS_PER_GROUP)
    quarter = lax.axis_index("ctx")
    rows = TILE_QUERY_ROWS
    head_size = k_ref.shape[2]
    scale = LOG2E / math.sqrt(head_size)
    shift, mask = local_rows.bit_length() - 1, local_rows - 1
    lane = lax.broadcasted_iota(jnp.int32, (rows, LANES), 1)
    sublane = lax.broadcasted_iota(jnp.int32, (rows, LANES), 0)

    def one_block(group):
        block = group * HEADS_PER_GROUP + member
        near = []
        for back in range(NEAR):
            place = jnp.maximum(group - jnp.where(member < back, 1, 0), 0)
            near.append(near_ref[place_of(lax.rem(member - back + HEADS_PER_GROUP, HEADS_PER_GROUP)), place])
        near_k = jnp.concatenate([one[:local_rows] for one in near] * 2, axis=0)
        near_v = jnp.concatenate([one[local_rows : 2 * local_rows] for one in near] * 2, axis=0)
        position = (block - (lane >> shift)) * rows + quarter * local_rows + (lane & mask)
        token = block * rows + ((sublane >> shift) ^ quarter) * local_rows + (sublane & mask)
        oldest = jnp.maximum((block * rows // KROWS - 1) * KROWS, 0)
        near_ok = (lane < rows) & (position <= token) & (position >= oldest)

        def columns_of(head):
            return pl.ds(pl.multiple_of(head * head_size, LANES), head_size)

        def scores(head):
            count = lists[place_of(head), group, COUNTS_AT + block]
            q = jnp.concatenate([q_ref[group, :, columns_of(head)] for q_ref in q_refs], axis=0)
            s = jnp.where(near_ok, nt(q, near_k), -jnp.inf)
            s_scr[head, KQ] = s
            high = s
            for slot in range(0, KQ, SLOTS_AT_ONCE):
                keys = [k_ref[lists[place_of(head), group, slot + i]] for i in range(SLOTS_AT_ONCE)]
                several = nt(q, jnp.concatenate(keys, axis=0))
                for i in range(SLOTS_AT_ONCE):
                    s = several[:, i * KROWS : (i + 1) * KROWS]
                    s = jnp.where(slot + i < count, s, -jnp.inf)
                    s_scr[head, slot + i] = s
                    high = jnp.maximum(high, s)
            m_scr[head] = high

        def sums(head, stats):
            top = m_scr[head]
            total = jnp.exp2(s_scr[head, KQ] * scale - top)
            acc = jnp.dot(total.astype(jnp.bfloat16), near_v, preferred_element_type=jnp.float32)
            for slot in range(0, KQ, SLOTS_AT_ONCE):
                weights = []
                for part in range(slot, slot + SLOTS_AT_ONCE):
                    p = jnp.exp2(s_scr[head, part] * scale - top)
                    total = total + p
                    weights.append(p.astype(jnp.bfloat16))
                values = [v_ref[lists[place_of(head), group, slot + i]] for i in range(SLOTS_AT_ONCE)]
                acc = acc + jnp.dot(
                    jnp.concatenate(weights, axis=1),
                    jnp.concatenate(values, axis=0),
                    preferred_element_type=jnp.float32,
                )
            acc = acc.astype(jnp.bfloat16)
            for part, out_ref in enumerate(out_refs):
                out_ref[group, :, columns_of(head)] = acc[
                    part * local_rows : (part + 1) * local_rows
                ]
            total = jnp.sum(total, axis=1, keepdims=True)
            stats = jnp.where(lane == head, top, stats)
            return jnp.where(lane == head + HEADS_PER_GROUP, total, stats)

        def score_step(turn, carry):
            for i in range(AT_ONCE):
                scores(turn * AT_ONCE + i)
            return carry

        def sum_step(turn, stats):
            for i in range(AT_ONCE):
                stats = sums(turn * AT_ONCE + i, stats)
            return stats

        steps = HEADS_PER_GROUP // AT_ONCE
        lax.fori_loop(0, steps, score_step, 0)
        for head in range(HEADS_PER_GROUP):
            top = jnp.max(m_scr[head], axis=1, keepdims=True) * scale
            m_scr[head] = jnp.broadcast_to(top, (rows, LANES))
        if groups == 1:
            v_copy.wait()
        else:
            pl.when(group == 0)(v_copy.wait)
        stats = lax.fori_loop(0, steps, sum_step, jnp.zeros((rows, LANES), jnp.float32))
        packed = jnp.zeros((rows, LANES), jnp.float32)
        for step in range(3):
            part = stats.astype(jnp.bfloat16).astype(jnp.float32)
            stats = stats - part
            by = step * 2 * HEADS_PER_GROUP
            packed = packed + (pltpu.roll(part, by, 1) if by else part)
        packed = packed.astype(jnp.bfloat16)
        width = HEADS_PER_GROUP * head_size
        for part, out_ref in enumerate(out_refs):
            out_ref[group, :, width:] = packed[part * local_rows : (part + 1) * local_rows]

    if groups == 1:
        one_block(0)
    else:
        pl.loop(0, groups)(one_block)


def merge_kernel(*refs):
    in_refs, out_ref = refs[:-1], refs[-1]
    groups, local_rows, full = in_refs[0].shape
    width = full - LANES
    head_size = width // HEADS_PER_GROUP

    def one_block(group):
        stats = []
        for in_ref in in_refs:
            packed = in_ref[group, :, width:].astype(jnp.float32)
            one = packed
            for step in (1, 2):
                one = one + pltpu.roll(packed, LANES - step * 2 * HEADS_PER_GROUP, 1)
            stats.append(one)
        top = stats[0]
        for one in stats[1:]:
            top = jnp.maximum(top, one)
        factors = [jnp.exp2(one - top) for one in stats]
        total = jnp.zeros((local_rows, LANES), jnp.float32)
        for one, factor in zip(stats, factors):
            total = total + pltpu.roll(one, LANES - HEADS_PER_GROUP, 1) * factor
        inverse = 1.0 / total
        factors = [factor * inverse for factor in factors]
        for head in range(HEADS_PER_GROUP):
            columns = slice(head * head_size, (head + 1) * head_size)
            mixed = jnp.zeros((local_rows, head_size), jnp.float32)
            for in_ref, factor in zip(in_refs, factors):
                mixed = mixed + in_ref[group, :, columns].astype(jnp.float32) * (
                    factor[:, head : head + 1]
                )
            out_ref[group, :, columns] = mixed.astype(jnp.bfloat16)

    if groups == 1:
        one_block(0)
    else:
        pl.loop(0, groups)(one_block)


def from_quarter(value, mask):
    return lax.ppermute(value, "ctx", [(device, device ^ mask) for device in range(CTX)])


def body(
    queries, new_token_keys, new_token_values, cache_keys, cache_values, block_ids, block_counts
):
    seq_count = lax.axis_size("seq")
    head_size = cache_keys.shape[2]
    local_rows = queries.shape[0]
    blocks = block_ids.shape[1]
    groups = seq_count // HEADS_PER_GROUP
    width = HEADS_PER_GROUP * head_size
    assert lax.axis_size("ctx") == CTX and cache_keys.shape[0] == 1
    assert local_rows * CTX == TILE_QUERY_ROWS and blocks <= LANES - COUNTS_AT
    assert head_size == LANES and local_rows & (local_rows - 1) == 0
    order = sorted(range(HEADS_PER_GROUP), key=place_of)
    same_group = [[g * HEADS_PER_GROUP + member for member in order] for g in range(groups)]
    if groups > 1:
        same_member = [
            [g * HEADS_PER_GROUP + r for g in range(groups)] for r in range(HEADS_PER_GROUP)
        ]

    def over_seq(pieces, members):
        return lax.all_to_all(
            pieces, "seq", split_axis=0, concat_axis=0, tiled=True, axis_index_groups=members
        )

    def in_hbm(value):
        return pltpu.with_memory_space_constraint(value, pltpu.HBM)

    def to_groups(rows):
        pieces = rows.reshape(local_rows, groups, -1).transpose(1, 0, 2)
        return pieces if groups == 1 else over_seq(pieces, same_member)

    vmem = pl.BlockSpec(memory_space=pltpu.VMEM)
    hbm = pl.BlockSpec(memory_space=pltpu.HBM)
    smem = pl.BlockSpec(memory_space=pltpu.SMEM)
    queries = to_groups(queries)
    others = [from_quarter(queries, mask) for mask in range(1, CTX)]
    small = (
        to_groups(new_token_keys),
        to_groups(new_token_values),
        block_ids,
        block_counts.reshape(1, blocks),
    )
    packed = pl.pallas_call(
        pack_kernel,
        out_shape=jax.ShapeDtypeStruct(
            (HEADS_PER_GROUP, groups, 2 * local_rows + LIST_ROWS, LANES), jnp.bfloat16
        ),
        in_specs=[hbm] * 4,
        out_specs=vmem,
        scratch_shapes=[pltpu.VMEM(one.shape, one.dtype) for one in small]
        + [pltpu.VMEM((LIST_ROWS, LANES), jnp.float32), pltpu.SemaphoreType.DMA((4,))],
        compiler_params=pltpu.CompilerParams(vmem_limit_bytes=4 * MIB),
        cost_estimate=pl.CostEstimate(flops=0, bytes_accessed=12 * MIB, transcendentals=0),
        name="pack",
    )(*[in_hbm(one) for one in small])
    large = (queries, cache_keys.reshape(-1, KROWS, head_size))
    queries, keys = pl.pallas_call(
        fetch_kernel,
        out_shape=[jax.ShapeDtypeStruct(one.shape, one.dtype) for one in large],
        in_specs=[hbm] * 2,
        out_specs=[vmem] * 2,
        scratch_shapes=[pltpu.SemaphoreType.DMA((2,))],
        compiler_params=pltpu.CompilerParams(vmem_limit_bytes=4 * MIB),
        cost_estimate=pl.CostEstimate(flops=0, bytes_accessed=4 * MIB, transcendentals=0),
        name="fetch",
    )(*[in_hbm(one) for one in large])
    near = over_seq(packed, same_group)
    lists = near[:, :, 2 * local_rows].astype(jnp.int32)
    tile = (TILE_QUERY_ROWS, KROWS)
    values = cache_values.reshape(-1, KROWS, head_size)
    partial = pl.pallas_call(
        attend_kernel,
        out_shape=[
            jax.ShapeDtypeStruct((groups, local_rows, width + LANES), jnp.bfloat16)
        ] * CTX,
        in_specs=[smem, vmem, vmem, hbm] + [vmem] * CTX,
        out_specs=[vmem] * CTX,
        scratch_shapes=[
            pltpu.VMEM((HEADS_PER_GROUP, KQ + 1) + tile, jnp.float32),
            pltpu.VMEM((HEADS_PER_GROUP,) + tile, jnp.float32),
            pltpu.VMEM(values.shape, values.dtype),
            pltpu.SemaphoreType.DMA,
        ],
        compiler_params=pltpu.CompilerParams(vmem_limit_bytes=24 * MIB),
        name="attend",
    )(lists, near, keys, in_hbm(values), queries, *others)
    partial = [from_quarter(partial[mask], mask) for mask in (2, 3, 1)] + [partial[0]]
    merged = pl.pallas_call(
        merge_kernel,
        out_shape=jax.ShapeDtypeStruct((groups, local_rows, width), jnp.bfloat16),
        in_specs=[vmem] * CTX,
        out_specs=vmem,
        compiler_params=pltpu.CompilerParams(vmem_limit_bytes=4 * MIB),
        name="merge",
    )(*partial)
    if groups > 1:
        merged = over_seq(merged, same_member)
    return merged.transpose(1, 0, 2).reshape(local_rows, groups * width)


def solution(mesh):
    return jax.shard_map(
        body,
        mesh=mesh,
        in_specs=(
            P(("seq", "ctx"), None),
            P(("seq", "ctx"), None),
            P(("seq", "ctx"), None),
            P("seq", "ctx", None),
            P("seq", "ctx", None),
            P("seq", None, "ctx", None),
            P("seq", None, "ctx"),
        ),
        out_specs=P(("seq", "ctx"), None),
        check_vma=False,
    )
```

```python
import math

import jax
import jax.numpy as jnp
from jax import lax
from jax.experimental import pallas as pl
from jax.experimental.pallas import tpu as pltpu
from jax.sharding import PartitionSpec as P

HEADS_PER_GROUP = 8
TILE_QUERY_ROWS = 64
KROWS = 128
KQ = 12
LANES = 128
CTX = 4
NEAR = 2 * KROWS // TILE_QUERY_ROWS
AT_ONCE = 4
SLOTS_AT_ONCE = 4
LIST_ROWS = 8
COUNTS_AT = 16
MIB = 1024 * 1024
LOG2E = 1.4426950408889634


def nt(a, b):
    return lax.dot_general(a, b, (((1,), (1,)), ((), ())), preferred_element_type=jnp.float32)


def pack_kernel(*refs):
    sources, out_ref, targets = refs[:4], refs[4], refs[5:9]
    scratch, sems = refs[9:]
    copies = [
        pltpu.make_async_copy(source, target, sems.at[i])
        for i, (source, target) in enumerate(zip(sources, targets))
    ]
    for copy in copies:
        copy.start()
    keys, values, ids, counts = targets
    members, groups, _, _ = out_ref.shape
    local_rows = keys.shape[1]
    blocks = ids.shape[1]
    scratch[...] = jnp.zeros_like(scratch)
    for copy in copies:
        copy.wait()
    scratch[0:1, COUNTS_AT : COUNTS_AT + blocks] = counts[...].astype(jnp.float32)
    for member in range(members):
        for group in range(groups):
            block = group * members + member
            scratch[0:1, :KQ] = ids[0, block].astype(jnp.float32)
            out_ref[place_of(member), group, :local_rows] = keys[group]
            out_ref[place_of(member), group, local_rows : 2 * local_rows] = values[group]
            out_ref[place_of(member), group, 2 * local_rows :] = scratch[...].astype(jnp.bfloat16)


def place_of(member):
    half = HEADS_PER_GROUP // 2
    if isinstance(member, int):
        return 2 * (member - half) if member >= half else HEADS_PER_GROUP - 1 - 2 * member
    return jnp.where(member >= half, 2 * (member - half), HEADS_PER_GROUP - 1 - 2 * member)


def fetch_kernel(*refs):
    count = len(refs) // 2
    copies = [
        pltpu.make_async_copy(refs[i], refs[count + i], refs[-1].at[i]) for i in range(count)
    ]
    for copy in copies:
        copy.start()
    for copy in copies:
        copy.wait()


def attend_kernel(lists, near_ref, k_ref, v_hbm, *refs):
    q_refs, out_refs = refs[:CTX], refs[CTX : 2 * CTX]
    s_scr, m_scr, v_ref, sem = refs[2 * CTX :]
    v_copy = pltpu.make_async_copy(v_hbm, v_ref, sem)
    v_copy.start()
    groups, local_rows, _ = q_refs[0].shape
    member = lax.rem(lax.axis_index("seq"), HEADS_PER_GROUP)
    quarter = lax.axis_index("ctx")
    rows = TILE_QUERY_ROWS
    head_size = k_ref.shape[2]
    scale = LOG2E / math.sqrt(head_size)
    shift, mask = local_rows.bit_length() - 1, local_rows - 1
    lane = lax.broadcasted_iota(jnp.int32, (rows, LANES), 1)
    sublane = lax.broadcasted_iota(jnp.int32, (rows, LANES), 0)

    def one_block(group):
        block = group * HEADS_PER_GROUP + member
        near = []
        for back in range(NEAR):
            place = jnp.maximum(group - jnp.where(member < back, 1, 0), 0)
            near.append(near_ref[place_of(lax.rem(member - back + HEADS_PER_GROUP, HEADS_PER_GROUP)), place])
        near_k = jnp.concatenate([one[:local_rows] for one in near] * 2, axis=0)
        near_v = jnp.concatenate([one[local_rows : 2 * local_rows] for one in near] * 2, axis=0)
        position = (block - (lane >> shift)) * rows + quarter * local_rows + (lane & mask)
        token = block * rows + ((sublane >> shift) ^ quarter) * local_rows + (sublane & mask)
        oldest = jnp.maximum((block * rows // KROWS - 1) * KROWS, 0)
        near_ok = (lane < rows) & (position <= token) & (position >= oldest)

        def columns_of(head):
            return pl.ds(pl.multiple_of(head * head_size, LANES), head_size)

        def scores(head):
            count = lists[place_of(head), group, COUNTS_AT + block]
            q = jnp.concatenate([q_ref[group, :, columns_of(head)] for q_ref in q_refs], axis=0)
            s = jnp.where(near_ok, nt(q, near_k), -jnp.inf)
            s_scr[head, KQ] = s
            high = s
            for slot in range(0, KQ, SLOTS_AT_ONCE):
                keys = [k_ref[lists[place_of(head), group, slot + i]] for i in range(SLOTS_AT_ONCE)]
                several = nt(q, jnp.concatenate(keys, axis=0))
                for i in range(SLOTS_AT_ONCE):
                    s = several[:, i * KROWS : (i + 1) * KROWS]
                    s = jnp.where(slot + i < count, s, -jnp.inf)
                    s_scr[head, slot + i] = s
                    high = jnp.maximum(high, s)
            m_scr[head] = high

        def sums(head, stats):
            top = m_scr[head]
            total = jnp.exp2(s_scr[head, KQ] * scale - top)
            acc = jnp.dot(total.astype(jnp.bfloat16), near_v, preferred_element_type=jnp.float32)
            for slot in range(0, KQ, SLOTS_AT_ONCE):
                weights = []
                for part in range(slot, slot + SLOTS_AT_ONCE):
                    p = jnp.exp2(s_scr[head, part] * scale - top)
                    total = total + p
                    weights.append(p.astype(jnp.bfloat16))
                values = [v_ref[lists[place_of(head), group, slot + i]] for i in range(SLOTS_AT_ONCE)]
                acc = acc + jnp.dot(
                    jnp.concatenate(weights, axis=1),
                    jnp.concatenate(values, axis=0),
                    preferred_element_type=jnp.float32,
                )
            acc = acc.astype(jnp.bfloat16)
            for part, out_ref in enumerate(out_refs):
                out_ref[group, :, columns_of(head)] = acc[
                    part * local_rows : (part + 1) * local_rows
                ]
            total = jnp.sum(total, axis=1, keepdims=True)
            stats = jnp.where(lane == head, top, stats)
            return jnp.where(lane == head + HEADS_PER_GROUP, total, stats)

        def score_step(turn, carry):
            for i in range(AT_ONCE):
                scores(turn * AT_ONCE + i)
            return carry

        def sum_step(turn, stats):
            for i in range(AT_ONCE):
                stats = sums(turn * AT_ONCE + i, stats)
            return stats

        steps = HEADS_PER_GROUP // AT_ONCE
        lax.fori_loop(0, steps, score_step, 0)
        for head in range(HEADS_PER_GROUP):
            top = jnp.max(m_scr[head], axis=1, keepdims=True) * scale
            m_scr[head] = jnp.broadcast_to(top, (rows, LANES))
        if groups == 1:
            v_copy.wait()
        else:
            pl.when(group == 0)(v_copy.wait)
        stats = lax.fori_loop(0, steps, sum_step, jnp.zeros((rows, LANES), jnp.float32))
        packed = jnp.zeros((rows, LANES), jnp.float32)
        for step in range(3):
            part = stats.astype(jnp.bfloat16).astype(jnp.float32)
            stats = stats - part
            by = step * 2 * HEADS_PER_GROUP
            packed = packed + (pltpu.roll(part, by, 1) if by else part)
        packed = packed.astype(jnp.bfloat16)
        width = HEADS_PER_GROUP * head_size
        for part, out_ref in enumerate(out_refs):
            out_ref[group, :, width:] = packed[part * local_rows : (part + 1) * local_rows]

    if groups == 1:
        one_block(0)
    else:
        pl.loop(0, groups)(one_block)


def merge_kernel(*refs):
    in_refs, out_ref = refs[:-1], refs[-1]
    groups, local_rows, full = in_refs[0].shape
    width = full - LANES
    head_size = width // HEADS_PER_GROUP

    def one_block(group):
        stats = []
        for in_ref in in_refs:
            packed = in_ref[group, :, width:].astype(jnp.float32)
            one = packed
            for step in (1, 2):
                one = one + pltpu.roll(packed, LANES - step * 2 * HEADS_PER_GROUP, 1)
            stats.append(one)
        top = stats[0]
        for one in stats[1:]:
            top = jnp.maximum(top, one)
        factors = [jnp.exp2(one - top) for one in stats]
        total = jnp.zeros((local_rows, LANES), jnp.float32)
        for one, factor in zip(stats, factors):
            total = total + pltpu.roll(one, LANES - HEADS_PER_GROUP, 1) * factor
        inverse = 1.0 / total
        factors = [factor * inverse for factor in factors]
        for head in range(HEADS_PER_GROUP):
            columns = slice(head * head_size, (head + 1) * head_size)
            mixed = jnp.zeros((local_rows, head_size), jnp.float32)
            for in_ref, factor in zip(in_refs, factors):
                mixed = mixed + in_ref[group, :, columns].astype(jnp.float32) * (
                    factor[:, head : head + 1]
                )
            out_ref[group, :, columns] = mixed.astype(jnp.bfloat16)

    if groups == 1:
        one_block(0)
    else:
        pl.loop(0, groups)(one_block)


def from_quarter(value, mask):
    return lax.ppermute(value, "ctx", [(device, device ^ mask) for device in range(CTX)])


def body(
    queries, new_token_keys, new_token_values, cache_keys, cache_values, block_ids, block_counts
):
    seq_count = lax.axis_size("seq")
    head_size = cache_keys.shape[2]
    local_rows = queries.shape[0]
    blocks = block_ids.shape[1]
    groups = seq_count // HEADS_PER_GROUP
    width = HEADS_PER_GROUP * head_size
    assert lax.axis_size("ctx") == CTX and cache_keys.shape[0] == 1
    assert local_rows * CTX == TILE_QUERY_ROWS and blocks <= LANES - COUNTS_AT
    assert head_size == LANES and local_rows & (local_rows - 1) == 0
    order = sorted(range(HEADS_PER_GROUP), key=place_of)
    same_group = [[g * HEADS_PER_GROUP + member for member in order] for g in range(groups)]
    if groups > 1:
        same_member = [
            [g * HEADS_PER_GROUP + r for g in range(groups)] for r in range(HEADS_PER_GROUP)
        ]

    def over_seq(pieces, members):
        return lax.all_to_all(
            pieces, "seq", split_axis=0, concat_axis=0, tiled=True, axis_index_groups=members
        )

    def in_hbm(value):
        return pltpu.with_memory_space_constraint(value, pltpu.HBM)

    def to_groups(rows):
        pieces = rows.reshape(local_rows, groups, -1).transpose(1, 0, 2)
        return pieces if groups == 1 else over_seq(pieces, same_member)

    vmem = pl.BlockSpec(memory_space=pltpu.VMEM)
    hbm = pl.BlockSpec(memory_space=pltpu.HBM)
    smem = pl.BlockSpec(memory_space=pltpu.SMEM)
    queries = to_groups(queries)
    others = [from_quarter(queries, mask) for mask in range(1, CTX)]
    small = (
        to_groups(new_token_keys),
        to_groups(new_token_values),
        block_ids,
        block_counts.reshape(1, blocks),
    )
    packed = pl.pallas_call(
        pack_kernel,
        out_shape=jax.ShapeDtypeStruct(
            (HEADS_PER_GROUP, groups, 2 * local_rows + LIST_ROWS, LANES), jnp.bfloat16
        ),
        in_specs=[hbm] * 4,
        out_specs=vmem,
        scratch_shapes=[pltpu.VMEM(one.shape, one.dtype) for one in small]
        + [pltpu.VMEM((LIST_ROWS, LANES), jnp.float32), pltpu.SemaphoreType.DMA((4,))],
        compiler_params=pltpu.CompilerParams(vmem_limit_bytes=4 * MIB),
        cost_estimate=pl.CostEstimate(flops=0, bytes_accessed=12 * MIB, transcendentals=0),
        name="pack",
    )(*[in_hbm(one) for one in small])
    large = (queries, cache_keys.reshape(-1, KROWS, head_size))
    queries, keys = pl.pallas_call(
        fetch_kernel,
        out_shape=[jax.ShapeDtypeStruct(one.shape, one.dtype) for one in large],
        in_specs=[hbm] * 2,
        out_specs=[vmem] * 2,
        scratch_shapes=[pltpu.SemaphoreType.DMA((2,))],
        compiler_params=pltpu.CompilerParams(vmem_limit_bytes=4 * MIB),
        cost_estimate=pl.CostEstimate(flops=0, bytes_accessed=4 * MIB, transcendentals=0),
        name="fetch",
    )(*[in_hbm(one) for one in large])
    near = over_seq(packed, same_group)
    lists = near[:, :, 2 * local_rows].astype(jnp.int32)
    tile = (TILE_QUERY_ROWS, KROWS)
    values = cache_values.reshape(-1, KROWS, head_size)
    partial = pl.pallas_call(
        attend_kernel,
        out_shape=[
            jax.ShapeDtypeStruct((groups, local_rows, width + LANES), jnp.bfloat16)
        ] * CTX,
        in_specs=[smem, vmem, vmem, hbm] + [vmem] * CTX,
        out_specs=[vmem] * CTX,
        scratch_shapes=[
            pltpu.VMEM((HEADS_PER_GROUP, KQ + 1) + tile, jnp.float32),
            pltpu.VMEM((HEADS_PER_GROUP,) + tile, jnp.float32),
            pltpu.VMEM(values.shape, values.dtype),
            pltpu.SemaphoreType.DMA,
        ],
        compiler_params=pltpu.CompilerParams(vmem_limit_bytes=24 * MIB),
        name="attend",
    )(lists, near, keys, in_hbm(values), queries, *others)
    partial = [from_quarter(partial[mask], mask) for mask in (3, 2, 1)] + [partial[0]]
    merged = pl.pallas_call(
        merge_kernel,
        out_shape=jax.ShapeDtypeStruct((groups, local_rows, width), jnp.bfloat16),
        in_specs=[vmem] * CTX,
        out_specs=vmem,
        compiler_params=pltpu.CompilerParams(vmem_limit_bytes=4 * MIB),
        name="merge",
    )(*partial)
    if groups > 1:
        merged = over_seq(merged, same_member)
    return merged.transpose(1, 0, 2).reshape(local_rows, groups * width)


def solution(mesh):
    return jax.shard_map(
        body,
        mesh=mesh,
        in_specs=(
            P(("seq", "ctx"), None),
            P(("seq", "ctx"), None),
            P(("seq", "ctx"), None),
            P("seq", "ctx", None),
            P("seq", "ctx", None),
            P("seq", None, "ctx", None),
            P("seq", None, "ctx"),
        ),
        out_specs=P(("seq", "ctx"), None),
        check_vma=False,
    )
```
